32 devices in a mesh: dp: 16 (over z, y, x), mp: 2 (over core).
Axes of the slice: x: 2, y: 2, z: 4, core: 2. Of those that a mesh axis runs over, the one named last changes fastest.
Arguments:
- inputs: bfloat16 [2, 16, 512, 768], P(None, 'dp'), may hold values from -6 to 6
- cotangent: bfloat16 [2, 16, 512, 768], P(None, 'dp'), may hold values from -6 to 6
- lengths: int32 [2, 16], P(None, 'dp'), may hold values from 64 to 256, as said below
- proj_weight: float32 [768, 3, 768], P('dp', None, 'mp'), may hold values from -0.21875 to 0.21875
- output_weight: float32 [768, 768], P('mp', 'dp'), may hold values from -0.875 to 0.875
- upper_weight: float32 [768, 3072], P('dp', 'mp'), may hold values from -0.21875 to 0.21875
- lower_weight: float32 [3072, 768], P('mp', 'dp'), may hold values from -0.109375 to 0.109375
- norm_gains: float32 [2, 768], P(None, 'dp'), may hold values from 0.5 to 1.5
- proj_first: float32 [768, 3, 768], P('dp', None, 'mp'), may hold values from -32 to 32
- output_first: float32 [768, 768], P('mp', 'dp'), may hold values from -7 to 7
- upper_first: float32 [768, 3072], P('dp', 'mp'), may hold values from -20 to 20
- lower_first: float32 [3072, 768], P('mp', 'dp'), may hold values from -40 to 40
- gains_first: float32 [2, 768], P(None, 'dp'), may hold values from -32 to 32
- proj_second: float32 [768, 3, 768], P('dp', None, 'mp'), may hold values from 67.1744 to 1081.344
- output_second: float32 [768, 768], P('mp', 'dp'), may hold values from 2.686976 to 43.08992
- upper_second: float32 [768, 3072], P('dp', 'mp'), may hold values from 24.24832 to 386.6624
- lower_second: float32 [3072, 768], P('mp', 'dp'), may hold values from 96.99328 to 1548.288
- gains_second: float32 [2, 768], P(None, 'dp'), may hold values from 67.1744 to 1081.344
Outputs:
- outputs: bfloat16 [2, 16, 512, 768], P(None, 'dp')
- input_grad: float32 [2, 16, 512, 768], P(None, 'dp')
- proj_new: float32 [768, 3, 768], P('dp', None, 'mp')
- output_new: float32 [768, 768], P('mp', 'dp')
- upper_new: float32 [768, 3072], P('dp', 'mp')
- lower_new: float32 [3072, 768], P('mp', 'dp')
- gains_new: float32 [2, 768], P(None, 'dp')
- proj_first_new: float32 [768, 3, 768], P('dp', None, 'mp')
- output_first_new: float32 [768, 768], P('mp', 'dp')
- upper_first_new: float32 [768, 3072], P('dp', 'mp')
- lower_first_new: float32 [3072, 768], P('mp', 'dp')
- gains_first_new: float32 [2, 768], P(None, 'dp')
- proj_second_new: float32 [768, 3, 768], P('dp', None, 'mp')
- output_second_new: float32 [768, 768], P('mp', 'dp')
- upper_second_new: float32 [768, 3072], P('dp', 'mp')
- lower_second_new: float32 [3072, 768], P('mp', 'dp')
- gains_second_new: float32 [2, 768], P(None, 'dp')
- proj_copy: bfloat16 [768, 3, 768], P('dp', None, 'mp')
- output_copy: bfloat16 [768, 768], P('mp', 'dp')
- upper_copy: bfloat16 [768, 3072], P('dp', 'mp')
- lower_copy: bfloat16 [3072, 768], P('mp', 'dp')
- gains_copy: bfloat16 [2, 768], P(None, 'dp')
The draws below stay inside these ranges and needn't reach their ends.
Inputs may be any that keep to these rules, and one draw needn't show every extreme that they name: `lengths`: each length is a multiple of 16, and in each micro-batch at least one sequence has exactly 256 positions.
All inputs are finite; a program needn't handle non-finite values.
Results may differ from the reference program's by a relative error of at most 0.015.
The reference program's roundings to bfloat16 on the way count: a program that leaves them out, or rounds other values in their place, can miss the bound.
Values may be sent and summed in bfloat16 or wider, within the bound.
No kernel may reach another device: no remote copies, remote signals or barrier semaphores. Data moves between devices by JAX's collectives and lax.ppermute only.
A program may use at most 128 MiB of HBM per device.

```python
import math
import jax
import jax.numpy as jnp
from jax import lax

D = 768
H = 12
HD = 64
FF = 3072
BLOCK = 16
LEN = 256
MICRO = 2
STEP = 10
SEQS = 16
ROWS = 512
N_MP = 2


def draw_lengths(key, part):
    key = jax.random.fold_in(key, 7)
    first_key, second_key = jax.random.split(key)
    blocks = jax.random.randint(first_key, (MICRO, SEQS), LEN // 64, LEN // 16 + 1)
    chosen = jax.random.randint(second_key, (MICRO, 1), 0, SEQS)
    longest = jnp.arange(SEQS)[None, :] == chosen
    return (jnp.where(longest, LEN // 16, blocks) * 16).astype(jnp.int32)


def shard_levels(rng, extent, cuts, smallest, high):
    gain, own = 1.0, jax.random.fold_in(rng, 6)
    for axis_at, shards_of in cuts:
        draws = jnp.exp(jax.random.uniform(jax.random.fold_in(own, axis_at), (shards_of,), jnp.float32, smallest / len(cuts), high / len(cuts)))
        gain = gain * jnp.repeat(draws, extent[axis_at] // shards_of).reshape([-1 if axis == axis_at else 1 for axis in range(len(extent))])
    return gain


def bell_draw(rng, dims, deviation, limit, cuts=(), kind=jnp.bfloat16):
    gain = shard_levels(rng, dims, cuts, -0.22, 0.18) if cuts else 1.0
    array = jax.random.normal(rng, dims, jnp.float32) * deviation * gain
    return jnp.minimum(jnp.maximum(array, -limit), limit).astype(kind)


def setup_inputs(seed: int = 0) -> dict:
    key_of = jax.random.split(jax.random.key(seed), 19)
    inputs = bell_draw(key_of[0], (MICRO, SEQS, ROWS, D), 1.0, 6.0, ((1, 16),))
    cotangent = bell_draw(key_of[1], (MICRO, SEQS, ROWS, D), 1.0, 6.0, ((1, 16),))
    lengths = draw_lengths(jax.random.fold_in(key_of[18], 71), 0)
    proj_weight = bell_draw(key_of[3], (D, 3, H * HD), D ** -0.5, 0.21875, ((0, 16), (2, 2)), jnp.float32)
    output_weight = bell_draw(key_of[4], (H * HD, D), (H * HD // 16) ** -0.5, 0.875, ((0, 2), (1, 16)), jnp.float32)
    upper_weight = bell_draw(key_of[5], (D, FF), D ** -0.5, 0.21875, ((0, 16), (1, 2)), jnp.float32)
    lower_weight = bell_draw(key_of[6], (FF, D), FF ** -0.5, 0.109375, ((0, 2), (1, 16)), jnp.float32)
    norm_gains = jnp.clip(1.0 + 0.1 * jax.random.normal(key_of[7], (2, D), jnp.float32), 0.5, 1.5)
    proj_first = bell_draw(key_of[8], (D, 3, H * HD), (0.0439 * (MICRO * SEQS * 2 * LEN) ** 0.5), 32.0, ((0, 16), (2, 2)), jnp.float32)
    output_first = bell_draw(key_of[9], (H * HD, D), (0.00878 * (MICRO * SEQS * 2 * LEN) ** 0.5), 7.0, ((0, 2), (1, 16)), jnp.float32)
    upper_first = bell_draw(key_of[10], (D, FF), (0.0263 * (MICRO * SEQS * 2 * LEN) ** 0.5), 20.0, ((0, 16), (1, 2)), jnp.float32)
    lower_first = bell_draw(key_of[11], (FF, D), (0.0527 * (MICRO * SEQS * 2 * LEN) ** 0.5), 40.0, ((0, 2), (1, 16)), jnp.float32)
    gains_first = bell_draw(key_of[12], (2, D), (0.0439 * (MICRO * SEQS * 2 * LEN) ** 0.5), 32.0, ((1, 16),), jnp.float32)
    proj_second = jnp.clip(jnp.exp(math.log(1081.344) - 2.7786678 * jax.random.uniform(key_of[13], (D, 3, H * HD), jnp.float32) ** shard_levels(key_of[13], (D, 3, H * HD), ((0, 16), (2, 2)), -0.2, 0.2)), 67.1744, 1081.344)
    output_second = jnp.clip(jnp.exp(math.log(43.08992) - 2.7748727 * jax.random.uniform(key_of[14], (H * HD, D), jnp.float32) ** shard_levels(key_of[14], (H * HD, D), ((0, 2), (1, 16)), -0.2, 0.2)), 2.686976, 43.08992)
    upper_second = jnp.clip(jnp.exp(math.log(386.6624) - 2.7692047 * jax.random.uniform(key_of[15], (D, FF), jnp.float32) ** shard_levels(key_of[15], (D, FF), ((0, 16), (1, 2)), -0.2, 0.2)), 24.24832, 386.6624)
    lower_second = jnp.clip(jnp.exp(math.log(1548.288) - 2.7702634 * jax.random.uniform(key_of[16], (FF, D), jnp.float32) ** shard_levels(key_of[16], (FF, D), ((0, 2), (1, 16)), -0.2, 0.2)), 96.99328, 1548.288)
    gains_second = jnp.clip(jnp.exp(math.log(1081.344) - 2.7786678 * jax.random.uniform(key_of[17], (2, D), jnp.float32) ** shard_levels(key_of[17], (2, D), ((1, 16),), -0.2, 0.2)), 67.1744, 1081.344)
    return {"inputs": inputs, "cotangent": cotangent, "lengths": lengths, "proj_weight": proj_weight, "output_weight": output_weight, "upper_weight": upper_weight, "lower_weight": lower_weight, "norm_gains": norm_gains, "proj_first": proj_first, "output_first": output_first, "upper_first": upper_first, "lower_first": lower_first, "gains_first": gains_first, "proj_second": proj_second, "output_second": output_second, "upper_second": upper_second, "lower_second": lower_second, "gains_second": gains_second}


EPSILON = 1e-05
BETA_ONE = 0.9
BETA_TWO = 0.95
ADAM_EPS = 1e-08
DECAY = 0.1
RATE_MATRIX = 0.02
RATE_OUTPUT = 0.1
RATE_GAIN = 0.8
HIGHEST_MODE = lax.Precision.HIGHEST

@jax.custom_vjp
def low(v):
    return lax.optimization_barrier(v.astype(jnp.bfloat16)).astype(jnp.float32)

@jax.custom_vjp
def low_back(v):
    return v

def low_keep(v):
    return (low(v), None)

def low_pass(kept, grad):
    return (grad,)

def back_keep(v):
    return (v, None)

def back_low(kept, grad):
    return (low(grad),)
low.defvjp(low_keep, low_pass)
low_back.defvjp(back_keep, back_low)

def normalize(values):
    centre = lax.optimization_barrier(jnp.mean(values, axis=-1, keepdims=True))
    shifted = values - centre
    spread = lax.optimization_barrier(jnp.mean(shifted * shifted, axis=-1, keepdims=True))
    return shifted * lax.rsqrt(spread + EPSILON)

def rotation(row_count, head_width):
    halfway = head_width // 2
    freqs = 10000.0 ** (-2.0 * jnp.arange(halfway).astype(jnp.float32) / head_width)
    places = (jnp.arange(row_count) % LEN).astype(jnp.float32)
    angles = places[:, None] * freqs[None, :]
    return (jnp.cos(angles), jnp.sin(angles))

def rotate(vectors, cosine, sine):
    halfway = vectors.shape[-1] // 2
    front = vectors[..., :halfway]
    behind = vectors[..., halfway:]
    cos_cols = cosine[:, None, :]
    sin_cols = sine[:, None, :]
    return jnp.concatenate([front * cos_cols - behind * sin_cols, behind * cos_cols + front * sin_cols], axis=-1)

def allowed(query_rows, key_rows, length):
    query_clean = query_rows >= LEN
    key_clean = key_rows >= LEN
    query_place = query_rows - LEN * query_clean.astype(jnp.int32)
    key_place = key_rows - LEN * key_clean.astype(jnp.int32)
    query_block = (query_place // BLOCK)[:, None]
    key_block = (key_place // BLOCK)[None, :]
    noisy_rule = jnp.where(key_clean[None, :], key_block < query_block, key_block == query_block)
    clean_rule = key_clean[None, :] & (key_block <= query_block)
    rule = jnp.where(query_clean[:, None], clean_rule, noisy_rule)
    return (rule & (key_place < length)[None, :]).astype(jnp.int32)

def layer(params, sequence, length):
    proj_master, output_master, upper_master, lower_master, gains_master = params
    proj_c = low(proj_master)
    output_c = low(output_master)
    upper_c = low(upper_master)
    lower_c = low(lower_master)
    gains_c = low(gains_master)
    row_count = sequence.shape[0]
    first_norm = low(normalize(sequence) * gains_c[0])
    mixed = low_back(jnp.einsum('rd,dcf->rcf', first_norm, proj_c, precision=HIGHEST_MODE))
    cosine, sine = rotation(row_count, HD)
    query = low(rotate(mixed[:, 0].reshape(row_count, H, HD), cosine, sine))
    keys = low(rotate(mixed[:, 1].reshape(row_count, H, HD), cosine, sine))
    values = low(mixed[:, 2].reshape(row_count, H, HD))
    scores = low_back(jnp.einsum('qhd,khd->hqk', query, keys, precision=HIGHEST_MODE) * HD ** (-0.5))
    row_ids = jnp.arange(row_count, dtype=jnp.int32)
    visible = allowed(row_ids, row_ids, length) == 1
    scores = jnp.where(visible[None], scores, -1e+30)
    maximum = lax.optimization_barrier(jnp.max(scores, axis=-1, keepdims=True))
    raised = jnp.exp(scores - maximum)
    probs = raised / lax.optimization_barrier(jnp.sum(raised, axis=-1, keepdims=True))
    heads_out = low_back(low(jnp.einsum('hqk,khd->qhd', low(probs), values, precision=HIGHEST_MODE)))
    grouped = heads_out.reshape(row_count, N_MP, H // N_MP * HD)
    attn_parts = jnp.einsum('rgf,gfd->grd', grouped, output_c.reshape(N_MP, H // N_MP * HD, D), precision=HIGHEST_MODE)
    attn = low_back(lax.optimization_barrier(jnp.sum(low(attn_parts), axis=0)))
    middle = sequence + attn
    second_norm = low(normalize(middle) * gains_c[1])
    upper = low_back(jnp.dot(second_norm, upper_c, precision=HIGHEST_MODE))
    active = low(jax.nn.gelu(upper, approximate=False))
    ffn_parts = jnp.einsum('rgf,gfd->grd', active.reshape(row_count, N_MP, FF // N_MP), lower_c.reshape(N_MP, FF // N_MP, D), precision=HIGHEST_MODE)
    return middle + low_back(lax.optimization_barrier(jnp.sum(low(ffn_parts), axis=0)))

def adamw_update(weight, first, second, grad, rate, decay):
    first_new = BETA_ONE * first + (1.0 - BETA_ONE) * grad
    second_new = BETA_TWO * second + (1.0 - BETA_TWO) * grad * grad
    corrected = first_new / (1.0 - BETA_ONE ** STEP) / (jnp.sqrt(second_new / (1.0 - BETA_TWO ** STEP)) + ADAM_EPS)
    return (weight - rate * (corrected + decay * weight), first_new, second_new)

def reference(inputs, cotangent, lengths, proj_weight, output_weight, upper_weight, lower_weight, norm_gains, proj_first, output_first, upper_first, lower_first, gains_first, proj_second, output_second, upper_second, lower_second, gains_second):
    params = (proj_weight, output_weight, upper_weight, lower_weight, norm_gains)
    seq_total = MICRO * SEQS
    flat_in = inputs.reshape(seq_total, ROWS, D)
    flat_ct = cotangent.reshape(seq_total, ROWS, D)
    flat_len = lengths.reshape(seq_total)
    places = jnp.arange(ROWS, dtype=jnp.int32) % LEN

    def visit(summed, packed):
        sequence, upstream, length = packed
        sequence = sequence.astype(jnp.float32)
        result, pull = jax.vjp(lambda weights, rows_in: layer(weights, rows_in, length), params, sequence)
        valid = (places < length).astype(jnp.float32)
        grads, grad_in = pull(upstream.astype(jnp.float32) * valid[:, None])
        summed = jax.tree.map(jnp.add, summed, grads)
        return (summed, (result.astype(jnp.bfloat16), grad_in))
    empty = jax.tree.map(jnp.zeros_like, params)
    grads, (results, grads_in) = lax.scan(visit, empty, (flat_in, flat_ct, flat_len))
    proj_new, proj_first_new, proj_second_new = adamw_update(proj_weight, proj_first, proj_second, grads[0], RATE_MATRIX, DECAY)
    output_new, output_first_new, output_second_new = adamw_update(output_weight, output_first, output_second, grads[1], RATE_OUTPUT, DECAY)
    upper_new, upper_first_new, upper_second_new = adamw_update(upper_weight, upper_first, upper_second, grads[2], RATE_MATRIX, DECAY)
    lower_new, lower_first_new, lower_second_new = adamw_update(lower_weight, lower_first, lower_second, grads[3], RATE_MATRIX, DECAY)
    gains_new, gains_first_new, gains_second_new = adamw_update(norm_gains, gains_first, gains_second, grads[4], RATE_GAIN, 0.0)
    return (results.reshape(MICRO, SEQS, ROWS, D), grads_in.reshape(MICRO, SEQS, ROWS, D), proj_new, output_new, upper_new, lower_new, gains_new, proj_first_new, output_first_new, upper_first_new, lower_first_new, gains_first_new, proj_second_new, output_second_new, upper_second_new, lower_second_new, gains_second_new, proj_new.astype(jnp.bfloat16), output_new.astype(jnp.bfloat16), upper_new.astype(jnp.bfloat16), lower_new.astype(jnp.bfloat16), gains_new.astype(jnp.bfloat16))
```

```python
from functools import partial

import jax
import jax.numpy as jnp
from jax import lax
from jax.sharding import PartitionSpec as P

HD = 64
BLOCK = 16
LEN = 256
STEP = 10

EPSILON = 1e-05
BETA_ONE = 0.9
BETA_TWO = 0.95
ADAM_EPS = 1e-08
DECAY = 0.1
RATE_MATRIX = 0.02
RATE_OUTPUT = 0.1
RATE_GAIN = 0.8

LANES = 128
BF = jnp.bfloat16
F32 = jnp.float32

NZ, NY, NX = 4, 2, 2
CHIPS = NZ * NY * NX


def chip_pairs(move):
    pairs = []
    for chip in range(CHIPS):
        z, y, x = chip // 4, chip // 2 % 2, chip % 2
        to_z, to_y, to_x = move(z, y, x)
        pairs.append((chip, to_z * 4 + to_y * 2 + to_x))
    return pairs


SWAP_X = chip_pairs(lambda z, y, x: (z, y, 1 - x))
SWAP_Y = chip_pairs(lambda z, y, x: (z, 1 - y, x))
SHIFT_Z = {k: chip_pairs(lambda z, y, x, k=k: ((z + k) % NZ, y, x)) for k in (1, 2, 3)}


def chip_place():
    chip = lax.axis_index("dp")
    return chip // 4, chip // 2 % 2, chip % 2


def exchange(value, pairs):
    return lax.ppermute(value, "dp", pairs)


def gather_rows(shard, cut):
    if lax.axis_size("dp") != CHIPS:
        return lax.all_gather(shard, "dp", axis=0, tiled=True)
    z, y, x = chip_place()
    arrived = [shard] + [exchange(shard, SHIFT_Z[k]) for k in (1, 2, 3)]
    pieces = jnp.stack(arrived)
    order = (z - jnp.arange(NZ)) % NZ

    def one_part(part, first, second, first_bit, second_bit):
        near = exchange(part, first)
        pair = jnp.where(first_bit == 0, jnp.stack([part, near]), jnp.stack([near, part]))
        far = exchange(pair, second)
        return jnp.where(second_bit == 0, jnp.stack([pair, far]), jnp.stack([far, pair]))

    part_a = one_part(pieces[:, :, :cut], SWAP_X, SWAP_Y, x, y)
    part_b = one_part(pieces[:, :, cut:], SWAP_Y, SWAP_X, y, x)
    part_b = part_b.transpose(1, 0, 2, 3, 4)
    whole = jnp.concatenate([part_a, part_b], axis=-1)
    whole = jnp.take(whole, order, axis=2).transpose(2, 0, 1, 3, 4)
    return whole.reshape(CHIPS * shard.shape[0], shard.shape[1])


def scatter_rows(partial_sum, cut):
    size = lax.axis_size("dp")
    if size != CHIPS:
        return lax.psum_scatter(
            partial_sum.astype(BF), "dp", scatter_dimension=0, tiled=True
        ).astype(F32)
    z, y, x = chip_place()
    rows = partial_sum.shape[0] // CHIPS
    grid = partial_sum.reshape(NZ, NY, NX, rows, -1)
    pick = lax.dynamic_index_in_dim

    def one_part(part, first, second, first_axis, first_bit, second_bit):
        sent = pick(part, 1 - first_bit, first_axis, keepdims=False).astype(BF)
        kept = pick(part, first_bit, first_axis, keepdims=False)
        half = kept + exchange(sent, first).astype(F32)
        sent = pick(half, 1 - second_bit, 1, keepdims=False).astype(BF)
        kept = pick(half, second_bit, 1, keepdims=False)
        return kept + exchange(sent, second).astype(F32)

    part_a = one_part(grid[..., :cut], SWAP_X, SWAP_Y, 2, x, y)
    part_b = one_part(grid[..., cut:], SWAP_Y, SWAP_X, 1, y, x)
    column = jnp.concatenate([part_a, part_b], axis=-1)
    total = pick(column, z, 0, keepdims=False)
    for k in (1, 2, 3):
        sent = pick(column, (z + k) % NZ, 0, keepdims=False).astype(BF)
        total = total + exchange(sent, SHIFT_Z[k]).astype(F32)
    return total


def sum_pair(value):
    other = lax.ppermute(value, "mp", [(0, 1), (1, 0)])
    return value.astype(F32) + other.astype(F32)


def normalize(values):
    centre = jnp.mean(values, axis=-1, keepdims=True)
    shifted = values - centre
    spread = jnp.mean(shifted * shifted, axis=-1, keepdims=True)
    return shifted * lax.rsqrt(spread + EPSILON)


def scaled_norm(values, gain):
    return normalize(values) * gain


def rotation(row_count, head_width):
    halfway = head_width // 2
    freqs = 10000.0 ** (-2.0 * jnp.arange(halfway).astype(jnp.float32) / head_width)
    places = (jnp.arange(row_count) % LEN).astype(jnp.float32)
    angles = places[:, None] * freqs[None, :]
    return (jnp.cos(angles), jnp.sin(angles))


def rotate(vectors, cosine, sine):
    halfway = vectors.shape[-1] // 2
    front = vectors[..., :halfway]
    behind = vectors[..., halfway:]
    cos_cols = cosine[:, None, :]
    sin_cols = sine[:, None, :]
    return jnp.concatenate(
        [front * cos_cols - behind * sin_cols, behind * cos_cols + front * sin_cols], axis=-1
    )


def allowed(query_rows, key_rows, length):
    query_clean = query_rows >= LEN
    key_clean = key_rows >= LEN
    query_place = query_rows - LEN * query_clean.astype(jnp.int32)
    key_place = key_rows - LEN * key_clean.astype(jnp.int32)
    query_block = (query_place // BLOCK)[:, None]
    key_block = (key_place // BLOCK)[None, :]
    noisy_rule = jnp.where(key_clean[None, :], key_block < query_block, key_block == query_block)
    clean_rule = key_clean[None, :] & (key_block <= query_block)
    rule = jnp.where(query_clean[:, None], clean_rule, noisy_rule)
    return rule & (key_place < length)[None, :]


def attend_scores(query, key, length):
    rows = jnp.arange(query.shape[1], dtype=jnp.int32)
    scores = jnp.einsum("hqd,hkd->hqk", query, key, preferred_element_type=F32) * (HD**-0.5)
    return jnp.where(allowed(rows, rows, length)[None], scores, -1e30)


def attend_forward(query, key, value, length):
    scores = attend_scores(query, key, length)
    maximum = jnp.max(scores, axis=-1, keepdims=True)
    raised = jnp.exp(scores - maximum)
    summed = jnp.sum(raised, axis=-1, keepdims=True)
    weights = (raised / summed).astype(BF)
    result = jnp.einsum("hqk,hkd->qhd", weights, value, preferred_element_type=F32)
    return result.astype(BF), maximum + jnp.log(summed)


def attend_backward(query, key, value, head_grads, logsums, length):
    scores = attend_scores(query, key, length)
    softmaxed = jnp.exp(scores - logsums)
    prob_grads = jnp.einsum("qhd,hkd->hqk", head_grads, value, preferred_element_type=F32)
    inner_sum = jnp.sum(softmaxed * prob_grads, axis=-1, keepdims=True)
    score_grads = (softmaxed * (prob_grads - inner_sum)).astype(BF)
    scale = HD**-0.5
    query_grads = jnp.einsum("hqk,hkd->qhd", score_grads, key, preferred_element_type=F32) * scale
    key_grads = jnp.einsum("hqk,hqd->khd", score_grads, query, preferred_element_type=F32) * scale
    value_grads = jnp.einsum(
        "hqk,qhd->khd", softmaxed.astype(BF), head_grads, preferred_element_type=F32
    )
    return query_grads, key_grads, value_grads


def adamw_update(weight, first, second, grad, rate, decay):
    first_new = BETA_ONE * first + (1.0 - BETA_ONE) * grad
    second_new = BETA_TWO * second + (1.0 - BETA_TWO) * grad * grad
    corrected = (
        first_new
        / (1.0 - BETA_ONE**STEP)
        / (jnp.sqrt(second_new / (1.0 - BETA_TWO**STEP)) + ADAM_EPS)
    )
    return (weight - rate * (corrected + decay * weight), first_new, second_new)


def shards(
    inputs,
    cotangent,
    lengths,
    proj_weight,
    output_weight,
    upper_weight,
    lower_weight,
    norm_gains,
    proj_first,
    output_first,
    upper_first,
    lower_first,
    gains_first,
    proj_second,
    output_second,
    upper_second,
    lower_second,
    gains_second,
):
    micro_count, seq_count, row_count, width = inputs.shape
    feat_count = proj_weight.shape[2]
    head_count = feat_count // HD
    hidden = upper_weight.shape[1]
    shard_rows = proj_weight.shape[0]
    gelu_exact = partial(jax.nn.gelu, approximate=False)
    cosine, sine = rotation(row_count, HD)
    places = jnp.arange(row_count, dtype=jnp.int32) % LEN

    gain_columns = jnp.pad(norm_gains.T.astype(BF), ((0, 0), (0, LANES - 2)))
    proj_cols = 3 * feat_count
    shard_one = jnp.concatenate(
        [
            gain_columns,
            proj_weight.astype(BF).reshape(shard_rows, proj_cols),
            output_weight.astype(BF).T,
        ],
        axis=1,
    )
    cut = LANES + (proj_cols + feat_count) // 2
    whole_one = gather_rows(shard_one, cut)
    gains_c = whole_one[:, :2].T.astype(F32)
    proj_c = whole_one[:, LANES : LANES + proj_cols]
    output_t = whole_one[:, LANES + proj_cols :]
    upper_c = gather_rows(upper_weight.astype(BF), hidden // 2)
    lower_t = gather_rows(lower_weight.astype(BF).T, hidden // 2)
    gain_one, gain_two = gains_c[0], gains_c[1]

    results_list, kept = [], []
    for micro in range(micro_count):
        length = lengths[micro, 0]
        flat_in = inputs[micro].astype(F32).reshape(-1, width)
        first_norm = scaled_norm(flat_in, gain_one).astype(BF)
        mixed = jnp.dot(first_norm, proj_c, preferred_element_type=F32)
        mixed = mixed.reshape(row_count, 3, head_count, HD)
        query = rotate(mixed[:, 0], cosine, sine).astype(BF).transpose(1, 0, 2)
        key = rotate(mixed[:, 1], cosine, sine).astype(BF).transpose(1, 0, 2)
        value = mixed[:, 2].astype(BF).transpose(1, 0, 2)
        heads_out, logsums = attend_forward(query, key, value, length)
        flat_heads = heads_out.reshape(-1, feat_count)
        attn_part = jnp.einsum("rf,df->rd", flat_heads, output_t, preferred_element_type=F32)
        middle = flat_in + sum_pair(attn_part.astype(BF))
        second_norm = scaled_norm(middle, gain_two).astype(BF)
        upper = jnp.dot(second_norm, upper_c, preferred_element_type=F32)
        active = gelu_exact(upper).astype(BF)
        valid = (places < length).astype(F32)
        up_grad = cotangent[micro, 0].astype(F32) * valid[:, None]
        kept.append(
            (flat_in, first_norm, query, key, value, logsums, flat_heads, middle, second_norm, upper, active, up_grad)
        )

    def both(left, right):
        return sum(
            jnp.einsum("rd,rf->df", a, b, preferred_element_type=F32) for a, b in zip(left, right)
        )

    lows = [k[11].astype(BF) for k in kept]
    lower_grad = scatter_rows(both(lows, [k[10] for k in kept]), hidden // 2)
    upper_grads, seconds = [], []
    for micro in range(micro_count):
        upper = kept[micro][9]
        active_grad = jnp.dot(lows[micro], lower_t, preferred_element_type=F32)
        upper_grad = jax.vjp(gelu_exact, upper)[1](active_grad)[0].astype(BF)
        upper_grads.append(upper_grad)
        seconds.append(
            jnp.einsum("rf,df->rd", upper_grad, upper_c, preferred_element_type=F32).astype(BF)
        )
    upper_wgrad = scatter_rows(both([k[8] for k in kept], upper_grads), hidden // 2)
    middle_grads, attn_lows, mixed_grads, gain_two_grad = [], [], [], 0.0
    for micro in range(micro_count):
        flat_in, first_norm, query, key, value, logsums, flat_heads, middle, _, _, _, up_grad = kept[micro]
        second_back = sum_pair(seconds[micro])
        middle_part, gain_part = jax.vjp(scaled_norm, middle, gain_two)[1](second_back)
        gain_two_grad = gain_two_grad + gain_part
        middle_grad = up_grad + middle_part
        attn_low = middle_grad.astype(BF)
        head_grads = jnp.dot(attn_low, output_t, preferred_element_type=F32).astype(BF)
        head_grads = head_grads.reshape(row_count, head_count, HD)
        query_grads, key_grads, value_grads = attend_backward(
            query, key, value, head_grads, logsums, lengths[micro, 0]
        )
        mixed_grad = jnp.stack(
            [rotate(query_grads, cosine, -sine), rotate(key_grads, cosine, -sine), value_grads],
            axis=1,
        )
        mixed_grads.append(mixed_grad.astype(BF).reshape(-1, proj_cols))
        middle_grads.append(middle_grad)
        attn_lows.append(attn_low)
    output_part = both(attn_lows, [k[6] for k in kept])
    proj_part = both([k[1] for k in kept], mixed_grads)
    one_grad = scatter_rows(
        jnp.concatenate([proj_part, output_part], axis=1), (proj_cols + feat_count) // 2
    )
    gain_one_grad, input_grads = 0.0, []
    for micro in range(micro_count):
        flat_in, _, _, _, _, _, _, middle, _, _, active, _ = kept[micro]
        ffn_part = jnp.einsum("rf,df->rd", active, lower_t, preferred_element_type=F32)
        result = middle + sum_pair(ffn_part.astype(BF))
        results_list.append(result.astype(BF).reshape(inputs.shape[1:]))
        first_back = jnp.einsum(
            "rc,dc->rd", mixed_grads[micro], proj_c, preferred_element_type=F32
        ).astype(BF)
        input_part, gain_part = jax.vjp(scaled_norm, flat_in, gain_one)[1](sum_pair(first_back))
        gain_one_grad = gain_one_grad + gain_part
        input_grads.append((middle_grads[micro] + input_part).reshape(inputs.shape[1:]))
    gain_parts = jnp.stack([gain_one_grad, gain_two_grad]).reshape(2, -1, shard_rows)
    gain_parts = lax.all_to_all(gain_parts.transpose(1, 0, 2), "dp", 0, 0, tiled=True)
    gains_grad = jnp.sum(gain_parts, axis=0)
    proj_grad = one_grad[:, :proj_cols].reshape(proj_weight.shape)
    output_grad = one_grad[:, proj_cols:].T
    lower_grad = lower_grad.T

    updates = [
        adamw_update(proj_weight, proj_first, proj_second, proj_grad, RATE_MATRIX, DECAY),
        adamw_update(output_weight, output_first, output_second, output_grad, RATE_OUTPUT, DECAY),
        adamw_update(upper_weight, upper_first, upper_second, upper_wgrad, RATE_MATRIX, DECAY),
        adamw_update(lower_weight, lower_first, lower_second, lower_grad, RATE_MATRIX, DECAY),
        adamw_update(norm_gains, gains_first, gains_second, gains_grad, RATE_GAIN, 0.0),
    ]
    return (
        jnp.stack(results_list),
        jnp.stack(input_grads),
        *[u[0] for u in updates],
        *[u[1] for u in updates],
        *[u[2] for u in updates],
        *[u[0].astype(BF) for u in updates],
    )


def solution(mesh):
    rows = P(None, "dp", None, None)
    weights = (P("dp", None, "mp"), P("mp", "dp"), P("dp", "mp"), P("mp", "dp"), P(None, "dp"))
    in_specs = (rows, rows, P(None, "dp"), *weights * 3)
    out_specs = (rows, rows, *weights * 4)
    return jax.shard_map(shards, mesh=mesh, in_specs=in_specs, out_specs=out_specs, check_vma=False)
```

```python
from functools import partial

import jax
import jax.numpy as jnp
from jax import lax
from jax.experimental import pallas as pl
from jax.experimental.pallas import tpu as pltpu
from jax.sharding import PartitionSpec as P

HD = 64
BLOCK = 16
LEN = 256
STEP = 10

EPSILON = 1e-05
BETA_ONE = 0.9
BETA_TWO = 0.95
ADAM_EPS = 1e-08
DECAY = 0.1
RATE_MATRIX = 0.02
RATE_OUTPUT = 0.1
RATE_GAIN = 0.8

LANES = 128
PAIR = 2 * HD
BF = jnp.bfloat16
F32 = jnp.float32
MASKED = -1e30
SCALE = HD**-0.5

NZ, NY, NX = 4, 2, 2
CHIPS = NZ * NY * NX


def call(kernel, out_shape, args, smem=(), scratch=(), flops=0, name=None):
    spaces = [
        pl.BlockSpec(memory_space=pltpu.SMEM if i in smem else pltpu.VMEM) for i in range(len(args))
    ]
    shapes = [jax.ShapeDtypeStruct(s, d) for s, d in out_shape]
    moved = sum(a.size * a.dtype.itemsize for a in [*args, *shapes])
    return pl.pallas_call(
        kernel,
        out_shape=shapes,
        in_specs=spaces,
        out_specs=[pl.BlockSpec(memory_space=pltpu.VMEM)] * len(shapes),
        scratch_shapes=list(scratch),
        compiler_params=pltpu.CompilerParams(vmem_limit_bytes=56 * 1024 * 1024),
        cost_estimate=pl.CostEstimate(flops=int(flops), bytes_accessed=moved, transcendentals=0),
        name=name,
    )(*args)


def dot(a, b):
    return jnp.dot(a, b, preferred_element_type=F32)


def dot_nt(a, b):
    return lax.dot_general(a, b, (((1,), (1,)), ((), ())), preferred_element_type=F32)


def dot_tn(a, b):
    return lax.dot_general(a, b, (((0,), (0,)), ((), ())), preferred_element_type=F32)


def norm_parts(values):
    centre = jnp.mean(values, axis=-1, keepdims=True)
    shifted = values - centre
    spread = jnp.mean(shifted * shifted, axis=-1, keepdims=True)
    inverse = lax.rsqrt(spread + EPSILON)
    return shifted * inverse, inverse


def norm_back(normed, inverse, grads, gain):
    scaled = grads * gain
    mean_one = jnp.mean(scaled, axis=-1, keepdims=True)
    mean_two = jnp.mean(scaled * normed, axis=-1, keepdims=True)
    return (scaled - mean_one - normed * mean_two) * inverse


def assemble_kernel(place, near_a, far_a, near_b, far_b, whole):
    z, y, x = place[0], place[1], place[2]
    rows, cut = near_a.shape[2], near_a.shape[3]
    for near in range(2):
        for k in range(NZ):
            for far in range(2):
                z_of = lax.rem(z + NZ - k, NZ) * 4
                row_a = z_of + (y ^ far) * 2 + (x ^ near)
                row_b = z_of + (y ^ near) * 2 + (x ^ far)
                at_a = pl.ds(pl.multiple_of(row_a * rows, rows), rows)
                at_b = pl.ds(pl.multiple_of(row_b * rows, rows), rows)
                whole[at_a, :cut] = (far_a if far else near_a)[near, k]
                whole[at_b, cut:] = (far_b if far else near_b)[near, k]


def assemble(place, near_a, far_a, near_b, far_b):
    rows = near_a.shape[2]
    columns = near_a.shape[3] + near_b.shape[3]
    return call(
        assemble_kernel,
        [((CHIPS * rows, columns), BF)],
        (place, near_a, far_a, near_b, far_b),
        smem=(0,),
        name="assemble",
    )[0]


def swap_halves(u):
    lane = lax.broadcasted_iota(jnp.int32, u.shape, 1)
    ahead = pltpu.roll(u, LANES - HD // 2, 1)
    behind = pltpu.roll(u, HD // 2, 1)
    return jnp.where(lane % HD < HD // 2, ahead, behind)


def qkv_kernel(inputs, gains, weight, cosine, sine, first_norm, mixed):
    feats = mixed.shape[1] // 3
    step = 256
    for start in range(0, inputs.shape[0], step):
        rows = pl.ds(start, step)
        normed, _ = norm_parts(inputs[rows, :].astype(F32))
        low = (normed * gains[0:1, :]).astype(BF)
        first_norm[rows, :] = low
        place = pl.ds(start % LEN, step)
        cos_rows, sin_rows = cosine[place, :], sine[place, :]
        product = dot(low, weight[:, feats : 4 * feats])
        for j in range(2 * feats // LANES):
            at = slice(j * LANES, (j + 1) * LANES)
            u = product[:, at]
            turned = (u * cos_rows + swap_halves(u) * sin_rows).astype(BF)
            if j < feats // LANES:
                turned = turned * jnp.asarray(SCALE, BF)
            mixed[rows, at] = turned
        mixed[rows, 2 * feats :] = product[:, 2 * feats :].astype(BF)


def visible_bias(length):
    row = lax.broadcasted_iota(jnp.int32, (LEN, LEN), 0) // BLOCK
    place = lax.broadcasted_iota(jnp.int32, (LEN, LEN), 1)
    col = place // BLOCK
    real = place < length
    bias = lambda seen: jnp.where(seen & real, 0.0, MASKED).astype(F32)
    noisy = jnp.concatenate([bias(col == row), bias(col < row)], axis=1)
    return noisy, bias(col <= row)


def own_lanes(value, head):
    lane = lax.broadcasted_iota(jnp.int32, value.shape, 1)
    mine = (lane < HD) if head == 0 else (lane >= HD)
    return jnp.where(mine, value, jnp.zeros_like(value))


def attend_kernel(micro, lengths, mixed, weight, heads, logsums, part):
    feats = heads.shape[1]
    bias_noisy, bias_clean = visible_bias(lengths[micro])
    lane = lax.broadcasted_iota(jnp.int32, (LEN, LANES), 1)
    base = micro * 2 * LEN
    sums = [jnp.zeros((LEN, LANES), F32), jnp.zeros((LEN, LANES), F32)]
    for pair in range(feats // PAIR):
        query, key, value = (
            mixed[pl.ds(base, 2 * LEN), c * feats + pair * PAIR : c * feats + (pair + 1) * PAIR]
            for c in range(3)
        )
        outs = [None, None]
        for head in range(2):
            mine = own_lanes(query, head)
            for clean in range(2):
                keys = key[LEN:] if clean else key
                values = value[LEN:] if clean else value
                scores = dot_nt(mine[clean * LEN : (clean + 1) * LEN], keys)
                scores = scores + (bias_clean if clean else bias_noisy)
                maximum = jnp.max(scores, axis=-1, keepdims=True)
                raised = jnp.exp(scores - maximum)
                summed = jnp.sum(raised, axis=-1, keepdims=True)
                weights = (raised * (1.0 / summed)).astype(BF)
                out = dot(weights, values)
                outs[clean] = out if head == 0 else jnp.where(lane < HD, outs[clean], out)
                sums[clean] = jnp.where(
                    lane == pair * 2 + head, maximum + jnp.log(summed), sums[clean]
                )
        for clean in range(2):
            heads[clean * LEN : (clean + 1) * LEN, pair * PAIR : (pair + 1) * PAIR] = outs[
                clean
            ].astype(BF)
    for clean in range(2):
        rows = slice(clean * LEN, (clean + 1) * LEN)
        logsums[rows, :] = sums[clean]
        part[rows, :] = dot_nt(heads[rows, :], weight[:, :feats]).astype(BF)


ERF_NUM = (
    -2.72614225801306e-10,
    2.77068142495902e-08,
    -2.10102402082508e-06,
    -5.69250639462346e-05,
    -7.34990630326855e-04,
    -2.95459980854025e-03,
    -1.60960333262415e-02,
)
ERF_DEN = (
    -1.45660718464996e-05,
    -2.13374055278905e-04,
    -1.68282697438203e-03,
    -7.37332916720468e-03,
    -1.42647390514189e-02,
)


def gelu_parts(v):
    u = jnp.clip(v * (0.5**0.5), -4.0, 4.0)
    square = u * u
    num = jnp.full_like(u, ERF_NUM[0])
    for c in ERF_NUM[1:]:
        num = num * square + c
    den = jnp.full_like(u, ERF_DEN[0])
    for c in ERF_DEN[1:]:
        den = den * square + c
    half = 0.5 + 0.5 * (u * num / den)
    bell = jnp.exp(v * v * -0.5) * 0.3989422804014327
    return v * half, half + v * bell


def upper_kernel(micro, inputs, own, other, gains, weight, middle, second_norm, active, slope):
    base = micro * 2 * LEN
    step, wide = 256, 512
    for start in range(0, 2 * LEN, step):
        rows = pl.ds(start, step)
        value = inputs[pl.ds(base + start, step), :].astype(F32) + (
            own[rows, :].astype(F32) + other[rows, :].astype(F32)
        )
        middle[rows, :] = value
        normed, _ = norm_parts(value)
        low = (normed * gains[1:2, :]).astype(BF)
        second_norm[rows, :] = low
        for c in range(0, weight.shape[1], wide):
            out, grad = gelu_parts(dot(low, weight[:, c : c + wide]))
            active[rows, c : c + wide] = out.astype(BF)
            slope[rows, c : c + wide] = grad.astype(BF)


def masked_rows(cotangent, start, step, length):
    place = lax.broadcasted_iota(jnp.int32, (step, 1), 0) + start % LEN
    rows = cotangent[pl.ds(start, step), :]
    return jnp.where(place < length, rows, jnp.zeros_like(rows))


def hidden_back_kernel(micro, lengths, cotangent, slope, lower, upper, upper_grad, part):
    base = micro * 2 * LEN
    step, wide = 256, 512
    for start in range(0, 2 * LEN, step):
        rows = pl.ds(start, step)
        low = masked_rows(cotangent, base + start, step, lengths[micro])
        total = jnp.zeros((step, part.shape[1]), F32)
        for c in range(0, lower.shape[1], wide):
            grad = dot(low, lower[:, c : c + wide]) * slope[rows, c : c + wide].astype(F32)
            grad = grad.astype(BF)
            upper_grad[rows, c : c + wide] = grad
            total = total + dot_nt(grad, upper[:, c : c + wide])
        part[rows, :] = total.astype(BF)


def middle_back_kernel(
    micro, lengths, cotangent, own, other, middle, gains, weight, middle_grad, low, head_grad, gain
):
    base = micro * 2 * LEN
    step = 256
    feats = head_grad.shape[1]
    gain[...] = jnp.zeros_like(gain)
    for start in range(0, 2 * LEN, step):
        rows = pl.ds(start, step)
        upstream = masked_rows(cotangent, base + start, step, lengths[micro]).astype(F32)
        back = own[rows, :].astype(F32) + other[rows, :].astype(F32)
        normed, inverse = norm_parts(middle[rows, :])
        gain[0:1, :] += jnp.sum(back * normed, axis=0, keepdims=True)
        grad = upstream + norm_back(normed, inverse, back, gains[1:2, :])
        middle_grad[rows, :] = grad
        low_grad = grad.astype(BF)
        low[rows, :] = low_grad
        head_grad[rows, :] = dot(low_grad, weight[:, :feats]).astype(BF)


def attend_back_kernel(
    micro, lengths, mixed, logsums, head_grad, cosine, sine, mixed_grad, key_sum, value_sum
):
    feats = head_grad.shape[1]
    bias_noisy, bias_clean = visible_bias(lengths[micro])
    base = micro * 2 * LEN
    cos_rows, sin_rows = cosine[...], sine[...]

    def turn_back(u):
        return u * cos_rows - swap_halves(u) * sin_rows

    lane = lax.broadcasted_iota(jnp.int32, (LEN, LANES), 1)
    for pair in range(feats // PAIR):
        cols = [
            slice(c * feats + pair * PAIR, c * feats + (pair + 1) * PAIR) for c in range(3)
        ]
        query, key, value = (mixed[pl.ds(base, 2 * LEN), c] for c in cols)
        upstream = head_grad[:, pair * PAIR : (pair + 1) * PAIR]
        query_grads = [None, None]
        for head in range(2):
            mine, mine_grad = own_lanes(query, head), own_lanes(upstream, head)
            for clean in range(2):
                rows = slice(clean * LEN, (clean + 1) * LEN)
                keys = key[LEN:] if clean else key
                values = value[LEN:] if clean else value
                at = pair * 2 + head
                scores = dot_nt(mine[rows], keys) + (bias_clean if clean else bias_noisy)
                probs = jnp.exp(scores - logsums[rows, at : at + 1])
                prob_grads = dot_nt(mine_grad[rows], values)
                inner = jnp.sum(probs * prob_grads, axis=-1, keepdims=True)
                score_grads = (probs * (prob_grads - inner)).astype(BF)
                grads = dot(score_grads, keys)
                query_grads[clean] = (
                    grads if head == 0 else jnp.where(lane < HD, query_grads[clean], grads)
                )
                key_part = dot_tn(score_grads, mine[rows])
                value_part = dot_tn(probs.astype(BF), mine_grad[rows])
                if head == 0 and not clean:
                    key_sum[...] = key_part
                    value_sum[...] = value_part
                elif not clean:
                    key_sum[...] += key_part
                    value_sum[...] += value_part
                else:
                    key_sum[LEN:, :] += key_part
                    value_sum[LEN:, :] += value_part
        for clean in range(2):
            rows = slice(clean * LEN, (clean + 1) * LEN)
            mixed_grad[rows, cols[0]] = turn_back(query_grads[clean] * SCALE).astype(BF)
            mixed_grad[rows, cols[1]] = turn_back(key_sum[rows, :]).astype(BF)
            mixed_grad[rows, cols[2]] = value_sum[rows, :].astype(BF)


def put_blocks(place, product, scratch, column, x_first):
    z, y, x = place[0], place[1], place[2]
    rows = product.shape[0] // CHIPS
    for chip in range(CHIPS):
        to_z = lax.rem(chip // 4 + NZ - z, NZ)
        to_y, to_x = y ^ (chip // 2 % 2), x ^ (chip % 2)
        at = (to_x * 2 + to_y if x_first else to_y * 2 + to_x) * NZ + to_z
        scratch[pl.ds(pl.multiple_of(at * rows, rows), rows), column] = product[
            chip * rows : (chip + 1) * rows
        ].astype(BF)


def write_products(place, products, outs, scratch):
    if len(outs) == 1:
        for column, value in products:
            outs[0][:, column : column + value.shape[1]] = value.astype(BF)
        return
    cut = outs[0].shape[1]
    for column, value in products:
        for half in range(2):
            low, high = max(column, half * cut), min(column + value.shape[1], (half + 1) * cut)
            if low < high:
                put_blocks(
                    place,
                    value[:, low - column : high - column],
                    scratch.at[half],
                    slice(low - half * cut, high - half * cut),
                    half == 0,
                )
    size = outs[0].shape[0]
    for half in range(2):
        outs[2 * half][...] = scratch[half, :size]
        outs[2 * half + 1][...] = scratch[half, size:]


def product_out(width, columns, local):
    if local:
        return [((width // 2, columns // 2), BF)] * 4, [pltpu.VMEM((2, width, columns // 2), BF)]
    return [((width, columns), BF)], []


def wide_grad_kernel(outs, masked, place, lengths, *refs):
    count = 1 if masked else 2
    lefts, rights = refs[:count], refs[count : count + 2]
    refs = refs[count + 2 :]
    out_refs, scratch = refs[:outs], refs[outs:]
    turned = scratch[0]
    rows = 2 * LEN
    for micro in range(2):
        if masked:
            for start in range(0, rows, LEN):
                low = masked_rows(lefts[0], micro * rows + start, LEN, lengths[micro])
                turned[:, micro * rows + start : micro * rows + start + LEN] = low.T
        else:
            turned[:, micro * rows : (micro + 1) * rows] = lefts[micro][...].T
    wide = 256
    products = []
    for c in range(0, rights[0].shape[1], wide):
        total = dot(turned[:, :rows], rights[0][:, c : c + wide])
        total = total + dot(turned[:, rows:], rights[1][:, c : c + wide])
        products.append((c, total))
    write_products(place, products, out_refs, scratch[1] if outs > 1 else None)


def wide_grad(place, lengths, lefts, rights, masked, local, name):
    width, columns = lefts[0].shape[1], rights[0].shape[1]
    out, scratch = product_out(width, columns, local)
    return call(
        partial(wide_grad_kernel, len(out), masked),
        out,
        (place, lengths, *lefts, *rights),
        smem=(0, 1),
        scratch=[pltpu.VMEM((width, 4 * LEN), BF)] + scratch,
        name=name,
    )


def proj_grad_kernel(outs, place, *refs):
    norms, mixed_grads, lows, heads = refs[0], refs[1:3], refs[3:5], refs[5:7]
    out_refs, scratch = refs[7 : 7 + outs], refs[7 + outs :]
    turned = scratch[0]
    rows = 2 * LEN
    products = []
    for micro in range(2):
        turned[:, micro * rows : (micro + 1) * rows] = lows[micro][...].T
    total = dot(turned[:, :rows], heads[0][...]) + dot(turned[:, rows:], heads[1][...])
    products.append((0, total))
    feats = heads[0].shape[1]
    for micro in range(2):
        turned[:, micro * rows : (micro + 1) * rows] = norms[pl.ds(micro * rows, rows), :].T
    for c in range(0, 3 * feats, feats):
        total = dot(turned[:, :rows], mixed_grads[0][:, c : c + feats])
        total = total + dot(turned[:, rows:], mixed_grads[1][:, c : c + feats])
        products.append((feats + c, total))
    write_products(place, products, out_refs, scratch[1] if outs > 1 else None)


def proj_grad(place, first_norm, mixed_grads, lows, heads, local):
    width, columns = first_norm.shape[1], 4 * heads[0].shape[1]
    out, scratch = product_out(width, columns, local)
    return call(
        partial(proj_grad_kernel, len(out)),
        out,
        (place, first_norm, *mixed_grads, *lows, *heads),
        smem=(0,),
        scratch=[pltpu.VMEM((width, 4 * LEN), BF)] + scratch,
        name="proj_grad",
    )


def chip_pairs(move):
    pairs = []
    for chip in range(CHIPS):
        to_z, to_y, to_x = move(chip // 4, chip // 2 % 2, chip % 2)
        pairs.append((chip, to_z * 4 + to_y * 2 + to_x))
    return pairs


SWAP_X = chip_pairs(lambda z, y, x: (z, y, 1 - x))
SWAP_Y = chip_pairs(lambda z, y, x: (z, 1 - y, x))
SHIFT_Z = {k: chip_pairs(lambda z, y, x, k=k: ((z + k) % NZ, y, x)) for k in (1, 2, 3)}


def exchange(value, pairs, name):
    with jax.named_scope(name):
        return lax.ppermute(value, "dp", pairs)


tie = lax.optimization_barrier


def start_gather(name, shard):
    if lax.axis_size("dp") != CHIPS:
        return [lax.all_gather(shard, "dp", axis=0, tiled=True)]
    return [shard] + [exchange(shard, SHIFT_Z[k], f"{name}_z{k}") for k in (1, 2, 3)]


def spread_near(name, arrived, cut):
    if len(arrived) == 1:
        return arrived
    part_a = jnp.stack([a[:, :cut] for a in arrived])
    part_b = jnp.stack([a[:, cut:] for a in arrived])
    near_a = jnp.stack([part_a, exchange(part_a, SWAP_X, f"{name}_near_a")])
    near_b = jnp.stack([part_b, exchange(part_b, SWAP_Y, f"{name}_near_b")])
    return [near_a, near_b]


def spread_far(name, near):
    if len(near) == 1:
        return near
    near_a, near_b = near
    far_a = exchange(near_a, SWAP_Y, f"{name}_far_a")
    return [near_a, far_a, near_b, exchange(near_b, SWAP_X, f"{name}_far_b")]


def assembled(place, pieces):
    return pieces[0] if len(pieces) == 1 else assemble(place, *pieces)


def scatter_first(name, parts):
    if len(parts) == 1:
        return parts
    halves = []
    for tag, kept, sent, move in (("a", *parts[:2], SWAP_X), ("b", *parts[2:], SWAP_Y)):
        rows, columns = kept.shape[0] // (2 * NZ), kept.shape[1]
        half = kept.astype(F32) + exchange(sent, move, f"{name}_first_{tag}").astype(F32)
        halves.append(half.reshape(2, NZ, rows, columns))
    return halves


def scatter_second(name, halves):
    if len(halves) == 1:
        return halves
    return [
        half[0] + exchange(half[1].astype(BF), move, f"{name}_second_{tag}").astype(F32)
        for tag, half, move in zip("ab", halves, (SWAP_Y, SWAP_X))
    ]


def scatter_last(name, columns):
    if len(columns) == 1:
        return lax.psum_scatter(columns[0], "dp", scatter_dimension=0, tiled=True).astype(F32)
    column = jnp.concatenate(columns, axis=-1)
    total = column[0]
    for k in (1, 2, 3):
        total = total + exchange(column[k].astype(BF), SHIFT_Z[k], f"{name}_z{k}").astype(F32)
    return total


def swapped(value):
    return lax.ppermute(value, "mp", [(0, 1), (1, 0)])


def rotation(row_count, head_width):
    halfway = head_width // 2
    freqs = 10000.0 ** (-2.0 * jnp.arange(halfway).astype(jnp.float32) / head_width)
    places = (jnp.arange(row_count) % LEN).astype(jnp.float32)
    angles = places[:, None] * freqs[None, :]
    return (jnp.cos(angles), jnp.sin(angles))


def adamw_update(weight, first, second, grad, rate, decay):
    first_new = BETA_ONE * first + (1.0 - BETA_ONE) * grad
    second_new = BETA_TWO * second + (1.0 - BETA_TWO) * grad * grad
    corrected = (
        first_new
        / (1.0 - BETA_ONE**STEP)
        / (jnp.sqrt(second_new / (1.0 - BETA_TWO**STEP)) + ADAM_EPS)
    )
    return (weight - rate * (corrected + decay * weight), first_new, second_new)


def shards(
    inputs,
    cotangent,
    lengths,
    proj_weight,
    output_weight,
    upper_weight,
    lower_weight,
    norm_gains,
    proj_first,
    output_first,
    upper_first,
    lower_first,
    gains_first,
    proj_second,
    output_second,
    upper_second,
    lower_second,
    gains_second,
):
    micro_count, _, row_count, width = inputs.shape
    feats = proj_weight.shape[2]
    hidden = upper_weight.shape[1]
    shard_rows = proj_weight.shape[0]
    local = lax.axis_size("dp") == CHIPS
    chip = lax.axis_index("dp").astype(jnp.int32)
    place = jnp.stack([chip // 4, chip // 2 % 2, chip % 2])
    micros = range(micro_count)
    lengths = lengths.reshape(-1)
    flat_in = inputs.reshape(-1, width)
    flat_ct = cotangent.reshape(-1, width)

    cosine, sine = rotation(LEN, HD)
    cosine = jnp.tile(cosine, (1, 4))
    sine = jnp.tile(jnp.concatenate([-sine, sine], axis=1), (1, 2))

    gain_columns = jnp.pad(norm_gains.T.astype(BF), ((0, 0), (0, LANES - 2)))
    shard_one = jnp.concatenate(
        [
            output_weight.astype(BF).T,
            proj_weight.astype(BF).reshape(shard_rows, 3 * feats),
            gain_columns,
        ],
        axis=1,
    )
    upper_low, lower_low = upper_weight.astype(BF), lower_weight.astype(BF).T
    arrived = start_gather("one", shard_one)
    upper_low, arrived = tie((upper_low, arrived))
    near = spread_near("one", arrived, 2 * feats)
    arrived_upper = start_gather("upper", upper_low)
    pieces = spread_far("one", near)
    arrived_upper, lower_low, pieces = tie((arrived_upper, lower_low, pieces))
    near_upper = spread_near("upper", arrived_upper, hidden // 2)
    arrived_lower = start_gather("lower", lower_low)
    one = assembled(place, pieces)
    gains_c = jnp.pad(one[:, 4 * feats : 4 * feats + 2].T.astype(F32), ((0, 6), (0, 0)))

    total_rows = micro_count * row_count
    first_norm, mixed = call(
        qkv_kernel,
        [((total_rows, width), BF), ((total_rows, 3 * feats), BF)],
        (flat_in, gains_c, one, cosine, sine),
        name="qkv",
    )
    heads, logsums, attn = [], [], []
    for m in micros:
        if m:
            mixed, near_upper, attn = tie((mixed, near_upper, attn))
            far_upper = spread_far("upper", near_upper)
        h, s, p = call(
            partial(attend_kernel, m),
            [((row_count, feats), BF), ((row_count, LANES), F32), ((row_count, width), BF)],
            (lengths, mixed, one),
            smem=(0,),
            name="attend",
        )
        heads.append(h)
        logsums.append(s)
        attn.append(p)
    far_upper, arrived_lower, attn = tie((far_upper, arrived_lower, attn))
    near_lower = spread_near("lower", arrived_lower, hidden // 2)
    upper_c = assembled(place, far_upper)
    middle, second_norm, active, slope = [], [], [], []
    for m in micros:
        if m:
            upper_c, near_lower, active = tie((upper_c, near_lower, active))
            far_lower = spread_far("lower", near_lower)
        outs = call(
            partial(upper_kernel, m),
            [
                ((row_count, width), F32),
                ((row_count, width), BF),
                ((row_count, hidden), BF),
                ((row_count, hidden), BF),
            ],
            (flat_in, attn[m], swapped(attn[m]), gains_c, upper_c),
            name="upper",
        )
        for kept, out in zip((middle, second_norm, active, slope), outs):
            kept.append(out)
    active, far_lower = tie((active, far_lower))
    lower_parts = wide_grad(place, lengths, [flat_ct], active, True, local, "lower_grad")
    lower_half = scatter_first("lower_sum", lower_parts)
    lower_t = assembled(place, far_lower)
    upper_grads, seconds, crossed = [], [], []
    for m in micros:
        if m:
            lower_t, lower_half, seconds = tie((lower_t, lower_half, seconds))
            lower_column = scatter_second("lower_sum", lower_half)
            crossed.append(swapped(seconds[0]))
        grad, part = call(
            partial(hidden_back_kernel, m),
            [((row_count, hidden), BF), ((row_count, width), BF)],
            (lengths, flat_ct, slope[m], lower_t, upper_c),
            smem=(0,),
            name="hidden_back",
        )
        upper_grads.append(grad)
        seconds.append(part)
    upper_grads, lower_column, seconds = tie((upper_grads, lower_column, seconds))
    crossed.append(swapped(seconds[1]))
    lower_sum = scatter_last("lower_sum", lower_column)
    upper_parts = wide_grad(place, lengths, second_norm, upper_grads, False, local, "upper_grad")
    upper_half = scatter_first("upper_sum", upper_parts)
    middle_grads, lows, mixed_grads, gain_two = [], [], [], []
    for m in micros:
        if m:
            upper_column, mixed_grads, crossed = tie((upper_column, mixed_grads, crossed))
            upper_sum = scatter_last("upper_sum", upper_column)
        middle_grad, low, head_grad, gain = call(
            partial(middle_back_kernel, m),
            [
                ((row_count, width), F32),
                ((row_count, width), BF),
                ((row_count, feats), BF),
                ((8, width), F32),
            ],
            (lengths, flat_ct, seconds[m], crossed[m], middle[m], gains_c, one),
            smem=(0,),
            name="middle_back",
        )
        if m == 0:
            head_grad, upper_half, lower_sum = tie((head_grad, upper_half, lower_sum))
            upper_column = scatter_second("upper_sum", upper_half)
        mixed_grads += call(
            partial(attend_back_kernel, m),
            [((row_count, 3 * feats), BF)],
            (lengths, mixed, logsums[m], head_grad, cosine, sine),
            smem=(0,),
            scratch=[pltpu.VMEM((row_count, LANES), F32)] * 2,
            name="attend_back",
        )
        middle_grads.append(middle_grad)
        lows.append(low)
        gain_two.append(gain[0])
    mixed_grads, upper_sum = tie((mixed_grads, upper_sum))
    one_parts = proj_grad(place, first_norm, mixed_grads, lows, heads, local)
    active, mixed_grads, one_parts = tie((active, mixed_grads, one_parts))
    one_column = scatter_second("one_sum", scatter_first("one_sum", one_parts))
    one_grad = scatter_last("one_sum", one_column)

    results, input_grads, gain_one = [], [], []
    for m in micros:
        ffn = dot_nt(active[m], lower_t).astype(BF)
        result = middle[m] + (ffn.astype(F32) + swapped(ffn).astype(F32))
        results.append(result.astype(BF).reshape(inputs.shape[1:]))
        back = dot_nt(mixed_grads[m], one[:, feats : 4 * feats]).astype(BF)
        back = back.astype(F32) + swapped(back).astype(F32)
        normed, inverse = norm_parts(inputs[m, 0].astype(F32))
        gain_one.append(jnp.sum(back * normed, axis=0))
        grad = middle_grads[m] + norm_back(normed, inverse, back, gains_c[0:1])
        input_grads.append(grad.reshape(inputs.shape[1:]))
    gain_parts = jnp.stack([sum(gain_one), sum(gain_two)]).reshape(2, -1, shard_rows)
    gain_parts = lax.all_to_all(gain_parts.transpose(1, 0, 2), "dp", 0, 0, tiled=True)
    gains_grad = jnp.sum(gain_parts, axis=0)
    proj_wgrad = one_grad[:, feats:].reshape(proj_weight.shape)
    output_grad = one_grad[:, :feats].T

    updates = [
        adamw_update(proj_weight, proj_first, proj_second, proj_wgrad, RATE_MATRIX, DECAY),
        adamw_update(output_weight, output_first, output_second, output_grad, RATE_OUTPUT, DECAY),
        adamw_update(upper_weight, upper_first, upper_second, upper_sum, RATE_MATRIX, DECAY),
        adamw_update(lower_weight, lower_first, lower_second, lower_sum.T, RATE_MATRIX, DECAY),
        adamw_update(norm_gains, gains_first, gains_second, gains_grad, RATE_GAIN, 0.0),
    ]
    return (
        jnp.stack(results),
        jnp.stack(input_grads),
        *[u[0] for u in updates],
        *[u[1] for u in updates],
        *[u[2] for u in updates],
        *[u[0].astype(BF) for u in updates],
    )


def solution(mesh):
    rows = P(None, "dp", None, None)
    weights = (P("dp", None, "mp"), P("mp", "dp"), P("dp", "mp"), P("mp", "dp"), P(None, "dp"))
    in_specs = (rows, rows, P(None, "dp"), *weights * 3)
    out_specs = (rows, rows, *weights * 4)
    return jax.shard_map(shards, mesh=mesh, in_specs=in_specs, out_specs=out_specs, check_vma=False)
```

```python
import math
from functools import partial

import jax
import jax.numpy as jnp
from jax import lax
from jax.experimental import pallas as pl
from jax.experimental.pallas import tpu as pltpu
from jax.sharding import PartitionSpec as P

HD = 64
BLOCK = 16
LEN = 256
STEP = 10

EPSILON = 1e-05
BETA_ONE = 0.9
BETA_TWO = 0.95
ADAM_EPS = 1e-08
DECAY = 0.1
RATE_MATRIX = 0.02
RATE_OUTPUT = 0.1
RATE_GAIN = 0.8

LANES = 128
SPARE = 6 * 1024 * 1024
PAIR = 2 * HD
BF = jnp.bfloat16
F32 = jnp.float32
MASKED = -1e30
SCALE = HD**-0.5

NZ, NY, NX = 4, 2, 2
CHIPS = NZ * NY * NX


def call(kernel, out_shape, args, smem=(), scratch=(), flops=0, name=None):
    spaces = [
        pl.BlockSpec(memory_space=pltpu.SMEM if i in smem else pltpu.VMEM) for i in range(len(args))
    ]
    shapes = [jax.ShapeDtypeStruct(s, d) for s, d in out_shape]
    moved = sum(a.size * a.dtype.itemsize for a in [*args, *shapes])
    held = moved + sum(math.prod(r.shape) * jnp.dtype(r.dtype).itemsize for r in scratch)
    return pl.pallas_call(
        kernel,
        out_shape=shapes,
        in_specs=spaces,
        out_specs=[pl.BlockSpec(memory_space=pltpu.VMEM)] * len(shapes),
        scratch_shapes=list(scratch),
        compiler_params=pltpu.CompilerParams(vmem_limit_bytes=held + SPARE),
        cost_estimate=pl.CostEstimate(flops=int(flops), bytes_accessed=moved, transcendentals=0),
        name=name,
    )(*args)


def dot(a, b):
    return jnp.dot(a, b, preferred_element_type=F32)


def dot_nt(a, b):
    return lax.dot_general(a, b, (((1,), (1,)), ((), ())), preferred_element_type=F32)


def dot_tn(a, b):
    return lax.dot_general(a, b, (((0,), (0,)), ((), ())), preferred_element_type=F32)


def norm_parts(values):
    centre = jnp.mean(values, axis=-1, keepdims=True)
    shifted = values - centre
    spread = jnp.mean(shifted * shifted, axis=-1, keepdims=True)
    inverse = lax.rsqrt(spread + EPSILON)
    return shifted * inverse, inverse


def norm_back(normed, inverse, grads, gain):
    scaled = grads * gain
    mean_one = jnp.mean(scaled, axis=-1, keepdims=True)
    mean_two = jnp.mean(scaled * normed, axis=-1, keepdims=True)
    return (scaled - mean_one - normed * mean_two) * inverse


def assemble_kernel(place, near_a, far_a, near_b, far_b, whole):
    z, y, x = place[0], place[1], place[2]
    rows, cut = near_a.shape[2], near_a.shape[3]
    for near in range(2):
        for k in range(NZ):
            for far in range(2):
                z_of = lax.rem(z + NZ - k, NZ) * 4
                row_a = z_of + (y ^ far) * 2 + (x ^ near)
                row_b = z_of + (y ^ near) * 2 + (x ^ far)
                at_a = pl.ds(pl.multiple_of(row_a * rows, rows), rows)
                at_b = pl.ds(pl.multiple_of(row_b * rows, rows), rows)
                whole[at_a, :cut] = (far_a if far else near_a)[near, k]
                whole[at_b, cut:] = (far_b if far else near_b)[near, k]


def assemble(place, near_a, far_a, near_b, far_b):
    rows = near_a.shape[2]
    columns = near_a.shape[3] + near_b.shape[3]
    return call(
        assemble_kernel,
        [((CHIPS * rows, columns), BF)],
        (place, near_a, far_a, near_b, far_b),
        smem=(0,),
        name="assemble",
    )[0]


def swap_halves(u):
    lane = lax.broadcasted_iota(jnp.int32, u.shape, 1)
    ahead = pltpu.roll(u, LANES - HD // 2, 1)
    behind = pltpu.roll(u, HD // 2, 1)
    return jnp.where(lane % HD < HD // 2, ahead, behind)


def qkv_kernel(inputs, gains, weight, cosine, sine, first_norm, mixed):
    feats = mixed.shape[1] // 3
    step = 256
    for start in range(0, inputs.shape[0], step):
        rows = pl.ds(start, step)
        normed, _ = norm_parts(inputs[rows, :].astype(F32))
        low = (normed * gains[0:1, :]).astype(BF)
        first_norm[rows, :] = low
        place = pl.ds(start % LEN, step)
        cos_rows, sin_rows = cosine[place, :], sine[place, :]
        product = dot(low, weight[:, feats : 4 * feats])
        for j in range(2 * feats // LANES):
            at = slice(j * LANES, (j + 1) * LANES)
            u = product[:, at]
            turned = (u * cos_rows + swap_halves(u) * sin_rows).astype(BF)
            if j < feats // LANES:
                turned = turned * jnp.asarray(SCALE, BF)
            mixed[rows, at] = turned
        mixed[rows, 2 * feats :] = product[:, 2 * feats :].astype(BF)


def visible_bias(length):
    row = lax.broadcasted_iota(jnp.int32, (LEN, LEN), 0) // BLOCK
    place = lax.broadcasted_iota(jnp.int32, (LEN, LEN), 1)
    col = place // BLOCK
    real = place < length
    bias = lambda seen: jnp.where(seen & real, 0.0, MASKED).astype(F32)
    noisy = jnp.concatenate([bias(col == row), bias(col < row)], axis=1)
    return noisy, bias(col <= row)


def own_lanes(value, head):
    lane = lax.broadcasted_iota(jnp.int32, value.shape, 1)
    mine = (lane < HD) if head == 0 else (lane >= HD)
    return jnp.where(mine, value, jnp.zeros_like(value))


def attend_kernel(micro, lengths, mixed, weight, heads, logsums, part):
    feats = heads.shape[1]
    bias_noisy, bias_clean = visible_bias(lengths[micro])
    lane = lax.broadcasted_iota(jnp.int32, (LEN, LANES), 1)
    base = micro * 2 * LEN
    sums = [jnp.zeros((LEN, LANES), F32), jnp.zeros((LEN, LANES), F32)]
    for pair in range(feats // PAIR):
        query, key, value = (
            mixed[pl.ds(base, 2 * LEN), c * feats + pair * PAIR : c * feats + (pair + 1) * PAIR]
            for c in range(3)
        )
        outs = [None, None]
        for head in range(2):
            mine = own_lanes(query, head)
            for clean in range(2):
                keys = key[LEN:] if clean else key
                values = value[LEN:] if clean else value
                scores = dot_nt(mine[clean * LEN : (clean + 1) * LEN], keys)
                scores = scores + (bias_clean if clean else bias_noisy)
                maximum = jnp.max(scores, axis=-1, keepdims=True)
                raised = jnp.exp(scores - maximum)
                summed = jnp.sum(raised, axis=-1, keepdims=True)
                weights = (raised * (1.0 / summed)).astype(BF)
                out = dot(weights, values)
                outs[clean] = out if head == 0 else jnp.where(lane < HD, outs[clean], out)
                sums[clean] = jnp.where(
                    lane == pair * 2 + head, maximum + jnp.log(summed), sums[clean]
                )
        for clean in range(2):
            heads[clean * LEN : (clean + 1) * LEN, pair * PAIR : (pair + 1) * PAIR] = outs[
                clean
            ].astype(BF)
    for clean in range(2):
        rows = slice(clean * LEN, (clean + 1) * LEN)
        logsums[rows, :] = sums[clean]
        part[rows, :] = dot_nt(heads[rows, :], weight[:, :feats]).astype(BF)


ERF_NUM = (
    -2.72614225801306e-10,
    2.77068142495902e-08,
    -2.10102402082508e-06,
    -5.69250639462346e-05,
    -7.34990630326855e-04,
    -2.95459980854025e-03,
    -1.60960333262415e-02,
)
ERF_DEN = (
    -1.45660718464996e-05,
    -2.13374055278905e-04,
    -1.68282697438203e-03,
    -7.37332916720468e-03,
    -1.42647390514189e-02,
)


def gelu_parts(v):
    u = jnp.clip(v * (0.5**0.5), -4.0, 4.0)
    square = u * u
    num = jnp.full_like(u, ERF_NUM[0])
    for c in ERF_NUM[1:]:
        num = num * square + c
    den = jnp.full_like(u, ERF_DEN[0])
    for c in ERF_DEN[1:]:
        den = den * square + c
    half = 0.5 + 0.5 * (u * num / den)
    bell = jnp.exp(v * v * -0.5) * 0.3989422804014327
    return v * half, half + v * bell


def upper_kernel(micro, inputs, own, other, gains, weight, middle, second_norm, active, slope):
    base = micro * 2 * LEN
    step, wide = 256, 512
    for start in range(0, 2 * LEN, step):
        rows = pl.ds(start, step)
        value = inputs[pl.ds(base + start, step), :].astype(F32) + (
            own[rows, :].astype(F32) + other[rows, :].astype(F32)
        )
        middle[rows, :] = value
        normed, _ = norm_parts(value)
        low = (normed * gains[1:2, :]).astype(BF)
        second_norm[rows, :] = low
        for c in range(0, weight.shape[1], wide):
            out, grad = gelu_parts(dot(low, weight[:, c : c + wide]))
            active[rows, c : c + wide] = out.astype(BF)
            slope[rows, c : c + wide] = grad.astype(BF)


def masked_rows(cotangent, start, step, length):
    place = lax.broadcasted_iota(jnp.int32, (step, 1), 0) + start % LEN
    rows = cotangent[pl.ds(start, step), :]
    return jnp.where(place < length, rows, jnp.zeros_like(rows))


def hidden_back_kernel(micro, lengths, cotangent, slope, lower, upper, upper_grad, part):
    base = micro * 2 * LEN
    step, wide = 256, 512
    for start in range(0, 2 * LEN, step):
        rows = pl.ds(start, step)
        low = masked_rows(cotangent, base + start, step, lengths[micro])
        total = jnp.zeros((step, part.shape[1]), F32)
        for c in range(0, lower.shape[1], wide):
            grad = dot(low, lower[:, c : c + wide]) * slope[rows, c : c + wide].astype(F32)
            grad = grad.astype(BF)
            upper_grad[rows, c : c + wide] = grad
            total = total + dot_nt(grad, upper[:, c : c + wide])
        part[rows, :] = total.astype(BF)


def middle_back_kernel(
    micro, lengths, cotangent, own, other, middle, gains, weight, middle_grad, low, head_grad, gain
):
    base = micro * 2 * LEN
    step = 256
    feats = head_grad.shape[1]
    gain[...] = jnp.zeros_like(gain)
    for start in range(0, 2 * LEN, step):
        rows = pl.ds(start, step)
        upstream = masked_rows(cotangent, base + start, step, lengths[micro]).astype(F32)
        back = own[rows, :].astype(F32) + other[rows, :].astype(F32)
        normed, inverse = norm_parts(middle[rows, :])
        gain[0:1, :] += jnp.sum(back * normed, axis=0, keepdims=True)
        grad = upstream + norm_back(normed, inverse, back, gains[1:2, :])
        middle_grad[rows, :] = grad
        low_grad = grad.astype(BF)
        low[rows, :] = low_grad
        head_grad[rows, :] = dot(low_grad, weight[:, :feats]).astype(BF)


def attend_back_kernel(
    micro, lengths, mixed, logsums, head_grad, cosine, sine, mixed_grad, key_sum, value_sum
):
    feats = head_grad.shape[1]
    bias_noisy, bias_clean = visible_bias(lengths[micro])
    base = micro * 2 * LEN
    cos_rows, sin_rows = cosine[...], sine[...]

    def turn_back(u):
        return u * cos_rows - swap_halves(u) * sin_rows

    lane = lax.broadcasted_iota(jnp.int32, (LEN, LANES), 1)
    for pair in range(feats // PAIR):
        cols = [
            slice(c * feats + pair * PAIR, c * feats + (pair + 1) * PAIR) for c in range(3)
        ]
        query, key, value = (mixed[pl.ds(base, 2 * LEN), c] for c in cols)
        upstream = head_grad[:, pair * PAIR : (pair + 1) * PAIR]
        query_grads = [None, None]
        for head in range(2):
            mine, mine_grad = own_lanes(query, head), own_lanes(upstream, head)
            for clean in range(2):
                rows = slice(clean * LEN, (clean + 1) * LEN)
                keys = key[LEN:] if clean else key
                values = value[LEN:] if clean else value
                at = pair * 2 + head
                scores = dot_nt(mine[rows], keys) + (bias_clean if clean else bias_noisy)
                probs = jnp.exp(scores - logsums[rows, at : at + 1])
                prob_grads = dot_nt(mine_grad[rows], values)
                inner = jnp.sum(probs * prob_grads, axis=-1, keepdims=True)
                score_grads = (probs * (prob_grads - inner)).astype(BF)
                grads = dot(score_grads, keys)
                query_grads[clean] = (
                    grads if head == 0 else jnp.where(lane < HD, query_grads[clean], grads)
                )
                key_part = dot_tn(score_grads, mine[rows])
                value_part = dot_tn(probs.astype(BF), mine_grad[rows])
                if head == 0 and not clean:
                    key_sum[...] = key_part
                    value_sum[...] = value_part
                elif not clean:
                    key_sum[...] += key_part
                    value_sum[...] += value_part
                else:
                    key_sum[LEN:, :] += key_part
                    value_sum[LEN:, :] += value_part
        for clean in range(2):
            rows = slice(clean * LEN, (clean + 1) * LEN)
            mixed_grad[rows, cols[0]] = turn_back(query_grads[clean] * SCALE).astype(BF)
            mixed_grad[rows, cols[1]] = turn_back(key_sum[rows, :]).astype(BF)
            mixed_grad[rows, cols[2]] = value_sum[rows, :].astype(BF)


def put_blocks(place, product, scratch, column, x_first):
    z, y, x = place[0], place[1], place[2]
    rows = product.shape[0] // CHIPS
    for chip in range(CHIPS):
        to_z = lax.rem(chip // 4 + NZ - z, NZ)
        to_y, to_x = y ^ (chip // 2 % 2), x ^ (chip % 2)
        at = (to_x * 2 + to_y if x_first else to_y * 2 + to_x) * NZ + to_z
        scratch[pl.ds(pl.multiple_of(at * rows, rows), rows), column] = product[
            chip * rows : (chip + 1) * rows
        ].astype(BF)


def write_products(place, products, outs, scratch):
    if len(outs) == 1:
        for column, value in products:
            outs[0][:, column : column + value.shape[1]] = value.astype(BF)
        return
    cut = outs[0].shape[1]
    for column, value in products:
        for half in range(2):
            low, high = max(column, half * cut), min(column + value.shape[1], (half + 1) * cut)
            if low < high:
                put_blocks(
                    place,
                    value[:, low - column : high - column],
                    scratch.at[half],
                    slice(low - half * cut, high - half * cut),
                    half == 0,
                )
    size = outs[0].shape[0]
    for half in range(2):
        outs[2 * half][...] = scratch[half, :size]
        outs[2 * half + 1][...] = scratch[half, size:]


def product_out(width, columns, local):
    if local:
        return [((width // 2, columns // 2), BF)] * 4, [pltpu.VMEM((2, width, columns // 2), BF)]
    return [((width, columns), BF)], []


def wide_grad_kernel(outs, masked, place, lengths, *refs):
    count = 1 if masked else 2
    lefts, rights = refs[:count], refs[count : count + 2]
    refs = refs[count + 2 :]
    out_refs, scratch = refs[:outs], refs[outs:]
    turned = scratch[0]
    rows = 2 * LEN
    for micro in range(2):
        if masked:
            for start in range(0, rows, LEN):
                low = masked_rows(lefts[0], micro * rows + start, LEN, lengths[micro])
                turned[:, micro * rows + start : micro * rows + start + LEN] = low.T
        else:
            turned[:, micro * rows : (micro + 1) * rows] = lefts[micro][...].T
    wide = 256
    products = []
    for c in range(0, rights[0].shape[1], wide):
        total = dot(turned[:, :rows], rights[0][:, c : c + wide])
        total = total + dot(turned[:, rows:], rights[1][:, c : c + wide])
        products.append((c, total))
    write_products(place, products, out_refs, scratch[1] if outs > 1 else None)


def wide_grad(place, lengths, lefts, rights, masked, local, name):
    width, columns = lefts[0].shape[1], rights[0].shape[1]
    out, scratch = product_out(width, columns, local)
    return call(
        partial(wide_grad_kernel, len(out), masked),
        out,
        (place, lengths, *lefts, *rights),
        smem=(0, 1),
        scratch=[pltpu.VMEM((width, 4 * LEN), BF)] + scratch,
        name=name,
    )


def proj_grad_kernel(outs, place, *refs):
    norms, mixed_grads, lows, heads = refs[0], refs[1:3], refs[3:5], refs[5:7]
    out_refs, scratch = refs[7 : 7 + outs], refs[7 + outs :]
    turned = scratch[0]
    rows = 2 * LEN
    products = []
    for micro in range(2):
        turned[:, micro * rows : (micro + 1) * rows] = lows[micro][...].T
    total = dot(turned[:, :rows], heads[0][...]) + dot(turned[:, rows:], heads[1][...])
    products.append((0, total))
    feats = heads[0].shape[1]
    for micro in range(2):
        turned[:, micro * rows : (micro + 1) * rows] = norms[pl.ds(micro * rows, rows), :].T
    for c in range(0, 3 * feats, feats):
        total = dot(turned[:, :rows], mixed_grads[0][:, c : c + feats])
        total = total + dot(turned[:, rows:], mixed_grads[1][:, c : c + feats])
        products.append((feats + c, total))
    write_products(place, products, out_refs, scratch[1] if outs > 1 else None)


def proj_grad(place, first_norm, mixed_grads, lows, heads, local):
    width, columns = first_norm.shape[1], 4 * heads[0].shape[1]
    out, scratch = product_out(width, columns, local)
    return call(
        partial(proj_grad_kernel, len(out)),
        out,
        (place, first_norm, *mixed_grads, *lows, *heads),
        smem=(0,),
        scratch=[pltpu.VMEM((width, 4 * LEN), BF)] + scratch,
        name="proj_grad",
    )


def chip_pairs(move):
    pairs = []
    for chip in range(CHIPS):
        to_z, to_y, to_x = move(chip // 4, chip // 2 % 2, chip % 2)
        pairs.append((chip, to_z * 4 + to_y * 2 + to_x))
    return pairs


SWAP_X = chip_pairs(lambda z, y, x: (z, y, 1 - x))
SWAP_Y = chip_pairs(lambda z, y, x: (z, 1 - y, x))
SHIFT_Z = {k: chip_pairs(lambda z, y, x, k=k: ((z + k) % NZ, y, x)) for k in (1, 2, 3)}


def exchange(value, pairs, name):
    with jax.named_scope(name):
        return lax.ppermute(value, "dp", pairs)


tie = lax.optimization_barrier


def start_gather(name, shard):
    if lax.axis_size("dp") != CHIPS:
        return [lax.all_gather(shard, "dp", axis=0, tiled=True)]
    return [shard] + [exchange(shard, SHIFT_Z[k], f"{name}_z{k}") for k in (1, 2, 3)]


def spread_near(name, arrived, cut):
    if len(arrived) == 1:
        return arrived
    part_a = jnp.stack([a[:, :cut] for a in arrived])
    part_b = jnp.stack([a[:, cut:] for a in arrived])
    near_a = jnp.stack([part_a, exchange(part_a, SWAP_X, f"{name}_near_a")])
    near_b = jnp.stack([part_b, exchange(part_b, SWAP_Y, f"{name}_near_b")])
    return [near_a, near_b]


def spread_far(name, near):
    if len(near) == 1:
        return near
    near_a, near_b = near
    far_a = exchange(near_a, SWAP_Y, f"{name}_far_a")
    return [near_a, far_a, near_b, exchange(near_b, SWAP_X, f"{name}_far_b")]


def assembled(place, pieces):
    return pieces[0] if len(pieces) == 1 else assemble(place, *pieces)


def scatter_first(name, parts):
    if len(parts) == 1:
        return parts
    halves = []
    for tag, kept, sent, move in (("a", *parts[:2], SWAP_X), ("b", *parts[2:], SWAP_Y)):
        rows, columns = kept.shape[0] // (2 * NZ), kept.shape[1]
        half = kept.astype(F32) + exchange(sent, move, f"{name}_first_{tag}").astype(F32)
        halves.append(half.reshape(2, NZ, rows, columns))
    return halves


def scatter_second(name, halves):
    if len(halves) == 1:
        return halves
    return [
        half[0] + exchange(half[1].astype(BF), move, f"{name}_second_{tag}").astype(F32)
        for tag, half, move in zip("ab", halves, (SWAP_Y, SWAP_X))
    ]


def scatter_last(name, columns):
    if len(columns) == 1:
        return lax.psum_scatter(columns[0], "dp", scatter_dimension=0, tiled=True).astype(F32)
    column = jnp.concatenate(columns, axis=-1)
    total = column[0]
    for k in (1, 2, 3):
        total = total + exchange(column[k].astype(BF), SHIFT_Z[k], f"{name}_z{k}").astype(F32)
    return total


def swapped(value):
    return lax.ppermute(value, "mp", [(0, 1), (1, 0)])


def rotation(row_count, head_width):
    halfway = head_width // 2
    freqs = 10000.0 ** (-2.0 * jnp.arange(halfway).astype(jnp.float32) / head_width)
    places = (jnp.arange(row_count) % LEN).astype(jnp.float32)
    angles = places[:, None] * freqs[None, :]
    return (jnp.cos(angles), jnp.sin(angles))


def adamw_update(weight, first, second, grad, rate, decay):
    first_new = BETA_ONE * first + (1.0 - BETA_ONE) * grad
    second_new = BETA_TWO * second + (1.0 - BETA_TWO) * grad * grad
    corrected = (
        first_new
        / (1.0 - BETA_ONE**STEP)
        / (jnp.sqrt(second_new / (1.0 - BETA_TWO**STEP)) + ADAM_EPS)
    )
    return (weight - rate * (corrected + decay * weight), first_new, second_new)


def shards(
    inputs,
    cotangent,
    lengths,
    proj_weight,
    output_weight,
    upper_weight,
    lower_weight,
    norm_gains,
    proj_first,
    output_first,
    upper_first,
    lower_first,
    gains_first,
    proj_second,
    output_second,
    upper_second,
    lower_second,
    gains_second,
):
    micro_count, _, row_count, width = inputs.shape
    feats = proj_weight.shape[2]
    hidden = upper_weight.shape[1]
    shard_rows = proj_weight.shape[0]
    local = lax.axis_size("dp") == CHIPS
    chip = lax.axis_index("dp").astype(jnp.int32)
    place = jnp.stack([chip // 4, chip // 2 % 2, chip % 2])
    micros = range(micro_count)
    lengths = lengths.reshape(-1)
    flat_in = inputs.reshape(-1, width)
    flat_ct = cotangent.reshape(-1, width)

    cosine, sine = rotation(LEN, HD)
    cosine = jnp.tile(cosine, (1, 4))
    sine = jnp.tile(jnp.concatenate([-sine, sine], axis=1), (1, 2))

    gain_columns = jnp.pad(norm_gains.T.astype(BF), ((0, 0), (0, LANES - 2)))
    shard_one = jnp.concatenate(
        [
            output_weight.astype(BF).T,
            proj_weight.astype(BF).reshape(shard_rows, 3 * feats),
            gain_columns,
        ],
        axis=1,
    )
    upper_low, lower_low = upper_weight.astype(BF), lower_weight.astype(BF).T
    arrived = start_gather("one", shard_one)
    upper_low, arrived = tie((upper_low, arrived))
    near = spread_near("one", arrived, 2 * feats)
    arrived_upper = start_gather("upper", upper_low)
    pieces = spread_far("one", near)
    arrived_upper, lower_low, pieces = tie((arrived_upper, lower_low, pieces))
    near_upper = spread_near("upper", arrived_upper, hidden // 2)
    arrived_lower = start_gather("lower", lower_low)
    one = assembled(place, pieces)
    gains_c = jnp.pad(one[:, 4 * feats : 4 * feats + 2].T.astype(F32), ((0, 6), (0, 0)))

    total_rows = micro_count * row_count
    first_norm, mixed = call(
        qkv_kernel,
        [((total_rows, width), BF), ((total_rows, 3 * feats), BF)],
        (flat_in, gains_c, one, cosine, sine),
        name="qkv",
    )
    heads, logsums, attn = [], [], []
    for m in micros:
        if m:
            mixed, near_upper, attn = tie((mixed, near_upper, attn))
            far_upper = spread_far("upper", near_upper)
        h, s, p = call(
            partial(attend_kernel, m),
            [((row_count, feats), BF), ((row_count, LANES), F32), ((row_count, width), BF)],
            (lengths, mixed, one),
            smem=(0,),
            name="attend",
        )
        heads.append(h)
        logsums.append(s)
        attn.append(p)
    far_upper, arrived_lower, attn = tie((far_upper, arrived_lower, attn))
    near_lower = spread_near("lower", arrived_lower, hidden // 2)
    upper_c = assembled(place, far_upper)
    middle, second_norm, active, slope = [], [], [], []
    for m in micros:
        if m:
            upper_c, near_lower, active = tie((upper_c, near_lower, active))
            far_lower = spread_far("lower", near_lower)
        outs = call(
            partial(upper_kernel, m),
            [
                ((row_count, width), F32),
                ((row_count, width), BF),
                ((row_count, hidden), BF),
                ((row_count, hidden), BF),
            ],
            (flat_in, attn[m], swapped(attn[m]), gains_c, upper_c),
            name="upper",
        )
        for kept, out in zip((middle, second_norm, active, slope), outs):
            kept.append(out)
    active, far_lower = tie((active, far_lower))
    lower_parts = wide_grad(place, lengths, [flat_ct], active, True, local, "lower_grad")
    lower_half = scatter_first("lower_sum", lower_parts)
    lower_t = assembled(place, far_lower)
    upper_grads, seconds, crossed = [], [], []
    for m in micros:
        if m:
            lower_t, lower_half, seconds = tie((lower_t, lower_half, seconds))
            lower_column = scatter_second("lower_sum", lower_half)
            crossed.append(swapped(seconds[0]))
        grad, part = call(
            partial(hidden_back_kernel, m),
            [((row_count, hidden), BF), ((row_count, width), BF)],
            (lengths, flat_ct, slope[m], lower_t, upper_c),
            smem=(0,),
            name="hidden_back",
        )
        upper_grads.append(grad)
        seconds.append(part)
    upper_grads, lower_column, seconds = tie((upper_grads, lower_column, seconds))
    crossed.append(swapped(seconds[1]))
    lower_sum = scatter_last("lower_sum", lower_column)
    upper_parts = wide_grad(place, lengths, second_norm, upper_grads, False, local, "upper_grad")
    upper_half = scatter_first("upper_sum", upper_parts)
    middle_grads, lows, mixed_grads, gain_two = [], [], [], []
    for m in micros:
        if m:
            upper_column, mixed_grads, crossed = tie((upper_column, mixed_grads, crossed))
            upper_sum = scatter_last("upper_sum", upper_column)
        middle_grad, low, head_grad, gain = call(
            partial(middle_back_kernel, m),
            [
                ((row_count, width), F32),
                ((row_count, width), BF),
                ((row_count, feats), BF),
                ((8, width), F32),
            ],
            (lengths, flat_ct, seconds[m], crossed[m], middle[m], gains_c, one),
            smem=(0,),
            name="middle_back",
        )
        if m == 0:
            head_grad, upper_half, lower_sum = tie((head_grad, upper_half, lower_sum))
            upper_column = scatter_second("upper_sum", upper_half)
        mixed_grads += call(
            partial(attend_back_kernel, m),
            [((row_count, 3 * feats), BF)],
            (lengths, mixed, logsums[m], head_grad, cosine, sine),
            smem=(0,),
            scratch=[pltpu.VMEM((row_count, LANES), F32)] * 2,
            name="attend_back",
        )
        middle_grads.append(middle_grad)
        lows.append(low)
        gain_two.append(gain[0])
    mixed_grads, upper_sum = tie((mixed_grads, upper_sum))
    one_parts = proj_grad(place, first_norm, mixed_grads, lows, heads, local)
    active, mixed_grads, one_parts = tie((active, mixed_grads, one_parts))
    one_column = scatter_second("one_sum", scatter_first("one_sum", one_parts))
    one_grad = scatter_last("one_sum", one_column)

    results, input_grads, gain_one = [], [], []
    for m in micros:
        ffn = dot_nt(active[m], lower_t).astype(BF)
        result = middle[m] + (ffn.astype(F32) + swapped(ffn).astype(F32))
        results.append(result.astype(BF).reshape(inputs.shape[1:]))
        back = dot_nt(mixed_grads[m], one[:, feats : 4 * feats]).astype(BF)
        back = back.astype(F32) + swapped(back).astype(F32)
        normed, inverse = norm_parts(inputs[m, 0].astype(F32))
        gain_one.append(jnp.sum(back * normed, axis=0))
        grad = middle_grads[m] + norm_back(normed, inverse, back, gains_c[0:1])
        input_grads.append(grad.reshape(inputs.shape[1:]))
    gain_parts = jnp.stack([sum(gain_one), sum(gain_two)]).reshape(2, -1, shard_rows)
    gain_parts = lax.all_to_all(gain_parts.transpose(1, 0, 2), "dp", 0, 0, tiled=True)
    gains_grad = jnp.sum(gain_parts, axis=0)
    proj_wgrad = one_grad[:, feats:].reshape(proj_weight.shape)
    output_grad = one_grad[:, :feats].T

    updates = [
        adamw_update(proj_weight, proj_first, proj_second, proj_wgrad, RATE_MATRIX, DECAY),
        adamw_update(output_weight, output_first, output_second, output_grad, RATE_OUTPUT, DECAY),
        adamw_update(upper_weight, upper_first, upper_second, upper_sum, RATE_MATRIX, DECAY),
        adamw_update(lower_weight, lower_first, lower_second, lower_sum.T, RATE_MATRIX, DECAY),
        adamw_update(norm_gains, gains_first, gains_second, gains_grad, RATE_GAIN, 0.0),
    ]
    return (
        jnp.stack(results),
        jnp.stack(input_grads),
        *[u[0] for u in updates],
        *[u[1] for u in updates],
        *[u[2] for u in updates],
        *[u[0].astype(BF) for u in updates],
    )


def solution(mesh):
    rows = P(None, "dp", None, None)
    weights = (P("dp", None, "mp"), P("mp", "dp"), P("dp", "mp"), P("mp", "dp"), P(None, "dp"))
    in_specs = (rows, rows, P(None, "dp"), *weights * 3)
    out_specs = (rows, rows, *weights * 4)
    return jax.shard_map(shards, mesh=mesh, in_specs=in_specs, out_specs=out_specs, check_vma=False)
```

```python
import math
from functools import partial

import jax
import jax.numpy as jnp
from jax import lax
from jax.experimental import pallas as pl
from jax.experimental.pallas import tpu as pltpu
from jax.sharding import PartitionSpec as P

HD = 64
BLOCK = 16
LEN = 256
STEP = 10

EPSILON = 1e-05
BETA_ONE = 0.9
BETA_TWO = 0.95
ADAM_EPS = 1e-08
DECAY = 0.1
RATE_MATRIX = 0.02
RATE_OUTPUT = 0.1
RATE_GAIN = 0.8

LANES = 128
SPARE = 6 * 1024 * 1024
PAIR = 2 * HD
BF = jnp.bfloat16
F32 = jnp.float32
MASKED = -1e30
SCALE = HD**-0.5

NZ, NY, NX = 4, 2, 2
CHIPS = NZ * NY * NX


def call(kernel, out_shape, args, smem=(), scratch=(), flops=0, name=None):
    spaces = [
        pl.BlockSpec(memory_space=pltpu.SMEM if i in smem else pltpu.VMEM) for i in range(len(args))
    ]
    shapes = [jax.ShapeDtypeStruct(s, d) for s, d in out_shape]
    moved = sum(a.size * a.dtype.itemsize for a in [*args, *shapes])
    held = moved + sum(math.prod(r.shape) * jnp.dtype(r.dtype).itemsize for r in scratch)
    return pl.pallas_call(
        kernel,
        out_shape=shapes,
        in_specs=spaces,
        out_specs=[pl.BlockSpec(memory_space=pltpu.VMEM)] * len(shapes),
        scratch_shapes=list(scratch),
        compiler_params=pltpu.CompilerParams(vmem_limit_bytes=held + SPARE),
        cost_estimate=pl.CostEstimate(flops=int(flops), bytes_accessed=moved, transcendentals=0),
        name=name,
    )(*args)


def dot(a, b):
    return jnp.dot(a, b, preferred_element_type=F32)


def dot_nt(a, b):
    return lax.dot_general(a, b, (((1,), (1,)), ((), ())), preferred_element_type=F32)


def dot_tn(a, b):
    return lax.dot_general(a, b, (((0,), (0,)), ((), ())), preferred_element_type=F32)


def norm_parts(values):
    centre = jnp.mean(values, axis=-1, keepdims=True)
    shifted = values - centre
    spread = jnp.mean(shifted * shifted, axis=-1, keepdims=True)
    inverse = lax.rsqrt(spread + EPSILON)
    return shifted * inverse, inverse


def norm_back(normed, inverse, grads, gain):
    scaled = grads * gain
    mean_one = jnp.mean(scaled, axis=-1, keepdims=True)
    mean_two = jnp.mean(scaled * normed, axis=-1, keepdims=True)
    return (scaled - mean_one - normed * mean_two) * inverse


def stack_kernel(*refs):
    pieces, (part_a, part_b) = refs[:NZ], refs[NZ:]
    rows, cut = pieces[0].shape[0], part_a.shape[1]
    for k, piece in enumerate(pieces):
        at = slice(k * rows, (k + 1) * rows)
        part_a[at, :] = piece[:, :cut]
        part_b[at, :] = piece[:, cut:]


def pair_kernel(part_a, got_a, part_b, got_b, near_a, near_b):
    rows = part_a.shape[0]
    for part, got, near in ((part_a, got_a, near_a), (part_b, got_b, near_b)):
        near[:rows, :] = part[...]
        near[rows:, :] = got[...]


def assemble_kernel(place, near_a, far_a, near_b, far_b, whole):
    z, y, x = place[0], place[1], place[2]
    rows, cut = near_a.shape[0] // (2 * NZ), near_a.shape[1]
    for near in range(2):
        for k in range(NZ):
            at = slice((near * NZ + k) * rows, (near * NZ + k + 1) * rows)
            for far in range(2):
                z_of = lax.rem(z + NZ - k, NZ) * 4
                row_a = z_of + (y ^ far) * 2 + (x ^ near)
                row_b = z_of + (y ^ near) * 2 + (x ^ far)
                to_a = pl.ds(pl.multiple_of(row_a * rows, rows), rows)
                to_b = pl.ds(pl.multiple_of(row_b * rows, rows), rows)
                whole[to_a, :cut] = (far_a if far else near_a)[at, :]
                whole[to_b, cut:] = (far_b if far else near_b)[at, :]


def join_kernel(near, far, block):
    rows = near.shape[0]
    block[:rows, :] = near[...]
    block[rows:, :] = far[...]


def assemble_late_kernel(place, blocks_a, blocks_b, whole):
    z, y, x = place[0], place[1], place[2]
    rows, cut = blocks_a[0].shape[0] // 4, blocks_a[0].shape[1]
    for k, (block_a, block_b) in enumerate(zip(blocks_a, blocks_b)):
        z_of = lax.rem(z + NZ - k, NZ) * 4
        for far in range(2):
            for near in range(2):
                at = slice((far * 2 + near) * rows, (far * 2 + near + 1) * rows)
                row_a = z_of + (y ^ far) * 2 + (x ^ near)
                row_b = z_of + (y ^ near) * 2 + (x ^ far)
                to_a = pl.ds(pl.multiple_of(row_a * rows, rows), rows)
                to_b = pl.ds(pl.multiple_of(row_b * rows, rows), rows)
                whole[to_a, :cut] = block_a[at, :]
                whole[to_b, cut:] = block_b[at, :]


def half_kernel(kept_a, got_a, kept_b, got_b, own_a, send_a, own_b, send_b):
    rows = own_a.shape[0]
    for kept, got, own, send in ((kept_a, got_a, own_a, send_a), (kept_b, got_b, own_b, send_b)):
        own[...] = kept[:rows, :].astype(F32) + got[:rows, :].astype(F32)
        send[...] = (kept[rows:, :].astype(F32) + got[rows:, :].astype(F32)).astype(BF)


def column_kernel(own_a, got_a, own_b, got_b, mine, *sends):
    rows, cut = mine.shape[0], own_a.shape[1]
    for columns, own, got in ((slice(0, cut), own_a, got_a), (slice(cut, None), own_b, got_b)):
        mine[:, columns] = own[:rows, :] + got[:rows, :].astype(F32)
        for k, send in enumerate(sends, 1):
            at = slice(k * rows, (k + 1) * rows)
            send[:, columns] = (own[at, :] + got[at, :].astype(F32)).astype(BF)


def swap_halves(u):
    lane = lax.broadcasted_iota(jnp.int32, u.shape, 1)
    ahead = pltpu.roll(u, LANES - HD // 2, 1)
    behind = pltpu.roll(u, HD // 2, 1)
    return jnp.where(lane % HD < HD // 2, ahead, behind)


def qkv_kernel(inputs, gains, weight, cosine, sine, first_norm, mixed):
    feats = mixed.shape[1] // 3
    step = 256
    for start in range(0, inputs.shape[0], step):
        rows = pl.ds(start, step)
        normed, _ = norm_parts(inputs[rows, :].astype(F32))
        low = (normed * gains[0:1, :]).astype(BF)
        first_norm[rows, :] = low
        place = pl.ds(start % LEN, step)
        cos_rows, sin_rows = cosine[place, :], sine[place, :]
        product = dot(low, weight[:, feats : 4 * feats])
        for j in range(2 * feats // LANES):
            at = slice(j * LANES, (j + 1) * LANES)
            u = product[:, at]
            turned = (u * cos_rows + swap_halves(u) * sin_rows).astype(BF)
            if j < feats // LANES:
                turned = turned * jnp.asarray(SCALE, BF)
            mixed[rows, at] = turned
        mixed[rows, 2 * feats :] = product[:, 2 * feats :].astype(BF)


def visible_bias(length):
    row = lax.broadcasted_iota(jnp.int32, (LEN, LEN), 0) // BLOCK
    place = lax.broadcasted_iota(jnp.int32, (LEN, LEN), 1)
    col = place // BLOCK
    real = place < length
    bias = lambda seen: jnp.where(seen & real, 0.0, MASKED).astype(F32)
    noisy = jnp.concatenate([bias(col == row), bias(col < row)], axis=1)
    return noisy, bias(col <= row)


def own_lanes(value, head):
    lane = lax.broadcasted_iota(jnp.int32, value.shape, 1)
    mine = (lane < HD) if head == 0 else (lane >= HD)
    return jnp.where(mine, value, jnp.zeros_like(value))


def attend_kernel(micro, lengths, mixed, weight, heads, logsums, part):
    feats = heads.shape[1]
    bias_noisy, bias_clean = visible_bias(lengths[micro])
    lane = lax.broadcasted_iota(jnp.int32, (LEN, LANES), 1)
    base = micro * 2 * LEN
    sums = [jnp.zeros((LEN, LANES), F32), jnp.zeros((LEN, LANES), F32)]
    for pair in range(feats // PAIR):
        query, key, value = (
            mixed[pl.ds(base, 2 * LEN), c * feats + pair * PAIR : c * feats + (pair + 1) * PAIR]
            for c in range(3)
        )
        outs = [None, None]
        for head in range(2):
            mine = own_lanes(query, head)
            for clean in range(2):
                keys = key[LEN:] if clean else key
                values = value[LEN:] if clean else value
                scores = dot_nt(mine[clean * LEN : (clean + 1) * LEN], keys)
                scores = scores + (bias_clean if clean else bias_noisy)
                maximum = jnp.max(scores, axis=-1, keepdims=True)
                raised = jnp.exp(scores - maximum)
                summed = jnp.sum(raised, axis=-1, keepdims=True)
                weights = (raised * (1.0 / summed)).astype(BF)
                out = dot(weights, values)
                outs[clean] = out if head == 0 else jnp.where(lane < HD, outs[clean], out)
                sums[clean] = jnp.where(
                    lane == pair * 2 + head, maximum + jnp.log(summed), sums[clean]
                )
        for clean in range(2):
            heads[clean * LEN : (clean + 1) * LEN, pair * PAIR : (pair + 1) * PAIR] = outs[
                clean
            ].astype(BF)
    for clean in range(2):
        rows = slice(clean * LEN, (clean + 1) * LEN)
        logsums[rows, :] = sums[clean]
        part[rows, :] = dot_nt(heads[rows, :], weight[:, :feats]).astype(BF)


ERF_NUM = (
    -2.72614225801306e-10,
    2.77068142495902e-08,
    -2.10102402082508e-06,
    -5.69250639462346e-05,
    -7.34990630326855e-04,
    -2.95459980854025e-03,
    -1.60960333262415e-02,
)
ERF_DEN = (
    -1.45660718464996e-05,
    -2.13374055278905e-04,
    -1.68282697438203e-03,
    -7.37332916720468e-03,
    -1.42647390514189e-02,
)


def gelu_parts(v):
    u = jnp.clip(v * (0.5**0.5), -4.0, 4.0)
    square = u * u
    num = jnp.full_like(u, ERF_NUM[0])
    for c in ERF_NUM[1:]:
        num = num * square + c
    den = jnp.full_like(u, ERF_DEN[0])
    for c in ERF_DEN[1:]:
        den = den * square + c
    half = 0.5 + 0.5 * (u * num / den)
    bell = jnp.exp(v * v * -0.5) * 0.3989422804014327
    return v * half, half + v * bell


def upper_kernel(micro, inputs, own, other, gains, weight, middle, second_norm, active, slope):
    base = micro * 2 * LEN
    step, wide = 256, 512
    for start in range(0, 2 * LEN, step):
        rows = pl.ds(start, step)
        value = inputs[pl.ds(base + start, step), :].astype(F32) + (
            own[rows, :].astype(F32) + other[rows, :].astype(F32)
        )
        middle[rows, :] = value
        normed, _ = norm_parts(value)
        low = (normed * gains[1:2, :]).astype(BF)
        second_norm[rows, :] = low
        for c in range(0, weight.shape[1], wide):
            out, grad = gelu_parts(dot(low, weight[:, c : c + wide]))
            active[rows, c : c + wide] = out.astype(BF)
            slope[rows, c : c + wide] = grad.astype(BF)


def masked_rows(cotangent, start, step, length):
    place = lax.broadcasted_iota(jnp.int32, (step, 1), 0) + start % LEN
    rows = cotangent[pl.ds(start, step), :]
    return jnp.where(place < length, rows, jnp.zeros_like(rows))


def hidden_back_kernel(micro, lengths, cotangent, slope, lower, upper, upper_grad, part):
    base = micro * 2 * LEN
    step, wide = 256, 512
    for start in range(0, 2 * LEN, step):
        rows = pl.ds(start, step)
        low = masked_rows(cotangent, base + start, step, lengths[micro])
        total = jnp.zeros((step, part.shape[1]), F32)
        for c in range(0, lower.shape[1], wide):
            grad = dot(low, lower[:, c : c + wide]) * slope[rows, c : c + wide].astype(F32)
            grad = grad.astype(BF)
            upper_grad[rows, c : c + wide] = grad
            total = total + dot_nt(grad, upper[:, c : c + wide])
        part[rows, :] = total.astype(BF)


def middle_back_kernel(
    micro, lengths, cotangent, own, other, middle, gains, weight, middle_grad, low, head_grad, gain
):
    base = micro * 2 * LEN
    step = 256
    feats = head_grad.shape[1]
    for start in range(0, 2 * LEN, step):
        rows = pl.ds(start, step)
        upstream = masked_rows(cotangent, base + start, step, lengths[micro]).astype(F32)
        back = own[rows, :].astype(F32) + other[rows, :].astype(F32)
        normed, inverse = norm_parts(middle[rows, :])
        gain[0:1, :] += jnp.sum(back * normed, axis=0, keepdims=True)
        grad = upstream + norm_back(normed, inverse, back, gains[1:2, :])
        middle_grad[rows, :] = grad
        low_grad = grad.astype(BF)
        low[rows, :] = low_grad
        head_grad[rows, :] = dot(low_grad, weight[:, :feats]).astype(BF)


def attend_back_kernel(
    micro, lengths, mixed, logsums, head_grad, cosine, sine, mixed_grad, key_sum, value_sum
):
    feats = head_grad.shape[1]
    bias_noisy, bias_clean = visible_bias(lengths[micro])
    base = micro * 2 * LEN
    cos_rows, sin_rows = cosine[...], sine[...]

    def turn_back(u):
        return u * cos_rows - swap_halves(u) * sin_rows

    lane = lax.broadcasted_iota(jnp.int32, (LEN, LANES), 1)
    for pair in range(feats // PAIR):
        cols = [
            slice(c * feats + pair * PAIR, c * feats + (pair + 1) * PAIR) for c in range(3)
        ]
        query, key, value = (mixed[pl.ds(base, 2 * LEN), c] for c in cols)
        upstream = head_grad[pl.ds(base, 2 * LEN), pair * PAIR : (pair + 1) * PAIR]
        query_grads = [None, None]
        for head in range(2):
            mine, mine_grad = own_lanes(query, head), own_lanes(upstream, head)
            for clean in range(2):
                rows = slice(clean * LEN, (clean + 1) * LEN)
                keys = key[LEN:] if clean else key
                values = value[LEN:] if clean else value
                at = pair * 2 + head
                scores = dot_nt(mine[rows], keys) + (bias_clean if clean else bias_noisy)
                logsum = logsums[pl.ds(base + clean * LEN, LEN), at : at + 1]
                probs = jnp.exp(scores - logsum)
                prob_grads = dot_nt(mine_grad[rows], values)
                inner = jnp.sum(probs * prob_grads, axis=-1, keepdims=True)
                score_grads = (probs * (prob_grads - inner)).astype(BF)
                grads = dot(score_grads, keys)
                query_grads[clean] = (
                    grads if head == 0 else jnp.where(lane < HD, query_grads[clean], grads)
                )
                key_part = dot_tn(score_grads, mine[rows])
                value_part = dot_tn(probs.astype(BF), mine_grad[rows])
                if head == 0 and not clean:
                    key_sum[...] = key_part
                    value_sum[...] = value_part
                elif not clean:
                    key_sum[...] += key_part
                    value_sum[...] += value_part
                else:
                    key_sum[LEN:, :] += key_part
                    value_sum[LEN:, :] += value_part
        for clean in range(2):
            rows = slice(clean * LEN, (clean + 1) * LEN)
            mixed_grad[rows, cols[0]] = turn_back(query_grads[clean] * SCALE).astype(BF)
            mixed_grad[rows, cols[1]] = turn_back(key_sum[rows, :]).astype(BF)
            mixed_grad[rows, cols[2]] = value_sum[rows, :].astype(BF)


def put_blocks(place, product, scratch, column, x_first):
    z, y, x = place[0], place[1], place[2]
    rows = product.shape[0] // CHIPS
    for chip in range(CHIPS):
        to_z = lax.rem(chip // 4 + NZ - z, NZ)
        to_y, to_x = y ^ (chip // 2 % 2), x ^ (chip % 2)
        at = (to_x * 2 + to_y if x_first else to_y * 2 + to_x) * NZ + to_z
        scratch[pl.ds(pl.multiple_of(at * rows, rows), rows), column] = product[
            chip * rows : (chip + 1) * rows
        ].astype(BF)


def write_products(place, products, outs, scratch):
    if len(outs) == 1:
        for column, value in products:
            outs[0][:, column : column + value.shape[1]] = value.astype(BF)
        return
    cut = outs[0].shape[1]
    end = cut + outs[2].shape[1]
    for column, value in products:
        for part, (first, last) in enumerate(((0, cut), (cut, end))):
            low, high = max(column, first), min(column + value.shape[1], last)
            if low < high:
                put_blocks(
                    place,
                    value[:, low - column : high - column],
                    scratch[part],
                    slice(low - first, high - first),
                    part == 0,
                )
    size = outs[0].shape[0]
    for part in range(2):
        outs[2 * part][...] = scratch[part][:size, :]
        outs[2 * part + 1][...] = scratch[part][size:, :]


def product_out(width, columns, cut, local):
    if local:
        cuts = (cut, columns - cut)
        out = [((width // 2, c), BF) for c in cuts for _ in range(2)]
        return out, [pltpu.VMEM((width, c), BF) for c in cuts]
    return [((width, columns), BF)], []


def sum_products(turned, right, column, wide=256):
    products = []
    for c in range(0, right.shape[1], wide):
        high = min(c + wide, right.shape[1])
        products.append((column + c, dot(turned[...], right[:, c:high])))
    return products


def lower_grad_kernel(outs, place, lengths, cotangent, active, *refs):
    out_refs, (turned, *scratch) = refs[:outs], refs[outs:]
    for micro in range(2):
        for start in range(micro * 2 * LEN, (micro + 1) * 2 * LEN, LEN):
            low = masked_rows(cotangent, start, LEN, lengths[micro])
            turned[:, start : start + LEN] = low.T
    write_products(place, sum_products(turned, active, 0), out_refs, scratch)


def grads_kernel(count, outs, place, *refs):
    pairs, out_refs = refs[: 2 * count], refs[2 * count : 2 * count + outs]
    turned, *scratch = refs[2 * count + outs :]
    products, column = [], 0
    for left, right in zip(pairs[::2], pairs[1::2]):
        for start in range(0, left.shape[0], LEN):
            turned[:, start : start + LEN] = left[start : start + LEN, :].T
        products += sum_products(turned, right, column)
        column += right.shape[1]
    write_products(place, products, out_refs, scratch)


def grad_parts(place, pairs, cut, local, name):
    width, columns = pairs[0][0].shape[1], sum(right.shape[1] for _, right in pairs)
    out, scratch = product_out(width, columns, cut, local)
    return call(
        partial(grads_kernel, len(pairs), len(out)),
        out,
        (place, *(a for pair in pairs for a in pair)),
        smem=(0,),
        scratch=[pltpu.VMEM((width, 4 * LEN), BF)] + scratch,
        name=name,
    )


def half_rows(micro):
    return pl.ds(micro * 2 * LEN, 2 * LEN)


def write_gains(weight, gains):
    columns = weight[:, weight.shape[1] - LANES :].astype(F32)
    gains[...] = columns.T[: gains.shape[0], :]


def first_step(assembles, *refs):
    if assembles:
        place, near_a, far_a, near_b, far_b, inputs, cosine, sine, *outs = refs
        gains, first_norm, mixed, weight = outs
        assemble_kernel(place, near_a, far_a, near_b, far_b, weight)
    else:
        weight, inputs, cosine, sine, gains, first_norm, mixed = refs
    write_gains(weight, gains)
    qkv_kernel(inputs, gains, weight, cosine, sine, first_norm, mixed)


def attend_step(lengths, mixed, weight, heads, logsums, part):
    for m in range(2):
        at = half_rows(m)
        attend_kernel(m, lengths, mixed, weight, heads.at[at], logsums.at[at], part.at[at])


def upper_step(assembles, *refs):
    count = 4 if assembles else 1
    place = None
    if assembles:
        place, near_a, far_a, near_b, far_b, *refs = refs
        lengths, inputs, own, other, gains, cotangent, *outs = refs
        outs, parts, (weight, *scratch) = outs[:4], outs[4:8], outs[8:]
        assemble_kernel(place, near_a, far_a, near_b, far_b, weight)
    else:
        weight, lengths, inputs, own, other, gains, cotangent, *outs = refs
        outs, parts, scratch = outs[:4], outs[4:5], outs[5:]
    for m in range(2):
        at = half_rows(m)
        upper_kernel(
            m, inputs, own.at[at], other.at[at], gains, weight, *(out.at[at] for out in outs)
        )
    lower_grad_kernel(count, place, lengths, cotangent, outs[2], *parts, *scratch)


def hidden_step(assembles, *refs):
    if assembles:
        place, *refs = refs
        blocks_a, blocks_b, refs = refs[:NZ], refs[NZ : 2 * NZ], refs[2 * NZ :]
        lengths, cotangent, slope, upper, second_norm, part, *parts = refs
        *parts, lower, upper_grad, turned, scratch_a, scratch_b = parts
        assemble_late_kernel(place, blocks_a, blocks_b, lower)
    else:
        lower, lengths, cotangent, slope, upper, second_norm, part, *parts = refs
        *parts, upper_grad, turned = parts
    for m in range(2):
        at = half_rows(m)
        hidden_back_kernel(
            m, lengths, cotangent, slope.at[at], lower, upper, upper_grad.at[at], part.at[at]
        )
    if assembles:
        scratch = [turned, scratch_a, scratch_b]
        grads_kernel(1, len(parts), place, second_norm, upper_grad, *parts, *scratch)
    else:
        grads_kernel(1, len(parts), None, second_norm, upper_grad, *parts, turned)


def middle_step(
    lengths, cotangent, own, other, middle, gains, weight, middle_grad, low, head_grad, gain
):
    gain[...] = jnp.zeros_like(gain)
    for m in range(2):
        at = half_rows(m)
        middle_back_kernel(
            m,
            lengths,
            cotangent,
            own.at[at],
            other.at[at],
            middle.at[at],
            gains,
            weight,
            middle_grad.at[at],
            low.at[at],
            head_grad.at[at],
            gain,
        )


def last_back_step(micro, outs, place, lengths, *refs):
    mixed, logsums, head_grad, cosine, sine, low, heads, first_norm, early, *refs = refs
    late, *refs = refs
    out_refs, (key_sum, value_sum, *scratch) = refs[:outs], refs[outs:]
    attend_back_kernel(
        micro, lengths, mixed, logsums, head_grad, cosine, sine, late, key_sum, value_sum
    )
    turned, *scratch = scratch
    rows = 2 * LEN

    def turn(left):
        for start in range(0, left.shape[0], LEN):
            turned[:, start : start + LEN] = left[start : start + LEN, :].T

    turn(low)
    products = sum_products(turned, heads, 0)
    turn(first_norm)
    for c in range(0, late.shape[1], LEN):
        high = min(c + LEN, late.shape[1])
        total = dot(turned[:, :rows], early[:, c:high]) + dot(turned[:, rows:], late[:, c:high])
        products.append((heads.shape[1] + c, total))
    write_products(place, products, out_refs, scratch)


def tail_kernel(active, lower, early, late, weight, sums):
    rows, feats = active.shape[0], early.shape[1] // 3
    step = 256
    for start in range(0, rows, step):
        at = pl.ds(start, step)
        sums[at, :] = dot_nt(active[at, :], lower[...]).astype(BF)
        mixed_grad = (early if start < rows // 2 else late)[pl.ds(start % (rows // 2), step), :]
        back = dot_nt(mixed_grad, weight[:, feats : 4 * feats])
        sums[pl.ds(rows + start, step), :] = back.astype(BF)


def last_kernel(own, other, middle, middle_grad, inputs, gains, results, input_grad, gain):
    rows = inputs.shape[0]
    step = 128
    gain[...] = jnp.zeros_like(gain)
    for start in range(0, rows, step):
        at, behind = pl.ds(start, step), pl.ds(rows + start, step)
        ffn = own[at, :].astype(F32) + other[at, :].astype(F32)
        results[at, :] = (middle[at, :] + ffn).astype(BF)
        back = own[behind, :].astype(F32) + other[behind, :].astype(F32)
        normed, inverse = norm_parts(inputs[at, :].astype(F32))
        gain[0:1, :] += jnp.sum(back * normed, axis=0, keepdims=True)
        input_grad[at, :] = middle_grad[at, :] + norm_back(normed, inverse, back, gains[0:1, :])


def chip_pairs(move):
    pairs = []
    for chip in range(CHIPS):
        to_z, to_y, to_x = move(chip // 4, chip // 2 % 2, chip % 2)
        pairs.append((chip, to_z * 4 + to_y * 2 + to_x))
    return pairs


SWAP_X = chip_pairs(lambda z, y, x: (z, y, 1 - x))
SWAP_Y = chip_pairs(lambda z, y, x: (z, 1 - y, x))
SHIFT_Z = {k: chip_pairs(lambda z, y, x, k=k: ((z + k) % NZ, y, x)) for k in (1, 2, 3)}


def exchange(value, pairs, name):
    with jax.named_scope(name):
        return lax.ppermute(value, "dp", pairs)


tie = lax.optimization_barrier


def start_gather(name, shard):
    if lax.axis_size("dp") != CHIPS:
        return [lax.all_gather(shard, "dp", axis=0, tiled=True)]
    return [shard] + [exchange(shard, SHIFT_Z[k], f"{name}_z{k}") for k in (1, 2, 3)]


def spread_near(name, arrived, cut):
    if len(arrived) == 1:
        return arrived
    rows, columns = arrived[0].shape
    out = [((NZ * rows, cut), BF), ((NZ * rows, columns - cut), BF)]
    part_a, part_b = call(stack_kernel, out, arrived, name="stack")
    return [
        part_a,
        exchange(part_a, SWAP_X, f"{name}_near_a"),
        part_b,
        exchange(part_b, SWAP_Y, f"{name}_near_b"),
    ]


def spread_far(name, near):
    if len(near) == 1:
        return near
    rows = 2 * near[0].shape[0]
    out = [((rows, near[0].shape[1]), BF), ((rows, near[2].shape[1]), BF)]
    near_a, near_b = call(pair_kernel, out, near, name="pair")
    far_a = exchange(near_a, SWAP_Y, f"{name}_far_a")
    return [near_a, far_a, near_b, exchange(near_b, SWAP_X, f"{name}_far_b")]


def step_with_weight(
    step, place, pieces, args, out, smem=(), scratch=(), lower_columns=0, name=None
):
    if len(pieces) == 1:
        smem = [i + 1 for i in smem]
        held = dict(smem=smem, scratch=scratch, name=name)
        outs = call(partial(step, False), out, (pieces[0], *args), **held)
        return [*outs, pieces[0]]
    smem = [0] + [i + 1 + len(pieces) for i in smem]
    columns = lower_columns or pieces[0].shape[1] + pieces[2].shape[1]
    whole = ((sum(p.size for p in pieces) // columns, columns), BF)
    held = dict(smem=smem, scratch=scratch, name=name)
    return call(partial(step, True), [*out, whole], (place, *pieces, *args), **held)


def spread_early(name, shard):
    if lax.axis_size("dp") != CHIPS:
        return [lax.all_gather(shard, "dp", axis=0, tiled=True)]
    rows, columns = shard.shape
    cut = columns // 2
    part_a, part_b = shard[:, :cut], shard[:, cut:]
    near_a = exchange(part_a, SWAP_X, f"{name}_near_a")
    near_b = exchange(part_b, SWAP_Y, f"{name}_near_b")
    out = [((2 * rows, cut), BF)] * 2
    near_a, near_b = call(pair_kernel, out, (part_a, near_a, part_b, near_b), name="pair")
    far_a = exchange(near_a, SWAP_Y, f"{name}_far_a")
    return [near_a, far_a, near_b, exchange(near_b, SWAP_X, f"{name}_far_b")]


def finish_late(name, near, far):
    out = [((2 * near.shape[0], near.shape[1]), BF)]
    (block,) = call(join_kernel, out, (near, far), name="join")
    return [block] + [exchange(block, SHIFT_Z[k], f"{name}_z{k}") for k in (1, 2, 3)]


def scatter_first(name, parts):
    if len(parts) == 1:
        return parts
    kept_a, sent_a, kept_b, sent_b = parts
    return [
        kept_a,
        exchange(sent_a, SWAP_X, f"{name}_first_a"),
        kept_b,
        exchange(sent_b, SWAP_Y, f"{name}_first_b"),
    ]


def scatter_second(name, halves):
    if len(halves) == 1:
        return halves
    rows = halves[0].shape[0] // 2
    out = [((rows, h.shape[1]), d) for h in (halves[0], halves[2]) for d in (F32, BF)]
    own_a, send_a, own_b, send_b = call(half_kernel, out, halves, name="half")
    return [
        own_a,
        exchange(send_a, SWAP_Y, f"{name}_second_a"),
        own_b,
        exchange(send_b, SWAP_X, f"{name}_second_b"),
    ]


def scatter_last(name, columns):
    if len(columns) == 1:
        return [lax.psum_scatter(columns[0], "dp", scatter_dimension=0, tiled=True)]
    rows, count = columns[0].shape[0] // NZ, columns[0].shape[1] + columns[2].shape[1]
    out = [((rows, count), F32)] + [((rows, count), BF)] * 3
    mine, *sends = call(column_kernel, out, columns, name="column")
    return [mine] + [exchange(s, SHIFT_Z[k], f"{name}_z{k}") for k, s in enumerate(sends, 1)]


def added(parts):
    return sum(p.astype(F32) for p in parts)


def swapped(value):
    return lax.ppermute(value, "mp", [(0, 1), (1, 0)])


def rotation(row_count, head_width):
    halfway = head_width // 2
    freqs = 10000.0 ** (-2.0 * jnp.arange(halfway).astype(jnp.float32) / head_width)
    places = (jnp.arange(row_count) % LEN).astype(jnp.float32)
    angles = places[:, None] * freqs[None, :]
    return (jnp.cos(angles), jnp.sin(angles))


def adamw_update(weight, first, second, grad, rate, decay):
    first_new = BETA_ONE * first + (1.0 - BETA_ONE) * grad
    second_new = BETA_TWO * second + (1.0 - BETA_TWO) * grad * grad
    corrected = (
        first_new
        / (1.0 - BETA_ONE**STEP)
        / (jnp.sqrt(second_new / (1.0 - BETA_TWO**STEP)) + ADAM_EPS)
    )
    return (weight - rate * (corrected + decay * weight), first_new, second_new)


def shards(
    inputs,
    cotangent,
    lengths,
    proj_weight,
    output_weight,
    upper_weight,
    lower_weight,
    norm_gains,
    proj_first,
    output_first,
    upper_first,
    lower_first,
    gains_first,
    proj_second,
    output_second,
    upper_second,
    lower_second,
    gains_second,
):
    micro_count, _, row_count, width = inputs.shape
    feats = proj_weight.shape[2]
    hidden = upper_weight.shape[1]
    shard_rows = proj_weight.shape[0]
    local = lax.axis_size("dp") == CHIPS
    chip = lax.axis_index("dp").astype(jnp.int32)
    place = jnp.stack([chip // 4, chip // 2 % 2, chip % 2])
    micros = range(micro_count)
    lengths = lengths.reshape(-1)
    flat_in = inputs.reshape(-1, width)
    flat_ct = cotangent.reshape(-1, width)

    cosine, sine = rotation(LEN, HD)
    cosine = jnp.tile(cosine, (1, 4))
    sine = jnp.tile(jnp.concatenate([-sine, sine], axis=1), (1, 2))

    gain_columns = jnp.pad(norm_gains.T.astype(BF), ((0, 0), (0, LANES - 2)))
    shard_one = jnp.concatenate(
        [
            output_weight.astype(BF).T,
            proj_weight.astype(BF).reshape(shard_rows, 3 * feats),
            gain_columns,
        ],
        axis=1,
    )
    upper_low, lower_low = upper_weight.astype(BF), lower_weight.astype(BF).T
    total_rows = micro_count * row_count
    wide, features = (total_rows, width), (total_rows, feats)
    arrived = start_gather("one", shard_one)
    early_lower = spread_early("lower", lower_low)
    arrived, upper_low, early_lower, cosine, sine = tie(
        (arrived, upper_low, early_lower, cosine, sine)
    )
    near = spread_near("one", arrived, 2 * feats)
    arrived_upper = start_gather("upper", upper_low)
    near, arrived_upper, early_lower = tie((near, arrived_upper, early_lower))
    pieces = spread_far("one", near)
    late_a = finish_late("lower_a", *early_lower[:2]) if local else []
    pieces, arrived_upper = tie((pieces, arrived_upper))
    near_upper = spread_near("upper", arrived_upper, hidden // 2)
    gains_c, first_norm, mixed, one = step_with_weight(
        first_step,
        place,
        pieces,
        (flat_in, cosine, sine),
        [((8, width), F32), (wide, BF), ((total_rows, 3 * feats), BF)],
        name="qkv",
    )
    mixed, near_upper, late_a, early_lower = tie((mixed, near_upper, late_a, early_lower))
    late_b = finish_late("lower_b", *early_lower[2:]) if local else early_lower
    far_upper = spread_far("upper", near_upper)
    heads, logsums, attn = call(
        attend_step,
        [(features, BF), ((total_rows, LANES), F32), (wide, BF)],
        (lengths, mixed, one),
        smem=(0,),
        name="attend",
    )
    far_upper, attn = tie((far_upper, attn))
    attn_other = swapped(attn)
    hidden_rows = (total_rows, hidden)
    part_out, part_scratch = product_out(width, hidden, hidden // 2, local)
    turned = pltpu.VMEM((width, total_rows), BF)
    middle, second_norm, active, slope, *lower_parts, upper_c = step_with_weight(
        upper_step,
        place,
        far_upper,
        (lengths, flat_in, attn, attn_other, gains_c, flat_ct),
        [(wide, F32), (wide, BF), (hidden_rows, BF), (hidden_rows, BF), *part_out],
        smem=(0,),
        scratch=[turned, *part_scratch],
        name="upper",
    )
    lower_parts, late_b = tie((lower_parts, late_b))
    lower_half = scatter_first("lower_sum", lower_parts)
    seconds, *upper_parts, lower_t = step_with_weight(
        hidden_step,
        place,
        [*late_a, *late_b],
        (lengths, flat_ct, slope, upper_c, second_norm),
        [(wide, BF), *part_out],
        smem=(0,),
        lower_columns=hidden,
        scratch=[pltpu.VMEM(hidden_rows, BF), turned, *part_scratch],
        name="hidden_back",
    )
    upper_parts, lower_half, seconds = tie((upper_parts, lower_half, seconds))
    seconds_other = swapped(seconds)
    lower_column = scatter_second("lower_sum", lower_half)
    seconds_other, upper_parts = tie((seconds_other, upper_parts))
    upper_half = scatter_first("upper_sum", upper_parts)
    middle_grad, low, head_grad, gain_two = call(
        middle_step,
        [(wide, F32), (wide, BF), (features, BF), ((8, width), F32)],
        (lengths, flat_ct, seconds, seconds_other, middle, gains_c, one),
        smem=(0,),
        name="middle_back",
    )
    grad_shape = (row_count, 3 * feats)
    sums_of = [pltpu.VMEM((row_count, LANES), F32)] * 2
    (early,) = call(
        partial(attend_back_kernel, 0),
        [(grad_shape, BF)],
        (lengths, mixed, logsums, head_grad, cosine, sine),
        smem=(0,),
        scratch=sums_of,
        name="attend_back",
    )
    early, head_grad, lower_column = tie((early, head_grad, lower_column))
    lower_sum = scatter_last("lower_sum", lower_column)
    part_out, part_scratch = product_out(width, 4 * feats, 2 * feats, local)
    late, *one_parts = call(
        partial(last_back_step, 1, len(part_out)),
        [(grad_shape, BF), *part_out],
        (place, lengths, mixed, logsums, head_grad, cosine, sine, low, heads, first_norm, early),
        smem=(0, 1),
        scratch=[*sums_of, turned, *part_scratch],
        name="last_back",
    )
    early, late, active, one_parts, upper_half, lower_sum = tie(
        (early, late, active, one_parts, upper_half, lower_sum)
    )
    one_half = scatter_first("one_sum", one_parts)
    upper_column = scatter_second("upper_sum", upper_half)
    (sums,) = call(
        tail_kernel,
        [((2 * total_rows, width), BF)],
        (active, lower_t, early, late, one),
        name="tail",
    )
    one_half, upper_column, sums = tie((one_half, upper_column, sums))
    sums_other = swapped(sums)
    one_column = scatter_second("one_sum", one_half)
    upper_sum = scatter_last("upper_sum", upper_column)
    results, input_grad, gain_one = call(
        last_kernel,
        [(wide, BF), (wide, F32), ((8, width), F32)],
        (sums, sums_other, middle, middle_grad, flat_in, gains_c),
        name="last",
    )
    gain_both = jnp.stack([gain_one[0], gain_two[0]])
    one_column, gain_both = tie((one_column, gain_both))
    one_sum = scatter_last("one_sum", one_column)
    lower_grad = added(lower_sum).T
    upper_wgrad = added(upper_sum)
    one_grad = added(one_sum)
    gain_parts = gain_both.reshape(2, -1, shard_rows)
    gain_parts = lax.all_to_all(gain_parts.transpose(1, 0, 2), "dp", 0, 0, tiled=True)
    gains_grad = jnp.sum(gain_parts, axis=0)
    proj_wgrad = one_grad[:, feats:].reshape(proj_weight.shape)
    output_grad = one_grad[:, :feats].T

    updates = [
        adamw_update(proj_weight, proj_first, proj_second, proj_wgrad, RATE_MATRIX, DECAY),
        adamw_update(output_weight, output_first, output_second, output_grad, RATE_OUTPUT, DECAY),
        adamw_update(upper_weight, upper_first, upper_second, upper_wgrad, RATE_MATRIX, DECAY),
        adamw_update(lower_weight, lower_first, lower_second, lower_grad, RATE_MATRIX, DECAY),
        adamw_update(norm_gains, gains_first, gains_second, gains_grad, RATE_GAIN, 0.0),
    ]
    return (
        results.reshape(inputs.shape),
        input_grad.reshape(inputs.shape),
        *[u[0] for u in updates],
        *[u[1] for u in updates],
        *[u[2] for u in updates],
        *[u[0].astype(BF) for u in updates],
    )


def solution(mesh):
    rows = P(None, "dp", None, None)
    weights = (P("dp", None, "mp"), P("mp", "dp"), P("dp", "mp"), P("mp", "dp"), P(None, "dp"))
    in_specs = (rows, rows, P(None, "dp"), *weights * 3)
    out_specs = (rows, rows, *weights * 4)
    return jax.shard_map(shards, mesh=mesh, in_specs=in_specs, out_specs=out_specs, check_vma=False)
```

```python
import math
from functools import partial

import jax
import jax.numpy as jnp
import numpy as np
from jax import lax
from jax.experimental import pallas as pl
from jax.experimental.pallas import tpu as pltpu
from jax.sharding import PartitionSpec as P

HD = 64
BLOCK = 16
LEN = 256
STEP = 10

EPSILON = 1e-05
BETA_ONE = 0.9
BETA_TWO = 0.95
ADAM_EPS = 1e-08
DECAY = 0.1
RATE_MATRIX = 0.02
RATE_OUTPUT = 0.1
RATE_GAIN = 0.8

LANES = 128
SPARE = 6 * 1024 * 1024
PAIR = 2 * HD
BF = jnp.bfloat16
F32 = jnp.float32
MASKED = -1e30
SCALE = HD**-0.5

NZ, NY, NX = 4, 2, 2
CHIPS = NZ * NY * NX


def call(kernel, out_shape, args, smem=(), scratch=(), flops=0, name=None):
    spaces = [
        pl.BlockSpec(memory_space=pltpu.SMEM if i in smem else pltpu.VMEM) for i in range(len(args))
    ]
    shapes = [jax.ShapeDtypeStruct(s, d) for s, d in out_shape]
    moved = sum(a.size * a.dtype.itemsize for a in [*args, *shapes])
    held = moved // 2 + sum(math.prod(r.shape) * jnp.dtype(r.dtype).itemsize for r in scratch)
    return pl.pallas_call(
        kernel,
        out_shape=shapes,
        in_specs=spaces,
        out_specs=[pl.BlockSpec(memory_space=pltpu.VMEM)] * len(shapes),
        scratch_shapes=list(scratch),
        compiler_params=pltpu.CompilerParams(vmem_limit_bytes=held + SPARE),
        cost_estimate=pl.CostEstimate(flops=int(flops), bytes_accessed=moved, transcendentals=0),
        name=name,
    )(*args)


def dot(a, b):
    return jnp.dot(a, b, preferred_element_type=F32)


def dot_nt(a, b):
    return lax.dot_general(a, b, (((1,), (1,)), ((), ())), preferred_element_type=F32)


def dot_tn(a, b):
    return lax.dot_general(a, b, (((0,), (0,)), ((), ())), preferred_element_type=F32)


def norm_parts(values):
    centre = jnp.mean(values, axis=-1, keepdims=True)
    shifted = values - centre
    spread = jnp.mean(shifted * shifted, axis=-1, keepdims=True)
    inverse = lax.rsqrt(spread + EPSILON)
    return shifted * inverse, inverse


def norm_back(normed, inverse, grads, gain):
    scaled = grads * gain
    mean_one = jnp.mean(scaled, axis=-1, keepdims=True)
    mean_two = jnp.mean(scaled * normed, axis=-1, keepdims=True)
    return (scaled - mean_one - normed * mean_two) * inverse


def stack_kernel(*refs):
    pieces, (part_a, part_b) = refs[:NZ], refs[NZ:]
    rows, cut = pieces[0].shape[0], part_a.shape[1]
    for k, piece in enumerate(pieces):
        at = slice(k * rows, (k + 1) * rows)
        part_a[at, :] = piece[:, :cut]
        part_b[at, :] = piece[:, cut:]


def pair_kernel(part_a, got_a, part_b, got_b, near_a, near_b):
    rows = part_a.shape[0]
    for part, got, near in ((part_a, got_a, near_a), (part_b, got_b, near_b)):
        near[:rows, :] = part[...]
        near[rows:, :] = got[...]


def assemble_kernel(place, near_a, far_a, near_b, far_b, whole):
    z, y, x = place[0], place[1], place[2]
    rows, cut = near_a.shape[0] // (2 * NZ), near_a.shape[1]
    for near in range(2):
        for k in range(NZ):
            at = slice((near * NZ + k) * rows, (near * NZ + k + 1) * rows)
            for far in range(2):
                z_of = lax.rem(z + NZ - k, NZ) * 4
                row_a = z_of + (y ^ far) * 2 + (x ^ near)
                row_b = z_of + (y ^ near) * 2 + (x ^ far)
                to_a = pl.ds(pl.multiple_of(row_a * rows, rows), rows)
                to_b = pl.ds(pl.multiple_of(row_b * rows, rows), rows)
                whole[to_a, :cut] = (far_a if far else near_a)[at, :]
                whole[to_b, cut:] = (far_b if far else near_b)[at, :]


def join_kernel(part_a, got_a, part_b, got_b, block):
    rows, cut = part_a.shape
    for columns, part, got in ((slice(0, cut), part_a, got_a), (slice(cut, None), part_b, got_b)):
        block[:rows, columns] = part[...]
        block[rows:, columns] = got[...]


def assemble_late_kernel(place, part_a, far_a, part_b, far_b, whole):
    z, y, x = place[0], place[1], place[2]
    rows, cut = part_a.shape[0] // (2 * NZ), part_a.shape[1]
    for k in range(NZ):
        z_of = lax.rem(z + NZ - k, NZ) * 4
        for near in range(2):
            at = slice((k * 2 + near) * rows, (k * 2 + near + 1) * rows)
            for far in range(2):
                row_a = z_of + (y ^ far) * 2 + (x ^ near)
                row_b = z_of + (y ^ near) * 2 + (x ^ far)
                to_a = pl.ds(pl.multiple_of(row_a * rows, rows), rows)
                to_b = pl.ds(pl.multiple_of(row_b * rows, rows), rows)
                whole[to_a, :cut] = (far_a if far else part_a)[at, :]
                whole[to_b, cut:] = (far_b if far else part_b)[at, :]


def half_kernel(kept_a, got_a, kept_b, got_b, own_a, send_a, own_b, send_b):
    rows = own_a.shape[0]
    for kept, got, own, send in ((kept_a, got_a, own_a, send_a), (kept_b, got_b, own_b, send_b)):
        own[...] = kept[:rows, :].astype(F32) + got[:rows, :].astype(F32)
        send[...] = (kept[rows:, :].astype(F32) + got[rows:, :].astype(F32)).astype(BF)


def column_kernel(own_a, got_a, own_b, got_b, mine, *sends):
    rows, cut = mine.shape[0], own_a.shape[1]
    for columns, own, got in ((slice(0, cut), own_a, got_a), (slice(cut, None), own_b, got_b)):
        mine[:, columns] = own[:rows, :] + got[:rows, :].astype(F32)
        for k, send in enumerate(sends, 1):
            at = slice(k * rows, (k + 1) * rows)
            send[:, columns] = (own[at, :] + got[at, :].astype(F32)).astype(BF)


def swap_halves(u):
    lane = lax.broadcasted_iota(jnp.int32, u.shape, 1)
    ahead = pltpu.roll(u, LANES - HD // 2, 1)
    behind = pltpu.roll(u, HD // 2, 1)
    return jnp.where(lane % HD < HD // 2, ahead, behind)


def qkv_kernel(inputs, gains, weight, cosine, sine, first_norm, mixed):
    feats = mixed.shape[1] // 3
    step = 256
    for start in range(0, inputs.shape[0], step):
        rows = pl.ds(start, step)
        normed, _ = norm_parts(inputs[rows, :].astype(F32))
        low = (normed * gains[0:1, :]).astype(BF)
        first_norm[rows, :] = low
        place = pl.ds(start % LEN, step)
        cos_rows, sin_rows = cosine[place, :], sine[place, :]
        product = dot(low, weight[:, feats : 4 * feats])
        for j in range(2 * feats // LANES):
            at = slice(j * LANES, (j + 1) * LANES)
            u = product[:, at]
            turned = (u * cos_rows + swap_halves(u) * sin_rows).astype(BF)
            if j < feats // LANES:
                turned = turned * jnp.asarray(SCALE, BF)
            mixed[rows, at] = turned
        mixed[rows, 2 * feats :] = product[:, 2 * feats :].astype(BF)


def visible_bias(length):
    row = lax.broadcasted_iota(jnp.int32, (LEN, LEN), 0) // BLOCK
    place = lax.broadcasted_iota(jnp.int32, (LEN, LEN), 1)
    col = place // BLOCK
    real = place < length
    bias = lambda seen: jnp.where(seen & real, 0.0, MASKED).astype(F32)
    noisy = jnp.concatenate([bias(col == row), bias(col < row)], axis=1)
    return noisy, bias(col <= row)


def own_lanes(value, head):
    lane = lax.broadcasted_iota(jnp.int32, value.shape, 1)
    mine = (lane < HD) if head == 0 else (lane >= HD)
    return jnp.where(mine, value, jnp.zeros_like(value))


def stacked_heads(value):
    first, second = own_lanes(value, 0), own_lanes(value, 1)
    return jnp.concatenate([first[:LEN], second[:LEN], first[LEN:], second[LEN:]])


def attend_kernel(micro, lengths, mixed, weight, heads, logsums, part):
    feats = heads.shape[1]
    bias_noisy, bias_clean = visible_bias(lengths[micro])
    lane = lax.broadcasted_iota(jnp.int32, (LEN, LANES), 1)
    base = micro * 2 * LEN
    sums = [jnp.zeros((LEN, LANES), F32), jnp.zeros((LEN, LANES), F32)]
    for pair in range(feats // PAIR):
        query, key, value = (
            mixed[pl.ds(base, 2 * LEN), c * feats + pair * PAIR : c * feats + (pair + 1) * PAIR]
            for c in range(3)
        )
        stacked = stacked_heads(query)
        on_clean = dot_nt(stacked, key[LEN:])
        on_noisy = dot_nt(stacked[: 2 * LEN], key[:LEN])
        clean_weights, noisy_weights = [], []
        for block in range(4):
            clean, head = divmod(block, 2)
            at = slice(block * LEN, (block + 1) * LEN)
            if clean:
                scores = on_clean[at] + bias_clean
                maximum = jnp.max(scores, axis=-1, keepdims=True)
                raised = jnp.exp(scores - maximum)
                summed = jnp.sum(raised, axis=-1, keepdims=True)
                clean_weights.append((raised * (1.0 / summed)).astype(BF))
            else:
                far = on_clean[at] + bias_noisy[:, LEN:]
                near = on_noisy[at] + bias_noisy[:, :LEN]
                maximum = jnp.max(jnp.maximum(far, near), axis=-1, keepdims=True)
                far, near = jnp.exp(far - maximum), jnp.exp(near - maximum)
                summed = jnp.sum(far + near, axis=-1, keepdims=True)
                inverse = 1.0 / summed
                clean_weights.append((far * inverse).astype(BF))
                noisy_weights.append((near * inverse).astype(BF))
            sums[clean] = jnp.where(
                lane == pair * 2 + head, maximum + jnp.log(summed), sums[clean]
            )
        out = dot(jnp.concatenate(clean_weights), value[LEN:])
        near = dot(jnp.concatenate(noisy_weights), value[:LEN])
        noisy = [out[h * LEN : (h + 1) * LEN] + near[h * LEN : (h + 1) * LEN] for h in range(2)]
        clean = [out[(2 + h) * LEN : (3 + h) * LEN] for h in range(2)]
        cols = slice(pair * PAIR, (pair + 1) * PAIR)
        heads[:LEN, cols] = jnp.where(lane < HD, *noisy).astype(BF)
        heads[LEN:, cols] = jnp.where(lane < HD, *clean).astype(BF)
    for clean in range(2):
        rows = slice(clean * LEN, (clean + 1) * LEN)
        logsums[rows, :] = sums[clean]
        part[rows, :] = dot_nt(heads[rows, :], weight[:, :feats]).astype(BF)


ERF_NUM = (
    -2.72614225801306e-10,
    2.77068142495902e-08,
    -2.10102402082508e-06,
    -5.69250639462346e-05,
    -7.34990630326855e-04,
    -2.95459980854025e-03,
    -1.60960333262415e-02,
)
ERF_DEN = (
    -1.45660718464996e-05,
    -2.13374055278905e-04,
    -1.68282697438203e-03,
    -7.37332916720468e-03,
    -1.42647390514189e-02,
)


def gelu_parts(v):
    u = jnp.clip(v * (0.5**0.5), -4.0, 4.0)
    square = u * u
    num = jnp.full_like(u, ERF_NUM[0])
    for c in ERF_NUM[1:]:
        num = num * square + c
    den = jnp.full_like(u, ERF_DEN[0])
    for c in ERF_DEN[1:]:
        den = den * square + c
    half = 0.5 + 0.5 * (u * num / den)
    bell = jnp.exp(v * v * -0.5) * 0.3989422804014327
    return v * half, half + v * bell


def upper_kernel(micro, inputs, own, other, gains, weight, middle, second_norm, active, slope):
    base = micro * 2 * LEN
    step, wide = 256, 512
    for start in range(0, 2 * LEN, step):
        rows = pl.ds(start, step)
        value = inputs[pl.ds(base + start, step), :].astype(F32) + (
            own[rows, :].astype(F32) + other[rows, :].astype(F32)
        )
        middle[rows, :] = value
        normed, _ = norm_parts(value)
        low = (normed * gains[1:2, :]).astype(BF)
        second_norm[rows, :] = low
        for c in range(0, weight.shape[1], wide):
            out, grad = gelu_parts(dot(low, weight[:, c : c + wide]))
            active[rows, c : c + wide] = out.astype(BF)
            slope[rows, c : c + wide] = grad.astype(BF)


def masked_rows(cotangent, start, step, length):
    place = lax.broadcasted_iota(jnp.int32, (step, 1), 0) + start % LEN
    rows = cotangent[pl.ds(start, step), :]
    return jnp.where(place < length, rows, jnp.zeros_like(rows))


def hidden_back_kernel(micro, lengths, cotangent, slope, lower, upper, upper_grad, part):
    base = micro * 2 * LEN
    step, wide = 256, 512
    for start in range(0, 2 * LEN, step):
        rows = pl.ds(start, step)
        low = masked_rows(cotangent, base + start, step, lengths[micro])
        total = jnp.zeros((step, part.shape[1]), F32)
        for c in range(0, lower.shape[1], wide):
            grad = dot(low, lower[:, c : c + wide]) * slope[rows, c : c + wide].astype(F32)
            grad = grad.astype(BF)
            upper_grad[rows, c : c + wide] = grad
            total = total + dot_nt(grad, upper[:, c : c + wide])
        part[rows, :] = total.astype(BF)


def middle_back_kernel(
    micro, lengths, cotangent, own, other, middle, gains, weight, middle_grad, low, head_grad
):
    base = micro * 2 * LEN
    step = 256
    feats = head_grad.shape[1]
    for start in range(0, 2 * LEN, step):
        rows = pl.ds(start, step)
        upstream = masked_rows(cotangent, base + start, step, lengths[micro]).astype(F32)
        back = own[rows, :].astype(F32) + other[rows, :].astype(F32)
        normed, inverse = norm_parts(middle[rows, :])
        grad = upstream + norm_back(normed, inverse, back, gains[1:2, :])
        middle_grad[rows, :] = grad
        low_grad = grad.astype(BF)
        low[rows, :] = low_grad
        head_grad[rows, :] = dot(low_grad, weight[:, :feats]).astype(BF)


def attend_back_kernel(
    micro, lengths, mixed, logsums, head_grad, cosine, sine, mixed_grad, key_sum, value_sum
):
    feats = head_grad.shape[1]
    bias_noisy, bias_clean = visible_bias(lengths[micro])
    base = micro * 2 * LEN
    cos_rows, sin_rows = cosine[...], sine[...]
    rows_of = [slice(block * LEN, (block + 1) * LEN) for block in range(4)]

    def turn_back(u):
        return u * cos_rows - swap_halves(u) * sin_rows

    lane = lax.broadcasted_iota(jnp.int32, (LEN, LANES), 1)
    for pair in range(feats // PAIR):
        cols = [
            slice(c * feats + pair * PAIR, c * feats + (pair + 1) * PAIR) for c in range(3)
        ]
        query, key, value = (mixed[pl.ds(base, 2 * LEN), c] for c in cols)
        stacked = stacked_heads(query)
        stacked_grad = stacked_heads(
            head_grad[pl.ds(base, 2 * LEN), pair * PAIR : (pair + 1) * PAIR]
        )
        score = [
            dot_nt(stacked[: 2 * LEN], key[:LEN]),
            dot_nt(stacked, key[LEN:]),
        ]
        prob_grad = [
            dot_nt(stacked_grad[: 2 * LEN], value[:LEN]),
            dot_nt(stacked_grad, value[LEN:]),
        ]
        probs_low, score_low = [[], []], [[], []]
        for block, at in enumerate(rows_of):
            clean, head = divmod(block, 2)
            index = pair * 2 + head
            logsum = logsums[pl.ds(base + clean * LEN, LEN), index : index + 1]
            parts = (1,) if clean else (0, 1)
            biases = {1: bias_clean} if clean else {0: bias_noisy[:, :LEN], 1: bias_noisy[:, LEN:]}
            probs = {p: jnp.exp(score[p][at] + biases[p] - logsum) for p in parts}
            products = [probs[p] * prob_grad[p][at] for p in parts]
            inner = jnp.sum(sum(products[1:], products[0]), axis=-1, keepdims=True)
            for p in parts:
                probs_low[p].append(probs[p].astype(BF))
                score_low[p].append((probs[p] * (prob_grad[p][at] - inner)).astype(BF))
        probs_low = [jnp.concatenate(blocks) for blocks in probs_low]
        score_low = [jnp.concatenate(blocks) for blocks in score_low]
        near, far = dot(score_low[0], key[:LEN]), dot(score_low[1], key[LEN:])
        noisy = [near[rows_of[h]] + far[rows_of[h]] for h in range(2)]
        clean = [far[rows_of[2 + h]] for h in range(2)]
        for p in range(2):
            rows = slice(p * LEN, (p + 1) * LEN)
            used = slice(0, (2 + 2 * p) * LEN)
            query_grad = jnp.where(lane < HD, *(clean if p else noisy))
            key_grad = dot_tn(score_low[p], stacked[used])
            value_grad = dot_tn(probs_low[p], stacked_grad[used])
            mixed_grad[rows, cols[0]] = turn_back(query_grad * SCALE).astype(BF)
            mixed_grad[rows, cols[1]] = turn_back(key_grad).astype(BF)
            mixed_grad[rows, cols[2]] = value_grad.astype(BF)


def put_blocks(place, product, scratch, column, x_first):
    z, y, x = place[0], place[1], place[2]
    rows = product.shape[0] // CHIPS
    for chip in range(CHIPS):
        to_z = lax.rem(chip // 4 + NZ - z, NZ)
        to_y, to_x = y ^ (chip // 2 % 2), x ^ (chip % 2)
        at = (to_x * 2 + to_y if x_first else to_y * 2 + to_x) * NZ + to_z
        scratch[pl.ds(pl.multiple_of(at * rows, rows), rows), column] = product[
            chip * rows : (chip + 1) * rows
        ].astype(BF)


def write_products(place, products, outs, scratch):
    if len(outs) == 1:
        for column, value in products:
            outs[0][:, column : column + value.shape[1]] = value.astype(BF)
        return
    cut = outs[0].shape[1]
    end = cut + outs[2].shape[1]
    for column, value in products:
        for part, (first, last) in enumerate(((0, cut), (cut, end))):
            low, high = max(column, first), min(column + value.shape[1], last)
            if low < high:
                put_blocks(
                    place,
                    value[:, low - column : high - column],
                    scratch[part],
                    slice(low - first, high - first),
                    part == 0,
                )
    size = outs[0].shape[0]
    for part in range(2):
        outs[2 * part][...] = scratch[part][:size, :]
        outs[2 * part + 1][...] = scratch[part][size:, :]


def product_out(width, columns, cut, local):
    if local:
        cuts = (cut, columns - cut)
        out = [((width // 2, c), BF) for c in cuts for _ in range(2)]
        return out, [pltpu.VMEM((width, c), BF) for c in cuts]
    return [((width, columns), BF)], []


def sum_products(turned, right, column, wide=256):
    products = []
    for c in range(0, right.shape[1], wide):
        high = min(c + wide, right.shape[1])
        products.append((column + c, dot(turned[...], right[:, c:high])))
    return products


def lower_grad_kernel(outs, place, lengths, cotangent, active, *refs):
    out_refs, (turned, *scratch) = refs[:outs], refs[outs:]
    for micro in range(2):
        for start in range(micro * 2 * LEN, (micro + 1) * 2 * LEN, LEN):
            low = masked_rows(cotangent, start, LEN, lengths[micro])
            turned[:, start : start + LEN] = low.T
    write_products(place, sum_products(turned, active, 0), out_refs, scratch)


def grads_kernel(count, outs, place, *refs):
    pairs, out_refs = refs[: 2 * count], refs[2 * count : 2 * count + outs]
    turned, *scratch = refs[2 * count + outs :]
    products, column = [], 0
    for left, right in zip(pairs[::2], pairs[1::2]):
        for start in range(0, left.shape[0], LEN):
            turned[:, start : start + LEN] = left[start : start + LEN, :].T
        products += sum_products(turned, right, column)
        column += right.shape[1]
    write_products(place, products, out_refs, scratch)


def grad_parts(place, pairs, cut, local, name):
    width, columns = pairs[0][0].shape[1], sum(right.shape[1] for _, right in pairs)
    out, scratch = product_out(width, columns, cut, local)
    return call(
        partial(grads_kernel, len(pairs), len(out)),
        out,
        (place, *(a for pair in pairs for a in pair)),
        smem=(0,),
        scratch=[pltpu.VMEM((width, 4 * LEN), BF)] + scratch,
        name=name,
    )


def half_rows(micro):
    return pl.ds(micro * 2 * LEN, 2 * LEN)


def write_gains(weight, gains):
    columns = weight[:, weight.shape[1] - LANES :].astype(F32)
    gains[...] = columns.T[: gains.shape[0], :]


def first_step(assembles, *refs):
    if assembles:
        place, near_a, far_a, near_b, far_b, inputs, cosine, sine, *outs = refs
        gains, first_norm, mixed, weight = outs
        assemble_kernel(place, near_a, far_a, near_b, far_b, weight)
    else:
        weight, inputs, cosine, sine, gains, first_norm, mixed = refs
    write_gains(weight, gains)
    qkv_kernel(inputs, gains, weight, cosine, sine, first_norm, mixed)


def attend_step(lengths, mixed, weight, heads, logsums, part):
    for m in range(2):
        at = half_rows(m)
        attend_kernel(m, lengths, mixed, weight, heads.at[at], logsums.at[at], part.at[at])


def upper_step(assembles, *refs):
    count = 4 if assembles else 1
    place = None
    if assembles:
        place, near_a, far_a, near_b, far_b, *refs = refs
        lengths, inputs, own, other, gains, cotangent, *outs = refs
        outs, parts, (weight, *scratch) = outs[:4], outs[4:8], outs[8:]
        assemble_kernel(place, near_a, far_a, near_b, far_b, weight)
    else:
        weight, lengths, inputs, own, other, gains, cotangent, *outs = refs
        outs, parts, scratch = outs[:4], outs[4:5], outs[5:]
    for m in range(2):
        at = half_rows(m)
        upper_kernel(
            m, inputs, own.at[at], other.at[at], gains, weight, *(out.at[at] for out in outs)
        )
    lower_grad_kernel(count, place, lengths, cotangent, outs[2], *parts, *scratch)


def hidden_step(assembles, *refs):
    if assembles:
        place, part_a, far_a, part_b, far_b, *refs = refs
        lengths, cotangent, slope, upper, second_norm, active, part, ffn, *parts = refs
        *parts, lower, upper_grad, turned, scratch_a, scratch_b = parts
        assemble_late_kernel(place, part_a, far_a, part_b, far_b, lower)
    else:
        lower, lengths, cotangent, slope, upper, second_norm, active, part, ffn, *parts = refs
        *parts, upper_grad, turned = parts
    for m in range(2):
        at = half_rows(m)
        hidden_back_kernel(
            m, lengths, cotangent, slope.at[at], lower, upper, upper_grad.at[at], part.at[at]
        )
    for start in range(0, active.shape[0], LEN):
        at = pl.ds(start, LEN)
        ffn[at, :] = dot_nt(active[at, :], lower[...]).astype(BF)
    if assembles:
        scratch = [turned, scratch_a, scratch_b]
        grads_kernel(1, len(parts), place, second_norm, upper_grad, *parts, *scratch)
    else:
        grads_kernel(1, len(parts), None, second_norm, upper_grad, *parts, turned)


def middle_step(
    lengths, cotangent, own, other, middle, gains, weight, middle_grad, low, head_grad
):
    for m in range(2):
        at = half_rows(m)
        middle_back_kernel(
            m,
            lengths,
            cotangent,
            own.at[at],
            other.at[at],
            middle.at[at],
            gains,
            weight,
            middle_grad.at[at],
            low.at[at],
            head_grad.at[at],
        )


def early_back_step(
    lengths,
    mixed,
    logsums,
    head_grad,
    cosine,
    sine,
    middle,
    ffn,
    ffn_other,
    early,
    results,
    key_sum,
    value_sum,
):
    attend_back_kernel(
        0, lengths, mixed, logsums, head_grad, cosine, sine, early, key_sum, value_sum
    )
    for start in range(0, middle.shape[0], LEN):
        at = pl.ds(start, LEN)
        total = ffn[at, :].astype(F32) + ffn_other[at, :].astype(F32)
        results[at, :] = (middle[at, :] + total).astype(BF)


def last_back_step(micro, outs, place, lengths, *refs):
    mixed, logsums, head_grad, cosine, sine, low, heads, first_norm, early, *refs = refs
    late, *refs = refs
    out_refs, (key_sum, value_sum, *scratch) = refs[:outs], refs[outs:]
    attend_back_kernel(
        micro, lengths, mixed, logsums, head_grad, cosine, sine, late, key_sum, value_sum
    )
    turned, *scratch = scratch
    rows = 2 * LEN

    def turn(left):
        for start in range(0, left.shape[0], LEN):
            turned[:, start : start + LEN] = left[start : start + LEN, :].T

    turn(low)
    products = sum_products(turned, heads, 0)
    turn(first_norm)
    for c in range(0, late.shape[1], LEN):
        high = min(c + LEN, late.shape[1])
        total = dot(turned[:, :rows], early[:, c:high]) + dot(turned[:, rows:], late[:, c:high])
        products.append((heads.shape[1] + c, total))
    write_products(place, products, out_refs, scratch)


def tail_kernel(early, late, weight, part):
    half, feats = early.shape[0], early.shape[1] // 3
    for start in range(0, 2 * half, LEN):
        mixed_grad = (early if start < half else late)[pl.ds(start % half, LEN), :]
        part[pl.ds(start, LEN), :] = dot_nt(mixed_grad, weight[:, feats : 4 * feats]).astype(BF)


def last_kernel(own, other, middle_grad, inputs, gains, input_grad):
    step = 128
    for start in range(0, inputs.shape[0], step):
        at = pl.ds(start, step)
        back = own[at, :].astype(F32) + other[at, :].astype(F32)
        normed, inverse = norm_parts(inputs[at, :].astype(F32))
        input_grad[at, :] = middle_grad[at, :] + norm_back(normed, inverse, back, gains[0:1, :])


def gains_step(own, other, weight, first, second, new, first_new, second_new, low):
    grad = (own[...] + other[...]) / weight[...].astype(BF).astype(F32)
    new[...], first_new[...], second_new[...] = adamw_update(
        weight[...], first[...], second[...], grad, RATE_GAIN, 0.0
    )
    low[...] = new[...].astype(BF)


def chip_pairs(move):
    pairs = []
    for chip in range(CHIPS):
        to_z, to_y, to_x = move(chip // 4, chip // 2 % 2, chip % 2)
        pairs.append((chip, to_z * 4 + to_y * 2 + to_x))
    return pairs


SWAP_X = chip_pairs(lambda z, y, x: (z, y, 1 - x))
SWAP_Y = chip_pairs(lambda z, y, x: (z, 1 - y, x))
SHIFT_Z = {k: chip_pairs(lambda z, y, x, k=k: ((z + k) % NZ, y, x)) for k in (1, 2, 3)}


def exchange(value, pairs, name):
    with jax.named_scope(name):
        return lax.ppermute(value, "dp", pairs)


tie = lax.optimization_barrier


def start_gather(name, shard, shifts=(1, 2, 3)):
    if lax.axis_size("dp") != CHIPS:
        return [lax.all_gather(shard, "dp", axis=0, tiled=True)] if 1 in shifts else [shard]
    return [shard] + [exchange(shard, SHIFT_Z[k], f"{name}_z{k}") for k in shifts]


def spread_near(name, arrived, cut):
    if len(arrived) == 1:
        return arrived
    rows, columns = arrived[0].shape
    out = [((NZ * rows, cut), BF), ((NZ * rows, columns - cut), BF)]
    part_a, part_b = call(stack_kernel, out, arrived, name="stack")
    return [
        part_a,
        exchange(part_a, SWAP_X, f"{name}_near_a"),
        part_b,
        exchange(part_b, SWAP_Y, f"{name}_near_b"),
    ]


def spread_far(name, near):
    if len(near) == 1:
        return near
    rows = 2 * near[0].shape[0]
    out = [((rows, near[0].shape[1]), BF), ((rows, near[2].shape[1]), BF)]
    near_a, near_b = call(pair_kernel, out, near, name="pair")
    far_a = exchange(near_a, SWAP_Y, f"{name}_far_a")
    return [near_a, far_a, near_b, exchange(near_b, SWAP_X, f"{name}_far_b")]


def step_with_weight(step, place, pieces, args, out, smem=(), scratch=(), name=None):
    if len(pieces) == 1:
        smem = [i + 1 for i in smem]
        held = dict(smem=smem, scratch=scratch, name=name)
        outs = call(partial(step, False), out, (pieces[0], *args), **held)
        return [*outs, pieces[0]]
    smem = [0] + [i + 1 + len(pieces) for i in smem]
    whole = ((2 * pieces[0].shape[0], pieces[0].shape[1] + pieces[2].shape[1]), BF)
    held = dict(smem=smem, scratch=scratch, name=name)
    return call(partial(step, True), [*out, whole], (place, *pieces, *args), **held)


def gather_near(name, shard):
    if lax.axis_size("dp") != CHIPS:
        return lax.all_gather(shard, "dp", axis=0, tiled=True)
    rows, columns = shard.shape
    cut = columns // 2
    part_a, part_b = shard[:, :cut], shard[:, cut:]
    got_a = exchange(part_a, SWAP_X, f"{name}_near_a")
    got_b = exchange(part_b, SWAP_Y, f"{name}_near_b")
    out = [((2 * rows, columns), BF)]
    return call(join_kernel, out, (part_a, got_a, part_b, got_b), name="join")[0]


def gather_z(name, block, shifts):
    if lax.axis_size("dp") != CHIPS:
        return []
    return [exchange(block, SHIFT_Z[k], f"{name}_z{k}") for k in shifts]


def gather_far(name, arrived):
    if len(arrived) == 1:
        return arrived
    rows, columns = arrived[0].shape
    cut = columns // 2
    out = [((NZ * rows, cut), BF)] * 2
    part_a, part_b = call(stack_kernel, out, arrived, name="stack")
    far_a = exchange(part_a, SWAP_Y, f"{name}_far_a")
    return [part_a, far_a, part_b, exchange(part_b, SWAP_X, f"{name}_far_b")]


def scatter_first(name, parts):
    if len(parts) == 1:
        return parts
    kept_a, sent_a, kept_b, sent_b = parts
    return [
        kept_a,
        exchange(sent_a, SWAP_X, f"{name}_first_a"),
        kept_b,
        exchange(sent_b, SWAP_Y, f"{name}_first_b"),
    ]


def scatter_half(halves):
    if len(halves) == 1:
        return halves
    rows = halves[0].shape[0] // 2
    out = [((rows, h.shape[1]), d) for h in (halves[0], halves[2]) for d in (F32, BF)]
    return call(half_kernel, out, halves, name="half")


def scatter_second(name, halves):
    if len(halves) == 1:
        return halves
    own_a, send_a, own_b, send_b = halves
    return [
        own_a,
        exchange(send_a, SWAP_Y, f"{name}_second_a"),
        own_b,
        exchange(send_b, SWAP_X, f"{name}_second_b"),
    ]


def scatter_column(columns):
    if len(columns) == 1:
        return columns
    rows, count = columns[0].shape[0] // NZ, columns[0].shape[1] + columns[2].shape[1]
    out = [((rows, count), F32)] + [((rows, count), BF)] * 3
    return call(column_kernel, out, columns, name="column")


def scatter_last(name, columns):
    if len(columns) == 1:
        return [lax.psum_scatter(columns[0], "dp", scatter_dimension=0, tiled=True)]
    mine, *sends = columns
    return [mine] + [exchange(s, SHIFT_Z[k], f"{name}_z{k}") for k, s in enumerate(sends, 1)]


def added(parts):
    return sum(p.astype(F32) for p in parts)


def swapped(value):
    return lax.ppermute(value, "mp", [(0, 1), (1, 0)])


def rotation():
    freqs = np.float32(10000.0) ** (np.float32(-2.0) * np.arange(HD // 2, dtype=np.float32) / np.float32(HD))
    angles = (np.arange(LEN, dtype=np.float32)[:, None] * freqs[None, :]).astype(np.float64)
    cosine, sine = np.cos(angles), np.sin(angles)
    cosine = np.tile(cosine, (1, 4)).astype(np.float32)
    return cosine, np.tile(np.concatenate([-sine, sine], axis=1), (1, 2)).astype(np.float32)


def row_sums(value):
    ones = jnp.ones((1, value.shape[1]), F32)
    contract = (((1,), (1,)), ((), ()))
    return lax.dot_general(
        ones, value, contract, precision=lax.Precision.HIGHEST, preferred_element_type=F32
    )


def adamw_update(weight, first, second, grad, rate, decay):
    first_new = BETA_ONE * first + (1.0 - BETA_ONE) * grad
    second_new = BETA_TWO * second + (1.0 - BETA_TWO) * grad * grad
    corrected = (
        first_new
        / (1.0 - BETA_ONE**STEP)
        / (jnp.sqrt(second_new / (1.0 - BETA_TWO**STEP)) + ADAM_EPS)
    )
    return (weight - rate * (corrected + decay * weight), first_new, second_new)


def shards(
    inputs,
    cotangent,
    lengths,
    proj_weight,
    output_weight,
    upper_weight,
    lower_weight,
    norm_gains,
    proj_first,
    output_first,
    upper_first,
    lower_first,
    gains_first,
    proj_second,
    output_second,
    upper_second,
    lower_second,
    gains_second,
):
    micro_count, _, row_count, width = inputs.shape
    feats = proj_weight.shape[2]
    hidden = upper_weight.shape[1]
    shard_rows = proj_weight.shape[0]
    local = lax.axis_size("dp") == CHIPS
    chip = lax.axis_index("dp").astype(jnp.int32)
    place = jnp.stack([chip // 4, chip // 2 % 2, chip % 2])
    micros = range(micro_count)
    lengths = lengths.reshape(-1)
    flat_in = inputs.reshape(-1, width)
    flat_ct = cotangent.reshape(-1, width)

    cosine, sine = (jnp.asarray(table) for table in rotation())

    gain_columns = jnp.pad(norm_gains.T.astype(BF), ((0, 0), (0, LANES - 2)))
    shard_one = jnp.concatenate(
        [
            output_weight.astype(BF).T,
            proj_weight.astype(BF).reshape(shard_rows, 3 * feats),
            gain_columns,
        ],
        axis=1,
    )
    upper_low, lower_low = upper_weight.astype(BF), lower_weight.astype(BF).T
    total_rows = micro_count * row_count
    wide, features = (total_rows, width), (total_rows, feats)
    arrived = start_gather("one", shard_one)
    near_lower = gather_near("lower", lower_low)
    arrived, upper_low, near_lower = tie((arrived, upper_low, near_lower))
    near = spread_near("one", arrived, 2 * feats)
    arrived_upper = start_gather("upper", upper_low, (1, 3))
    near, arrived_upper, upper_low = tie((near, arrived_upper, upper_low))
    pieces = spread_far("one", near)
    opposite = start_gather("upper", upper_low, (2,))[1:]
    opposite, near_lower = tie((opposite, near_lower)) if local else (opposite, near_lower)
    arrived_upper = [*arrived_upper[:2], *opposite, *arrived_upper[2:]]
    beside_lower = gather_z("lower", near_lower, (1, 3))
    pieces, arrived_upper = tie((pieces, arrived_upper))
    near_upper = spread_near("upper", arrived_upper, hidden // 2)
    gains_c, first_norm, mixed, one = step_with_weight(
        first_step,
        place,
        pieces,
        (flat_in, cosine, sine),
        [((8, width), F32), (wide, BF), ((total_rows, 3 * feats), BF)],
        name="qkv",
    )
    mixed, near_upper, beside_lower, near_lower = tie((mixed, near_upper, beside_lower, near_lower))
    opposite_lower = gather_z("lower", near_lower, (2,))
    far_upper = spread_far("upper", near_upper)
    heads, logsums, attn = call(
        attend_step,
        [(features, BF), ((total_rows, LANES), F32), (wide, BF)],
        (lengths, mixed, one),
        smem=(0,),
        name="attend",
    )
    far_upper, opposite_lower, attn = tie((far_upper, opposite_lower, attn))
    arrived_lower = [near_lower, *beside_lower[:1], *opposite_lower, *beside_lower[1:]]
    attn_other = swapped(attn)
    far_lower = gather_far("lower", arrived_lower)
    hidden_rows = (total_rows, hidden)
    part_out, part_scratch = product_out(width, hidden, hidden // 2, local)
    turned = pltpu.VMEM((width, total_rows), BF)
    middle, second_norm, active, slope, *lower_parts, upper_c = step_with_weight(
        upper_step,
        place,
        far_upper,
        (lengths, flat_in, attn, attn_other, gains_c, flat_ct),
        [(wide, F32), (wide, BF), (hidden_rows, BF), (hidden_rows, BF), *part_out],
        smem=(0,),
        scratch=[turned, *part_scratch],
        name="upper",
    )
    lower_parts, far_lower = tie((lower_parts, far_lower))
    lower_half = scatter_first("lower_sum", lower_parts)
    seconds, ffn, *upper_parts, _ = step_with_weight(
        hidden_step,
        place,
        far_lower,
        (lengths, flat_ct, slope, upper_c, second_norm, active),
        [(wide, BF), (wide, BF), *part_out],
        smem=(0,),
        scratch=[pltpu.VMEM(hidden_rows, BF), turned, *part_scratch],
        name="hidden_back",
    )
    upper_parts, lower_half, seconds = tie((upper_parts, lower_half, seconds))
    lower_half, seconds = tie((scatter_half(lower_half), seconds))
    lower_column = scatter_second("lower_sum", lower_half)
    seconds_other = swapped(seconds)
    upper_half = scatter_first("upper_sum", upper_parts)
    seconds_other, ffn = tie((seconds_other, ffn))
    ffn_other = swapped(ffn)
    middle_grad, low, head_grad = call(
        middle_step,
        [(wide, F32), (wide, BF), (features, BF)],
        (lengths, flat_ct, seconds, seconds_other, middle, gains_c, one),
        smem=(0,),
        name="middle_back",
    )
    grad_shape = (row_count, 3 * feats)
    sums_of = [pltpu.VMEM((row_count, LANES), F32)] * 2
    early, results = call(
        early_back_step,
        [(grad_shape, BF), (wide, BF)],
        (lengths, mixed, logsums, head_grad, cosine, sine, middle, ffn, ffn_other),
        smem=(0,),
        scratch=sums_of,
        name="attend_back",
    )
    early, head_grad, lower_column, upper_half = tie((early, head_grad, lower_column, upper_half))
    lower_sum = scatter_last("lower_sum", scatter_column(lower_column))
    upper_column = scatter_second("upper_sum", scatter_half(upper_half))
    part_out, part_scratch = product_out(width, 4 * feats, 2 * feats, local)
    late, *one_parts = call(
        partial(last_back_step, 1, len(part_out)),
        [(grad_shape, BF), *part_out],
        (place, lengths, mixed, logsums, head_grad, cosine, sine, low, heads, first_norm, early),
        smem=(0, 1),
        scratch=[*sums_of, turned, *part_scratch],
        name="last_back",
    )
    late, one_parts, upper_column, lower_sum = tie((late, one_parts, upper_column, lower_sum))
    one_half = scatter_first("one_sum", one_parts)
    upper_sum = scatter_last("upper_sum", scatter_column(upper_column))
    (sums,) = call(tail_kernel, [(wide, BF)], (early, late, one), name="tail")
    sums, one_half, upper_sum = tie((sums, one_half, upper_sum))
    one_column = scatter_second("one_sum", scatter_half(one_half))
    sums_other = swapped(sums)
    (input_grad,) = call(
        last_kernel,
        [(wide, F32)],
        (sums, sums_other, middle_grad, flat_in, gains_c),
        name="last",
    )
    one_column, input_grad = tie((one_column, input_grad))
    one_column, lower_sum, upper_sum = tie((scatter_column(one_column), lower_sum, upper_sum))
    one_sum = scatter_last("one_sum", one_column)
    lower_grad = added(lower_sum).T
    upper_wgrad = added(upper_sum)
    one_grad = tie(added(one_sum))
    turn = lambda a: a.transpose(1, 0, 2)
    proj_wgrad = jnp.stack([one_grad[:, c * feats : (c + 1) * feats] for c in (1, 2, 3)])
    proj_update = adamw_update(
        turn(proj_weight), turn(proj_first), turn(proj_second), proj_wgrad, RATE_MATRIX, DECAY
    )
    output_grad = one_grad[:, :feats].T
    kept = [
        row_sums(shard_one[:, feats : 4 * feats].astype(F32) * one_grad[:, feats:]),
        row_sums(upper_weight.astype(BF).astype(F32) * upper_wgrad),
    ]
    kept = jnp.concatenate(kept)
    gains_update = call(
        gains_step,
        [(norm_gains.shape, F32)] * 3 + [(norm_gains.shape, BF)],
        (kept, swapped(kept), norm_gains, gains_first, gains_second),
        name="gains",
    )

    updates = [
        [turn(u) for u in proj_update],
        adamw_update(output_weight, output_first, output_second, output_grad, RATE_OUTPUT, DECAY),
        adamw_update(upper_weight, upper_first, upper_second, upper_wgrad, RATE_MATRIX, DECAY),
        adamw_update(lower_weight, lower_first, lower_second, lower_grad, RATE_MATRIX, DECAY),
    ]
    return (
        results.reshape(inputs.shape),
        input_grad.reshape(inputs.shape),
        *[u[0] for u in updates],
        gains_update[0],
        *[u[1] for u in updates],
        gains_update[1],
        *[u[2] for u in updates],
        gains_update[2],
        *[u[0].astype(BF) for u in updates],
        gains_update[3],
    )


def solution(mesh):
    rows = P(None, "dp", None, None)
    weights = (P("dp", None, "mp"), P("mp", "dp"), P("dp", "mp"), P("mp", "dp"), P(None, "dp"))
    in_specs = (rows, rows, P(None, "dp"), *weights * 3)
    out_specs = (rows, rows, *weights * 4)
    return jax.shard_map(shards, mesh=mesh, in_specs=in_specs, out_specs=out_specs, check_vma=False)
```

```python
import math
from functools import partial

import jax
import jax.numpy as jnp
import numpy as np
from jax import lax
from jax.experimental import pallas as pl
from jax.experimental.pallas import tpu as pltpu
from jax.sharding import PartitionSpec as P

HD = 64
BLOCK = 16
LEN = 256
STEP = 10

EPSILON = 1e-05
BETA_ONE = 0.9
BETA_TWO = 0.95
ADAM_EPS = 1e-08
DECAY = 0.1
RATE_MATRIX = 0.02
RATE_OUTPUT = 0.1
RATE_GAIN = 0.8

LANES = 128
SPARE = 6 * 1024 * 1024
PAIR = 2 * HD
BF = jnp.bfloat16
F32 = jnp.float32
MASKED = -1e30
SCALE = HD**-0.5

NZ, NY, NX = 4, 2, 2
CHIPS = NZ * NY * NX


def call(kernel, out_shape, args, smem=(), scratch=(), flops=0, name=None):
    spaces = [
        pl.BlockSpec(memory_space=pltpu.SMEM if i in smem else pltpu.VMEM) for i in range(len(args))
    ]
    shapes = [jax.ShapeDtypeStruct(s, d) for s, d in out_shape]
    moved = sum(a.size * a.dtype.itemsize for a in [*args, *shapes])
    held = moved // 2 + sum(math.prod(r.shape) * jnp.dtype(r.dtype).itemsize for r in scratch)
    return pl.pallas_call(
        kernel,
        out_shape=shapes,
        in_specs=spaces,
        out_specs=[pl.BlockSpec(memory_space=pltpu.VMEM)] * len(shapes),
        scratch_shapes=list(scratch),
        compiler_params=pltpu.CompilerParams(vmem_limit_bytes=held + SPARE),
        cost_estimate=pl.CostEstimate(flops=int(flops), bytes_accessed=moved, transcendentals=0),
        name=name,
    )(*args)


def dot(a, b):
    return jnp.dot(a, b, preferred_element_type=F32)


def dot_nt(a, b):
    return lax.dot_general(a, b, (((1,), (1,)), ((), ())), preferred_element_type=F32)


def dot_tn(a, b):
    return lax.dot_general(a, b, (((0,), (0,)), ((), ())), preferred_element_type=F32)


def norm_parts(values):
    centre = jnp.mean(values, axis=-1, keepdims=True)
    shifted = values - centre
    spread = jnp.mean(shifted * shifted, axis=-1, keepdims=True)
    inverse = lax.rsqrt(spread + EPSILON)
    return shifted * inverse, inverse


def norm_back(normed, inverse, grads, gain):
    scaled = grads * gain
    mean_one = jnp.mean(scaled, axis=-1, keepdims=True)
    mean_two = jnp.mean(scaled * normed, axis=-1, keepdims=True)
    return (scaled - mean_one - normed * mean_two) * inverse


def stack_kernel(*refs):
    pieces, (part_a, part_b) = refs[:NZ], refs[NZ:]
    rows, cut = pieces[0].shape[0], part_a.shape[1]
    for k, piece in enumerate(pieces):
        at = slice(k * rows, (k + 1) * rows)
        part_a[at, :] = piece[:, :cut]
        part_b[at, :] = piece[:, cut:]


def pair_kernel(part_a, got_a, part_b, got_b, near_a, near_b):
    rows = part_a.shape[0]
    for part, got, near in ((part_a, got_a, near_a), (part_b, got_b, near_b)):
        near[:rows, :] = part[...]
        near[rows:, :] = got[...]


def assemble_kernel(place, near_a, far_a, near_b, far_b, whole):
    z, y, x = place[0], place[1], place[2]
    rows, cut = near_a.shape[0] // (2 * NZ), near_a.shape[1]
    for near in range(2):
        for k in range(NZ):
            at = slice((near * NZ + k) * rows, (near * NZ + k + 1) * rows)
            for far in range(2):
                z_of = lax.rem(z + NZ - k, NZ) * 4
                row_a = z_of + (y ^ far) * 2 + (x ^ near)
                row_b = z_of + (y ^ near) * 2 + (x ^ far)
                to_a = pl.ds(pl.multiple_of(row_a * rows, rows), rows)
                to_b = pl.ds(pl.multiple_of(row_b * rows, rows), rows)
                whole[to_a, :cut] = (far_a if far else near_a)[at, :]
                whole[to_b, cut:] = (far_b if far else near_b)[at, :]


def join_kernel(part_a, got_a, part_b, got_b, block):
    rows, cut = part_a.shape
    for columns, part, got in ((slice(0, cut), part_a, got_a), (slice(cut, None), part_b, got_b)):
        block[:rows, columns] = part[...]
        block[rows:, columns] = got[...]


def assemble_late_kernel(place, part_a, far_a, part_b, far_b, whole):
    z, y, x = place[0], place[1], place[2]
    rows, cut = part_a.shape[0] // (2 * NZ), part_a.shape[1]
    for k in range(NZ):
        z_of = lax.rem(z + NZ - k, NZ) * 4
        for near in range(2):
            at = slice((k * 2 + near) * rows, (k * 2 + near + 1) * rows)
            for far in range(2):
                row_a = z_of + (y ^ far) * 2 + (x ^ near)
                row_b = z_of + (y ^ near) * 2 + (x ^ far)
                to_a = pl.ds(pl.multiple_of(row_a * rows, rows), rows)
                to_b = pl.ds(pl.multiple_of(row_b * rows, rows), rows)
                whole[to_a, :cut] = (far_a if far else part_a)[at, :]
                whole[to_b, cut:] = (far_b if far else part_b)[at, :]


def half_kernel(kept_a, got_a, kept_b, got_b, own_a, send_a, own_b, send_b):
    rows = own_a.shape[0]
    for kept, got, own, send in ((kept_a, got_a, own_a, send_a), (kept_b, got_b, own_b, send_b)):
        own[...] = kept[:rows, :].astype(F32) + got[:rows, :].astype(F32)
        send[...] = (kept[rows:, :].astype(F32) + got[rows:, :].astype(F32)).astype(BF)


def column_kernel(own_a, got_a, own_b, got_b, mine, *sends):
    rows, cut = mine.shape[0], own_a.shape[1]
    for columns, own, got in ((slice(0, cut), own_a, got_a), (slice(cut, None), own_b, got_b)):
        mine[:, columns] = own[:rows, :] + got[:rows, :].astype(F32)
        for k, send in enumerate(sends, 1):
            at = slice(k * rows, (k + 1) * rows)
            send[:, columns] = (own[at, :] + got[at, :].astype(F32)).astype(BF)


def swap_halves(u):
    lane = lax.broadcasted_iota(jnp.int32, u.shape, 1)
    ahead = pltpu.roll(u, LANES - HD // 2, 1)
    behind = pltpu.roll(u, HD // 2, 1)
    return jnp.where(lane % HD < HD // 2, ahead, behind)


def qkv_kernel(inputs, gains, weight, cosine, sine, first_norm, mixed):
    feats = mixed.shape[1] // 3
    step = 256
    for start in range(0, inputs.shape[0], step):
        rows = pl.ds(start, step)
        normed, _ = norm_parts(inputs[rows, :].astype(F32))
        low = (normed * gains[0:1, :]).astype(BF)
        first_norm[rows, :] = low
        place = pl.ds(start % LEN, step)
        cos_rows, sin_rows = cosine[place, :], sine[place, :]
        product = dot(low, weight[:, feats : 4 * feats])
        for j in range(2 * feats // LANES):
            at = slice(j * LANES, (j + 1) * LANES)
            u = product[:, at]
            turned = (u * cos_rows + swap_halves(u) * sin_rows).astype(BF)
            if j < feats // LANES:
                turned = turned * jnp.asarray(SCALE, BF)
            mixed[rows, at] = turned
        mixed[rows, 2 * feats :] = product[:, 2 * feats :].astype(BF)


def visible_bias(length):
    row = lax.broadcasted_iota(jnp.int32, (LEN, LEN), 0) // BLOCK
    place = lax.broadcasted_iota(jnp.int32, (LEN, LEN), 1)
    col = place // BLOCK
    real = place < length
    bias = lambda seen: jnp.where(seen & real, 0.0, MASKED).astype(F32)
    noisy = jnp.concatenate([bias(col == row), bias(col < row)], axis=1)
    return noisy, bias(col <= row)


def own_lanes(value, head):
    lane = lax.broadcasted_iota(jnp.int32, value.shape, 1)
    mine = (lane < HD) if head == 0 else (lane >= HD)
    return jnp.where(mine, value, jnp.zeros_like(value))


def stacked_heads(value):
    first, second = own_lanes(value, 0), own_lanes(value, 1)
    return jnp.concatenate([first[:LEN], second[:LEN], first[LEN:], second[LEN:]])


def attend_kernel(micro, lengths, mixed, weight, heads, logsums, part):
    feats = heads.shape[1]
    bias_noisy, bias_clean = visible_bias(lengths[micro])
    lane = lax.broadcasted_iota(jnp.int32, (LEN, LANES), 1)
    base = micro * 2 * LEN
    sums = [jnp.zeros((LEN, LANES), F32), jnp.zeros((LEN, LANES), F32)]
    for pair in range(feats // PAIR):
        query, key, value = (
            mixed[pl.ds(base, 2 * LEN), c * feats + pair * PAIR : c * feats + (pair + 1) * PAIR]
            for c in range(3)
        )
        stacked = stacked_heads(query)
        on_clean = dot_nt(stacked, key[LEN:])
        on_noisy = dot_nt(stacked[: 2 * LEN], key[:LEN])
        clean_weights, noisy_weights = [], []
        for block in range(4):
            clean, head = divmod(block, 2)
            at = slice(block * LEN, (block + 1) * LEN)
            if clean:
                scores = on_clean[at] + bias_clean
                maximum = jnp.max(scores, axis=-1, keepdims=True)
                raised = jnp.exp(scores - maximum)
                summed = jnp.sum(raised, axis=-1, keepdims=True)
                clean_weights.append((raised * (1.0 / summed)).astype(BF))
            else:
                far = on_clean[at] + bias_noisy[:, LEN:]
                near = on_noisy[at] + bias_noisy[:, :LEN]
                maximum = jnp.max(jnp.maximum(far, near), axis=-1, keepdims=True)
                far, near = jnp.exp(far - maximum), jnp.exp(near - maximum)
                summed = jnp.sum(far + near, axis=-1, keepdims=True)
                inverse = 1.0 / summed
                clean_weights.append((far * inverse).astype(BF))
                noisy_weights.append((near * inverse).astype(BF))
            sums[clean] = jnp.where(
                lane == pair * 2 + head, maximum + jnp.log(summed), sums[clean]
            )
        out = dot(jnp.concatenate(clean_weights), value[LEN:])
        near = dot(jnp.concatenate(noisy_weights), value[:LEN])
        noisy = [out[h * LEN : (h + 1) * LEN] + near[h * LEN : (h + 1) * LEN] for h in range(2)]
        clean = [out[(2 + h) * LEN : (3 + h) * LEN] for h in range(2)]
        cols = slice(pair * PAIR, (pair + 1) * PAIR)
        heads[:LEN, cols] = jnp.where(lane < HD, *noisy).astype(BF)
        heads[LEN:, cols] = jnp.where(lane < HD, *clean).astype(BF)
    for clean in range(2):
        rows = slice(clean * LEN, (clean + 1) * LEN)
        logsums[rows, :] = sums[clean]
        part[rows, :] = dot_nt(heads[rows, :], weight[:, :feats]).astype(BF)


ERF_NUM = (
    -2.72614225801306e-10,
    2.77068142495902e-08,
    -2.10102402082508e-06,
    -5.69250639462346e-05,
    -7.34990630326855e-04,
    -2.95459980854025e-03,
    -1.60960333262415e-02,
)
ERF_DEN = (
    -1.45660718464996e-05,
    -2.13374055278905e-04,
    -1.68282697438203e-03,
    -7.37332916720468e-03,
    -1.42647390514189e-02,
)


def gelu_parts(v):
    u = jnp.clip(v * (0.5**0.5), -4.0, 4.0)
    square = u * u
    num = jnp.full_like(u, ERF_NUM[0])
    for c in ERF_NUM[1:]:
        num = num * square + c
    den = jnp.full_like(u, ERF_DEN[0])
    for c in ERF_DEN[1:]:
        den = den * square + c
    half = 0.5 + 0.5 * (u * num / den)
    bell = jnp.exp(v * v * -0.5) * 0.3989422804014327
    return v * half, half + v * bell


def upper_kernel(micro, inputs, own, other, gains, weight, middle, second_norm, active, slope):
    base = micro * 2 * LEN
    step, wide = 256, 512
    for start in range(0, 2 * LEN, step):
        rows = pl.ds(start, step)
        value = inputs[pl.ds(base + start, step), :].astype(F32) + (
            own[rows, :].astype(F32) + other[rows, :].astype(F32)
        )
        middle[rows, :] = value
        normed, _ = norm_parts(value)
        low = (normed * gains[1:2, :]).astype(BF)
        second_norm[rows, :] = low
        for c in range(0, weight.shape[1], wide):
            out, grad = gelu_parts(dot(low, weight[:, c : c + wide]))
            active[rows, c : c + wide] = out.astype(BF)
            slope[rows, c : c + wide] = grad.astype(BF)


def masked_rows(cotangent, start, step, length):
    place = lax.broadcasted_iota(jnp.int32, (step, 1), 0) + start % LEN
    rows = cotangent[pl.ds(start, step), :]
    return jnp.where(place < length, rows, jnp.zeros_like(rows))


def hidden_back_kernel(micro, lengths, cotangent, slope, lower, upper, upper_grad, part):
    base = micro * 2 * LEN
    step, wide = 256, 512
    for start in range(0, 2 * LEN, step):
        rows = pl.ds(start, step)
        low = masked_rows(cotangent, base + start, step, lengths[micro])
        total = jnp.zeros((step, part.shape[1]), F32)
        for c in range(0, lower.shape[1], wide):
            grad = dot(low, lower[:, c : c + wide]) * slope[rows, c : c + wide].astype(F32)
            grad = grad.astype(BF)
            upper_grad[rows, c : c + wide] = grad
            total = total + dot_nt(grad, upper[:, c : c + wide])
        part[rows, :] = total.astype(BF)


def middle_back_kernel(
    micro, lengths, cotangent, own, other, middle, gains, weight, middle_grad, low, head_grad
):
    base = micro * 2 * LEN
    step = 256
    feats = head_grad.shape[1]
    for start in range(0, 2 * LEN, step):
        rows = pl.ds(start, step)
        upstream = masked_rows(cotangent, base + start, step, lengths[micro]).astype(F32)
        back = own[rows, :].astype(F32) + other[rows, :].astype(F32)
        normed, inverse = norm_parts(middle[rows, :])
        grad = upstream + norm_back(normed, inverse, back, gains[1:2, :])
        middle_grad[rows, :] = grad
        low_grad = grad.astype(BF)
        low[rows, :] = low_grad
        head_grad[rows, :] = dot(low_grad, weight[:, :feats]).astype(BF)


def attend_back_kernel(
    micro, lengths, mixed, logsums, head_grad, cosine, sine, mixed_grad, key_sum, value_sum
):
    feats = head_grad.shape[1]
    bias_noisy, bias_clean = visible_bias(lengths[micro])
    base = micro * 2 * LEN
    cos_rows, sin_rows = cosine[...], sine[...]
    rows_of = [slice(block * LEN, (block + 1) * LEN) for block in range(4)]

    def turn_back(u):
        return u * cos_rows - swap_halves(u) * sin_rows

    lane = lax.broadcasted_iota(jnp.int32, (LEN, LANES), 1)
    for pair in range(feats // PAIR):
        cols = [
            slice(c * feats + pair * PAIR, c * feats + (pair + 1) * PAIR) for c in range(3)
        ]
        query, key, value = (mixed[pl.ds(base, 2 * LEN), c] for c in cols)
        stacked = stacked_heads(query)
        stacked_grad = stacked_heads(
            head_grad[pl.ds(base, 2 * LEN), pair * PAIR : (pair + 1) * PAIR]
        )
        score = [
            dot_nt(stacked[: 2 * LEN], key[:LEN]),
            dot_nt(stacked, key[LEN:]),
        ]
        prob_grad = [
            dot_nt(stacked_grad[: 2 * LEN], value[:LEN]),
            dot_nt(stacked_grad, value[LEN:]),
        ]
        probs_low, score_low = [[], []], [[], []]
        for block, at in enumerate(rows_of):
            clean, head = divmod(block, 2)
            index = pair * 2 + head
            logsum = logsums[pl.ds(base + clean * LEN, LEN), index : index + 1]
            parts = (1,) if clean else (0, 1)
            biases = {1: bias_clean} if clean else {0: bias_noisy[:, :LEN], 1: bias_noisy[:, LEN:]}
            probs = {p: jnp.exp(score[p][at] + biases[p] - logsum) for p in parts}
            products = [probs[p] * prob_grad[p][at] for p in parts]
            inner = jnp.sum(sum(products[1:], products[0]), axis=-1, keepdims=True)
            for p in parts:
                probs_low[p].append(probs[p].astype(BF))
                score_low[p].append((probs[p] * (prob_grad[p][at] - inner)).astype(BF))
        probs_low = [jnp.concatenate(blocks) for blocks in probs_low]
        score_low = [jnp.concatenate(blocks) for blocks in score_low]
        near, far = dot(score_low[0], key[:LEN]), dot(score_low[1], key[LEN:])
        noisy = [near[rows_of[h]] + far[rows_of[h]] for h in range(2)]
        clean = [far[rows_of[2 + h]] for h in range(2)]
        for p in range(2):
            rows = slice(p * LEN, (p + 1) * LEN)
            used = slice(0, (2 + 2 * p) * LEN)
            query_grad = jnp.where(lane < HD, *(clean if p else noisy))
            key_grad = dot_tn(score_low[p], stacked[used])
            value_grad = dot_tn(probs_low[p], stacked_grad[used])
            mixed_grad[rows, cols[0]] = turn_back(query_grad * SCALE).astype(BF)
            mixed_grad[rows, cols[1]] = turn_back(key_grad).astype(BF)
            mixed_grad[rows, cols[2]] = value_grad.astype(BF)


def put_blocks(place, product, scratch, column, x_first):
    z, y, x = place[0], place[1], place[2]
    rows = product.shape[0] // CHIPS
    for chip in range(CHIPS):
        to_z = lax.rem(chip // 4 + NZ - z, NZ)
        to_y, to_x = y ^ (chip // 2 % 2), x ^ (chip % 2)
        at = (to_x * 2 + to_y if x_first else to_y * 2 + to_x) * NZ + to_z
        scratch[pl.ds(pl.multiple_of(at * rows, rows), rows), column] = product[
            chip * rows : (chip + 1) * rows
        ].astype(BF)


def write_products(place, products, outs, scratch):
    if len(outs) == 1:
        for column, value in products:
            outs[0][:, column : column + value.shape[1]] = value.astype(BF)
        return
    cut = outs[0].shape[1]
    end = cut + outs[2].shape[1]
    for column, value in products:
        for part, (first, last) in enumerate(((0, cut), (cut, end))):
            low, high = max(column, first), min(column + value.shape[1], last)
            if low < high:
                put_blocks(
                    place,
                    value[:, low - column : high - column],
                    scratch[part],
                    slice(low - first, high - first),
                    part == 0,
                )
    size = outs[0].shape[0]
    for part in range(2):
        outs[2 * part][...] = scratch[part][:size, :]
        outs[2 * part + 1][...] = scratch[part][size:, :]


def product_out(width, columns, cut, local):
    if local:
        cuts = (cut, columns - cut)
        out = [((width // 2, c), BF) for c in cuts for _ in range(2)]
        return out, [pltpu.VMEM((width, c), BF) for c in cuts]
    return [((width, columns), BF)], []


def sum_products(turned, right, column, wide=256):
    products = []
    for c in range(0, right.shape[1], wide):
        high = min(c + wide, right.shape[1])
        products.append((column + c, dot(turned[...], right[:, c:high])))
    return products


def lower_grad_kernel(outs, place, lengths, cotangent, active, *refs):
    out_refs, (turned, *scratch) = refs[:outs], refs[outs:]
    for micro in range(2):
        for start in range(micro * 2 * LEN, (micro + 1) * 2 * LEN, LEN):
            low = masked_rows(cotangent, start, LEN, lengths[micro])
            turned[:, start : start + LEN] = low.T
    write_products(place, sum_products(turned, active, 0), out_refs, scratch)


def grads_kernel(count, outs, place, *refs):
    pairs, out_refs = refs[: 2 * count], refs[2 * count : 2 * count + outs]
    turned, *scratch = refs[2 * count + outs :]
    products, column = [], 0
    for left, right in zip(pairs[::2], pairs[1::2]):
        for start in range(0, left.shape[0], LEN):
            turned[:, start : start + LEN] = left[start : start + LEN, :].T
        products += sum_products(turned, right, column)
        column += right.shape[1]
    write_products(place, products, out_refs, scratch)


def grad_parts(place, pairs, cut, local, name):
    width, columns = pairs[0][0].shape[1], sum(right.shape[1] for _, right in pairs)
    out, scratch = product_out(width, columns, cut, local)
    return call(
        partial(grads_kernel, len(pairs), len(out)),
        out,
        (place, *(a for pair in pairs for a in pair)),
        smem=(0,),
        scratch=[pltpu.VMEM((width, 4 * LEN), BF)] + scratch,
        name=name,
    )


def half_rows(micro):
    return pl.ds(micro * 2 * LEN, 2 * LEN)


def write_gains(weight, gains):
    columns = weight[:, weight.shape[1] - LANES :].astype(F32)
    gains[...] = columns.T[: gains.shape[0], :]


def first_step(assembles, *refs):
    if assembles:
        place, near_a, far_a, near_b, far_b, inputs, cosine, sine, *outs = refs
        gains, first_norm, mixed, weight = outs
        assemble_kernel(place, near_a, far_a, near_b, far_b, weight)
    else:
        weight, inputs, cosine, sine, gains, first_norm, mixed = refs
    write_gains(weight, gains)
    qkv_kernel(inputs, gains, weight, cosine, sine, first_norm, mixed)


def attend_step(lengths, mixed, weight, heads, logsums, part):
    for m in range(2):
        at = half_rows(m)
        attend_kernel(m, lengths, mixed, weight, heads.at[at], logsums.at[at], part.at[at])


def upper_step(assembles, *refs):
    count = 4 if assembles else 1
    place = None
    if assembles:
        place, near_a, far_a, near_b, far_b, *refs = refs
        lengths, inputs, own, other, gains, cotangent, *outs = refs
        outs, parts, (weight, *scratch) = outs[:4], outs[4:8], outs[8:]
        assemble_kernel(place, near_a, far_a, near_b, far_b, weight)
    else:
        weight, lengths, inputs, own, other, gains, cotangent, *outs = refs
        outs, parts, scratch = outs[:4], outs[4:5], outs[5:]
    for m in range(2):
        at = half_rows(m)
        upper_kernel(
            m, inputs, own.at[at], other.at[at], gains, weight, *(out.at[at] for out in outs)
        )
    lower_grad_kernel(count, place, lengths, cotangent, outs[2], *parts, *scratch)


def hidden_step(assembles, *refs):
    if assembles:
        place, part_a, far_a, part_b, far_b, *refs = refs
        lengths, cotangent, slope, upper, second_norm, active, part, ffn, *parts = refs
        *parts, lower, upper_grad, turned, scratch_a, scratch_b = parts
        assemble_late_kernel(place, part_a, far_a, part_b, far_b, lower)
    else:
        lower, lengths, cotangent, slope, upper, second_norm, active, part, ffn, *parts = refs
        *parts, upper_grad, turned = parts
    for m in range(2):
        at = half_rows(m)
        hidden_back_kernel(
            m, lengths, cotangent, slope.at[at], lower, upper, upper_grad.at[at], part.at[at]
        )
    for start in range(0, active.shape[0], LEN):
        at = pl.ds(start, LEN)
        ffn[at, :] = dot_nt(active[at, :], lower[...]).astype(BF)
    if assembles:
        scratch = [turned, scratch_a, scratch_b]
        grads_kernel(1, len(parts), place, second_norm, upper_grad, *parts, *scratch)
    else:
        grads_kernel(1, len(parts), None, second_norm, upper_grad, *parts, turned)


def middle_step(
    lengths, cotangent, own, other, middle, gains, weight, middle_grad, low, head_grad
):
    for m in range(2):
        at = half_rows(m)
        middle_back_kernel(
            m,
            lengths,
            cotangent,
            own.at[at],
            other.at[at],
            middle.at[at],
            gains,
            weight,
            middle_grad.at[at],
            low.at[at],
            head_grad.at[at],
        )


def early_back_step(
    lengths,
    mixed,
    logsums,
    head_grad,
    cosine,
    sine,
    middle,
    ffn,
    ffn_other,
    early,
    results,
    key_sum,
    value_sum,
):
    attend_back_kernel(
        0, lengths, mixed, logsums, head_grad, cosine, sine, early, key_sum, value_sum
    )
    for start in range(0, middle.shape[0], LEN):
        at = pl.ds(start, LEN)
        total = ffn[at, :].astype(F32) + ffn_other[at, :].astype(F32)
        results[at, :] = (middle[at, :] + total).astype(BF)


def last_back_step(micro, outs, place, lengths, *refs):
    mixed, logsums, head_grad, cosine, sine, low, heads, first_norm, early, *refs = refs
    late, *refs = refs
    out_refs, (key_sum, value_sum, *scratch) = refs[:outs], refs[outs:]
    attend_back_kernel(
        micro, lengths, mixed, logsums, head_grad, cosine, sine, late, key_sum, value_sum
    )
    turned, *scratch = scratch
    rows = 2 * LEN

    def turn(left):
        for start in range(0, left.shape[0], LEN):
            turned[:, start : start + LEN] = left[start : start + LEN, :].T

    turn(low)
    products = sum_products(turned, heads, 0)
    turn(first_norm)
    for c in range(0, late.shape[1], LEN):
        high = min(c + LEN, late.shape[1])
        total = dot(turned[:, :rows], early[:, c:high]) + dot(turned[:, rows:], late[:, c:high])
        products.append((heads.shape[1] + c, total))
    write_products(place, products, out_refs, scratch)


def tail_kernel(early, late, weight, part):
    half, feats = early.shape[0], early.shape[1] // 3
    for start in range(0, 2 * half, LEN):
        mixed_grad = (early if start < half else late)[pl.ds(start % half, LEN), :]
        part[pl.ds(start, LEN), :] = dot_nt(mixed_grad, weight[:, feats : 4 * feats]).astype(BF)


def last_kernel(own, other, middle_grad, inputs, gains, input_grad):
    step = 128
    for start in range(0, inputs.shape[0], step):
        at = pl.ds(start, step)
        back = own[at, :].astype(F32) + other[at, :].astype(F32)
        normed, inverse = norm_parts(inputs[at, :].astype(F32))
        input_grad[at, :] = middle_grad[at, :] + norm_back(normed, inverse, back, gains[0:1, :])


def gains_step(own, other, weight, first, second, new, first_new, second_new, low):
    grad = (own[...] + other[...]) / weight[...].astype(BF).astype(F32)
    new[...], first_new[...], second_new[...] = adamw_update(
        weight[...], first[...], second[...], grad, RATE_GAIN, 0.0
    )
    low[...] = new[...].astype(BF)


def chip_pairs(move):
    pairs = []
    for chip in range(CHIPS):
        to_z, to_y, to_x = move(chip // 4, chip // 2 % 2, chip % 2)
        pairs.append((chip, to_z * 4 + to_y * 2 + to_x))
    return pairs


SWAP_X = chip_pairs(lambda z, y, x: (z, y, 1 - x))
SWAP_Y = chip_pairs(lambda z, y, x: (z, 1 - y, x))
SHIFT_Z = {k: chip_pairs(lambda z, y, x, k=k: ((z + k) % NZ, y, x)) for k in (1, 2, 3)}


def exchange(value, pairs, name):
    with jax.named_scope(name):
        return lax.ppermute(value, "dp", pairs)


tie = lax.optimization_barrier


def start_gather(name, shard, shifts=(1, 2, 3)):
    if lax.axis_size("dp") != CHIPS:
        return [lax.all_gather(shard, "dp", axis=0, tiled=True)] if 1 in shifts else [shard]
    return [shard] + [exchange(shard, SHIFT_Z[k], f"{name}_z{k}") for k in shifts]


def spread_near(name, arrived, cut):
    if len(arrived) == 1:
        return arrived
    rows, columns = arrived[0].shape
    out = [((NZ * rows, cut), BF), ((NZ * rows, columns - cut), BF)]
    part_a, part_b = call(stack_kernel, out, arrived, name="stack")
    return [
        part_a,
        exchange(part_a, SWAP_X, f"{name}_near_a"),
        part_b,
        exchange(part_b, SWAP_Y, f"{name}_near_b"),
    ]


def spread_far(name, near):
    if len(near) == 1:
        return near
    rows = 2 * near[0].shape[0]
    out = [((rows, near[0].shape[1]), BF), ((rows, near[2].shape[1]), BF)]
    near_a, near_b = call(pair_kernel, out, near, name="pair")
    far_a = exchange(near_a, SWAP_Y, f"{name}_far_a")
    return [near_a, far_a, near_b, exchange(near_b, SWAP_X, f"{name}_far_b")]


def step_with_weight(step, place, pieces, args, out, smem=(), scratch=(), name=None):
    if len(pieces) == 1:
        smem = [i + 1 for i in smem]
        held = dict(smem=smem, scratch=scratch, name=name)
        outs = call(partial(step, False), out, (pieces[0], *args), **held)
        return [*outs, pieces[0]]
    smem = [0] + [i + 1 + len(pieces) for i in smem]
    whole = ((2 * pieces[0].shape[0], pieces[0].shape[1] + pieces[2].shape[1]), BF)
    held = dict(smem=smem, scratch=scratch, name=name)
    return call(partial(step, True), [*out, whole], (place, *pieces, *args), **held)


def gather_near(name, shard):
    if lax.axis_size("dp") != CHIPS:
        return lax.all_gather(shard, "dp", axis=0, tiled=True)
    rows, columns = shard.shape
    cut = columns // 2
    part_a, part_b = shard[:, :cut], shard[:, cut:]
    got_a = exchange(part_a, SWAP_X, f"{name}_near_a")
    got_b = exchange(part_b, SWAP_Y, f"{name}_near_b")
    out = [((2 * rows, columns), BF)]
    return call(join_kernel, out, (part_a, got_a, part_b, got_b), name="join")[0]


def gather_z(name, block, shifts):
    if lax.axis_size("dp") != CHIPS:
        return []
    return [exchange(block, SHIFT_Z[k], f"{name}_z{k}") for k in shifts]


def gather_far(name, arrived):
    if len(arrived) == 1:
        return arrived
    rows, columns = arrived[0].shape
    cut = columns // 2
    out = [((NZ * rows, cut), BF)] * 2
    part_a, part_b = call(stack_kernel, out, arrived, name="stack")
    far_a = exchange(part_a, SWAP_Y, f"{name}_far_a")
    return [part_a, far_a, part_b, exchange(part_b, SWAP_X, f"{name}_far_b")]


def scatter_first(name, parts):
    if len(parts) == 1:
        return parts
    kept_a, sent_a, kept_b, sent_b = parts
    return [
        kept_a,
        exchange(sent_a, SWAP_X, f"{name}_first_a"),
        kept_b,
        exchange(sent_b, SWAP_Y, f"{name}_first_b"),
    ]


def scatter_half(halves):
    if len(halves) == 1:
        return halves
    rows = halves[0].shape[0] // 2
    out = [((rows, h.shape[1]), d) for h in (halves[0], halves[2]) for d in (F32, BF)]
    return call(half_kernel, out, halves, name="half")


def scatter_second(name, halves):
    if len(halves) == 1:
        return halves
    own_a, send_a, own_b, send_b = halves
    return [
        own_a,
        exchange(send_a, SWAP_Y, f"{name}_second_a"),
        own_b,
        exchange(send_b, SWAP_X, f"{name}_second_b"),
    ]


def scatter_column(columns):
    if len(columns) == 1:
        return columns
    rows, count = columns[0].shape[0] // NZ, columns[0].shape[1] + columns[2].shape[1]
    out = [((rows, count), F32)] + [((rows, count), BF)] * 3
    return call(column_kernel, out, columns, name="column")


def scatter_last(name, columns):
    if len(columns) == 1:
        return [lax.psum_scatter(columns[0], "dp", scatter_dimension=0, tiled=True)]
    mine, *sends = columns
    return [mine] + [exchange(s, SHIFT_Z[k], f"{name}_z{k}") for k, s in enumerate(sends, 1)]


def added(parts):
    return sum(p.astype(F32) for p in parts)


def swapped(value):
    return lax.ppermute(value, "mp", [(0, 1), (1, 0)])


def rotation():
    freqs = np.float32(10000.0) ** (np.float32(-2.0) * np.arange(HD // 2, dtype=np.float32) / np.float32(HD))
    angles = (np.arange(LEN, dtype=np.float32)[:, None] * freqs[None, :]).astype(np.float64)
    cosine, sine = np.cos(angles), np.sin(angles)
    cosine = np.tile(cosine, (1, 4)).astype(np.float32)
    return cosine, np.tile(np.concatenate([-sine, sine], axis=1), (1, 2)).astype(np.float32)


def row_sums(value):
    ones = jnp.ones((1, value.shape[1]), F32)
    contract = (((1,), (1,)), ((), ()))
    return lax.dot_general(
        ones, value, contract, precision=lax.Precision.HIGHEST, preferred_element_type=F32
    )


def adamw_update(weight, first, second, grad, rate, decay):
    first_new = BETA_ONE * first + (1.0 - BETA_ONE) * grad
    second_new = BETA_TWO * second + (1.0 - BETA_TWO) * grad * grad
    corrected = (
        first_new
        / (1.0 - BETA_ONE**STEP)
        / (jnp.sqrt(second_new / (1.0 - BETA_TWO**STEP)) + ADAM_EPS)
    )
    return (weight - rate * (corrected + decay * weight), first_new, second_new)


def shards(
    inputs,
    cotangent,
    lengths,
    proj_weight,
    output_weight,
    upper_weight,
    lower_weight,
    norm_gains,
    proj_first,
    output_first,
    upper_first,
    lower_first,
    gains_first,
    proj_second,
    output_second,
    upper_second,
    lower_second,
    gains_second,
):
    micro_count, _, row_count, width = inputs.shape
    feats = proj_weight.shape[2]
    hidden = upper_weight.shape[1]
    shard_rows = proj_weight.shape[0]
    local = lax.axis_size("dp") == CHIPS
    chip = lax.axis_index("dp").astype(jnp.int32)
    place = jnp.stack([chip // 4, chip // 2 % 2, chip % 2])
    micros = range(micro_count)
    lengths = lengths.reshape(-1)
    flat_in = inputs.reshape(-1, width)
    flat_ct = cotangent.reshape(-1, width)

    cosine, sine = (jnp.asarray(table) for table in rotation())

    gain_columns = jnp.pad(norm_gains.T.astype(BF), ((0, 0), (0, LANES - 2)))
    shard_one = jnp.concatenate(
        [
            output_weight.astype(BF).T,
            proj_weight.astype(BF).reshape(shard_rows, 3 * feats),
            gain_columns,
        ],
        axis=1,
    )
    upper_low, lower_low = upper_weight.astype(BF), lower_weight.astype(BF).T
    total_rows = micro_count * row_count
    wide, features = (total_rows, width), (total_rows, feats)
    arrived = start_gather("one", shard_one)
    near_lower = gather_near("lower", lower_low)
    arrived, upper_low, near_lower = tie((arrived, upper_low, near_lower))
    near = spread_near("one", arrived, 2 * feats)
    arrived_upper = start_gather("upper", upper_low, (1, 3))
    near, arrived_upper, upper_low = tie((near, arrived_upper, upper_low))
    pieces = spread_far("one", near)
    opposite = start_gather("upper", upper_low, (2,))[1:]
    opposite, near_lower = tie((opposite, near_lower)) if local else (opposite, near_lower)
    arrived_upper = [*arrived_upper[:2], *opposite, *arrived_upper[2:]]
    beside_lower = gather_z("lower", near_lower, (1, 3))
    near_upper = spread_near("upper", arrived_upper, hidden // 2)
    gains_c, first_norm, mixed, one = step_with_weight(
        first_step,
        place,
        pieces,
        (flat_in, cosine, sine),
        [((8, width), F32), (wide, BF), ((total_rows, 3 * feats), BF)],
        name="qkv",
    )
    mixed, near_upper, beside_lower, near_lower = tie((mixed, near_upper, beside_lower, near_lower))
    opposite_lower = gather_z("lower", near_lower, (2,))
    far_upper = spread_far("upper", near_upper)
    heads, logsums, attn = call(
        attend_step,
        [(features, BF), ((total_rows, LANES), F32), (wide, BF)],
        (lengths, mixed, one),
        smem=(0,),
        name="attend",
    )
    far_upper, opposite_lower, attn = tie((far_upper, opposite_lower, attn))
    arrived_lower = [near_lower, *beside_lower[:1], *opposite_lower, *beside_lower[1:]]
    attn_other = swapped(attn)
    far_lower = gather_far("lower", arrived_lower)
    hidden_rows = (total_rows, hidden)
    part_out, part_scratch = product_out(width, hidden, hidden // 2, local)
    turned = pltpu.VMEM((width, total_rows), BF)
    middle, second_norm, active, slope, *lower_parts, upper_c = step_with_weight(
        upper_step,
        place,
        far_upper,
        (lengths, flat_in, attn, attn_other, gains_c, flat_ct),
        [(wide, F32), (wide, BF), (hidden_rows, BF), (hidden_rows, BF), *part_out],
        smem=(0,),
        scratch=[turned, *part_scratch],
        name="upper",
    )
    lower_parts, far_lower = tie((lower_parts, far_lower))
    lower_half = scatter_first("lower_sum", lower_parts)
    seconds, ffn, *upper_parts, _ = step_with_weight(
        hidden_step,
        place,
        far_lower,
        (lengths, flat_ct, slope, upper_c, second_norm, active),
        [(wide, BF), (wide, BF), *part_out],
        smem=(0,),
        scratch=[pltpu.VMEM(hidden_rows, BF), turned, *part_scratch],
        name="hidden_back",
    )
    upper_parts, lower_half, seconds = tie((upper_parts, lower_half, seconds))
    lower_half, seconds = tie((scatter_half(lower_half), seconds))
    lower_column = scatter_second("lower_sum", lower_half)
    seconds_other = swapped(seconds)
    upper_half = scatter_first("upper_sum", upper_parts)
    seconds_other, ffn = tie((seconds_other, ffn))
    ffn_other = swapped(ffn)
    middle_grad, low, head_grad = call(
        middle_step,
        [(wide, F32), (wide, BF), (features, BF)],
        (lengths, flat_ct, seconds, seconds_other, middle, gains_c, one),
        smem=(0,),
        name="middle_back",
    )
    grad_shape = (row_count, 3 * feats)
    sums_of = [pltpu.VMEM((row_count, LANES), F32)] * 2
    early, results = call(
        early_back_step,
        [(grad_shape, BF), (wide, BF)],
        (lengths, mixed, logsums, head_grad, cosine, sine, middle, ffn, ffn_other),
        smem=(0,),
        scratch=sums_of,
        name="attend_back",
    )
    early, head_grad, lower_column, upper_half = tie((early, head_grad, lower_column, upper_half))
    lower_sum = scatter_last("lower_sum", scatter_column(lower_column))
    upper_column = scatter_second("upper_sum", scatter_half(upper_half))
    part_out, part_scratch = product_out(width, 4 * feats, 2 * feats, local)
    late, *one_parts = call(
        partial(last_back_step, 1, len(part_out)),
        [(grad_shape, BF), *part_out],
        (place, lengths, mixed, logsums, head_grad, cosine, sine, low, heads, first_norm, early),
        smem=(0, 1),
        scratch=[*sums_of, turned, *part_scratch],
        name="last_back",
    )
    late, one_parts, upper_column, lower_sum = tie((late, one_parts, upper_column, lower_sum))
    one_half = scatter_first("one_sum", one_parts)
    upper_sum = scatter_last("upper_sum", scatter_column(upper_column))
    (sums,) = call(tail_kernel, [(wide, BF)], (early, late, one), name="tail")
    sums, one_half, upper_sum = tie((sums, one_half, upper_sum))
    one_column = scatter_second("one_sum", scatter_half(one_half))
    sums_other = swapped(sums)
    (input_grad,) = call(
        last_kernel,
        [(wide, F32)],
        (sums, sums_other, middle_grad, flat_in, gains_c),
        name="last",
    )
    one_column, input_grad = tie((one_column, input_grad))
    one_column, lower_sum, upper_sum = tie((scatter_column(one_column), lower_sum, upper_sum))
    one_sum = scatter_last("one_sum", one_column)
    lower_grad = added(lower_sum).T
    upper_wgrad = added(upper_sum)
    one_grad = tie(added(one_sum))
    turn = lambda a: a.transpose(1, 0, 2)
    proj_wgrad = jnp.stack([one_grad[:, c * feats : (c + 1) * feats] for c in (1, 2, 3)])
    proj_update = adamw_update(
        turn(proj_weight), turn(proj_first), turn(proj_second), proj_wgrad, RATE_MATRIX, DECAY
    )
    output_grad = one_grad[:, :feats].T
    kept = [
        row_sums(shard_one[:, feats : 4 * feats].astype(F32) * one_grad[:, feats:]),
        row_sums(upper_weight.astype(BF).astype(F32) * upper_wgrad),
    ]
    kept = jnp.concatenate(kept)
    gains_update = call(
        gains_step,
        [(norm_gains.shape, F32)] * 3 + [(norm_gains.shape, BF)],
        (kept, swapped(kept), norm_gains, gains_first, gains_second),
        name="gains",
    )

    updates = [
        [turn(u) for u in proj_update],
        adamw_update(output_weight, output_first, output_second, output_grad, RATE_OUTPUT, DECAY),
        adamw_update(upper_weight, upper_first, upper_second, upper_wgrad, RATE_MATRIX, DECAY),
        adamw_update(lower_weight, lower_first, lower_second, lower_grad, RATE_MATRIX, DECAY),
    ]
    return (
        results.reshape(inputs.shape),
        input_grad.reshape(inputs.shape),
        *[u[0] for u in updates],
        gains_update[0],
        *[u[1] for u in updates],
        gains_update[1],
        *[u[2] for u in updates],
        gains_update[2],
        *[u[0].astype(BF) for u in updates],
        gains_update[3],
    )


def solution(mesh):
    rows = P(None, "dp", None, None)
    weights = (P("dp", None, "mp"), P("mp", "dp"), P("dp", "mp"), P("mp", "dp"), P(None, "dp"))
    in_specs = (rows, rows, P(None, "dp"), *weights * 3)
    out_specs = (rows, rows, *weights * 4)
    return jax.shard_map(shards, mesh=mesh, in_specs=in_specs, out_specs=out_specs, check_vma=False)
```

```python
import math
from functools import partial

import jax
import jax.numpy as jnp
import numpy as np
from jax import lax
from jax.experimental import pallas as pl
from jax.experimental.pallas import tpu as pltpu
from jax.sharding import PartitionSpec as P

HD = 64
BLOCK = 16
LEN = 256
STEP = 10

EPSILON = 1e-05
BETA_ONE = 0.9
BETA_TWO = 0.95
ADAM_EPS = 1e-08
DECAY = 0.1
RATE_MATRIX = 0.02
RATE_OUTPUT = 0.1
RATE_GAIN = 0.8

LANES = 128
SPARE = 6 * 1024 * 1024
PAIR = 2 * HD
BF = jnp.bfloat16
F32 = jnp.float32
MASKED = -1e30
SCALE = HD**-0.5

NZ, NY, NX = 4, 2, 2
CHIPS = NZ * NY * NX


def call(kernel, out_shape, args, smem=(), scratch=(), flops=0, name=None):
    spaces = [
        pl.BlockSpec(memory_space=pltpu.SMEM if i in smem else pltpu.VMEM) for i in range(len(args))
    ]
    shapes = [jax.ShapeDtypeStruct(s, d) for s, d in out_shape]
    moved = sum(a.size * a.dtype.itemsize for a in [*args, *shapes])
    held = moved // 2 + sum(math.prod(r.shape) * jnp.dtype(r.dtype).itemsize for r in scratch)
    return pl.pallas_call(
        kernel,
        out_shape=shapes,
        in_specs=spaces,
        out_specs=[pl.BlockSpec(memory_space=pltpu.VMEM)] * len(shapes),
        scratch_shapes=list(scratch),
        compiler_params=pltpu.CompilerParams(vmem_limit_bytes=held + SPARE),
        cost_estimate=pl.CostEstimate(flops=int(flops), bytes_accessed=moved, transcendentals=0),
        name=name,
    )(*args)


def dot(a, b):
    return jnp.dot(a, b, preferred_element_type=F32)


def dot_nt(a, b):
    return lax.dot_general(a, b, (((1,), (1,)), ((), ())), preferred_element_type=F32)


def dot_tn(a, b):
    return lax.dot_general(a, b, (((0,), (0,)), ((), ())), preferred_element_type=F32)


def norm_parts(values):
    centre = jnp.mean(values, axis=-1, keepdims=True)
    shifted = values - centre
    spread = jnp.mean(shifted * shifted, axis=-1, keepdims=True)
    inverse = lax.rsqrt(spread + EPSILON)
    return shifted * inverse, inverse


def norm_back(normed, inverse, grads, gain):
    scaled = grads * gain
    mean_one = jnp.mean(scaled, axis=-1, keepdims=True)
    mean_two = jnp.mean(scaled * normed, axis=-1, keepdims=True)
    return (scaled - mean_one - normed * mean_two) * inverse


def stack_kernel(*refs):
    pieces, (part_a, part_b) = refs[:NZ], refs[NZ:]
    rows, cut = pieces[0].shape[0], part_a.shape[1]
    for k, piece in enumerate(pieces):
        at = slice(k * rows, (k + 1) * rows)
        part_a[at, :] = piece[:, :cut]
        part_b[at, :] = piece[:, cut:]


def pair_kernel(part_a, got_a, part_b, got_b, near_a, near_b):
    rows = part_a.shape[0]
    for part, got, near in ((part_a, got_a, near_a), (part_b, got_b, near_b)):
        near[:rows, :] = part[...]
        near[rows:, :] = got[...]


def assemble_kernel(place, near_a, far_a, near_b, far_b, whole):
    z, y, x = place[0], place[1], place[2]
    rows, cut = near_a.shape[0] // (2 * NZ), near_a.shape[1]
    for near in range(2):
        for k in range(NZ):
            at = slice((near * NZ + k) * rows, (near * NZ + k + 1) * rows)
            for far in range(2):
                z_of = lax.rem(z + NZ - k, NZ) * 4
                row_a = z_of + (y ^ far) * 2 + (x ^ near)
                row_b = z_of + (y ^ near) * 2 + (x ^ far)
                to_a = pl.ds(pl.multiple_of(row_a * rows, rows), rows)
                to_b = pl.ds(pl.multiple_of(row_b * rows, rows), rows)
                whole[to_a, :cut] = (far_a if far else near_a)[at, :]
                whole[to_b, cut:] = (far_b if far else near_b)[at, :]


def join_kernel(part_a, got_a, part_b, got_b, block):
    rows, cut = part_a.shape
    for columns, part, got in ((slice(0, cut), part_a, got_a), (slice(cut, None), part_b, got_b)):
        block[:rows, columns] = part[...]
        block[rows:, columns] = got[...]


def assemble_late_kernel(place, part_a, far_a, part_b, far_b, whole):
    z, y, x = place[0], place[1], place[2]
    rows, cut = part_a.shape[0] // (2 * NZ), part_a.shape[1]
    for k in range(NZ):
        z_of = lax.rem(z + NZ - k, NZ) * 4
        for near in range(2):
            at = slice((k * 2 + near) * rows, (k * 2 + near + 1) * rows)
            for far in range(2):
                row_a = z_of + (y ^ far) * 2 + (x ^ near)
                row_b = z_of + (y ^ near) * 2 + (x ^ far)
                to_a = pl.ds(pl.multiple_of(row_a * rows, rows), rows)
                to_b = pl.ds(pl.multiple_of(row_b * rows, rows), rows)
                whole[to_a, :cut] = (far_a if far else part_a)[at, :]
                whole[to_b, cut:] = (far_b if far else part_b)[at, :]


def half_kernel(kept_a, got_a, kept_b, got_b, own_a, send_a, own_b, send_b):
    rows = own_a.shape[0]
    for kept, got, own, send in ((kept_a, got_a, own_a, send_a), (kept_b, got_b, own_b, send_b)):
        own[...] = kept[:rows, :].astype(F32) + got[:rows, :].astype(F32)
        send[...] = (kept[rows:, :].astype(F32) + got[rows:, :].astype(F32)).astype(BF)


def column_kernel(own_a, got_a, own_b, got_b, mine, *sends):
    rows, cut = mine.shape[0], own_a.shape[1]
    for columns, own, got in ((slice(0, cut), own_a, got_a), (slice(cut, None), own_b, got_b)):
        mine[:, columns] = own[:rows, :] + got[:rows, :].astype(F32)
        for k, send in enumerate(sends, 1):
            at = slice(k * rows, (k + 1) * rows)
            send[:, columns] = (own[at, :] + got[at, :].astype(F32)).astype(BF)


def swap_halves(u):
    lane = lax.broadcasted_iota(jnp.int32, u.shape, 1)
    ahead = pltpu.roll(u, LANES - HD // 2, 1)
    behind = pltpu.roll(u, HD // 2, 1)
    return jnp.where(lane % HD < HD // 2, ahead, behind)


def qkv_kernel(inputs, gains, weight, cosine, sine, first_norm, mixed):
    feats = mixed.shape[1] // 3
    step = 256
    for start in range(0, inputs.shape[0], step):
        rows = pl.ds(start, step)
        normed, _ = norm_parts(inputs[rows, :].astype(F32))
        low = (normed * gains[0:1, :]).astype(BF)
        first_norm[rows, :] = low
        place = pl.ds(start % LEN, step)
        cos_rows, sin_rows = cosine[place, :], sine[place, :]
        product = dot(low, weight[:, feats : 4 * feats])
        for j in range(2 * feats // LANES):
            at = slice(j * LANES, (j + 1) * LANES)
            u = product[:, at]
            turned = (u * cos_rows + swap_halves(u) * sin_rows).astype(BF)
            if j < feats // LANES:
                turned = turned * jnp.asarray(SCALE, BF)
            mixed[rows, at] = turned
        mixed[rows, 2 * feats :] = product[:, 2 * feats :].astype(BF)


def visible_bias(length):
    row = lax.broadcasted_iota(jnp.int32, (LEN, LEN), 0) // BLOCK
    place = lax.broadcasted_iota(jnp.int32, (LEN, LEN), 1)
    col = place // BLOCK
    real = place < length
    bias = lambda seen: jnp.where(seen & real, 0.0, MASKED).astype(F32)
    noisy = jnp.concatenate([bias(col == row), bias(col < row)], axis=1)
    return noisy, bias(col <= row)


def own_lanes(value, head):
    lane = lax.broadcasted_iota(jnp.int32, value.shape, 1)
    mine = (lane < HD) if head == 0 else (lane >= HD)
    return jnp.where(mine, value, jnp.zeros_like(value))


def stacked_heads(value):
    first, second = own_lanes(value, 0), own_lanes(value, 1)
    return jnp.concatenate([first[:LEN], second[:LEN], first[LEN:], second[LEN:]])


def attend_kernel(micro, lengths, mixed, weight, heads, logsums, part):
    feats = heads.shape[1]
    bias_noisy, bias_clean = visible_bias(lengths[micro])
    lane = lax.broadcasted_iota(jnp.int32, (LEN, LANES), 1)
    base = micro * 2 * LEN
    sums = [jnp.zeros((LEN, LANES), F32), jnp.zeros((LEN, LANES), F32)]
    for pair in range(feats // PAIR):
        query, key, value = (
            mixed[pl.ds(base, 2 * LEN), c * feats + pair * PAIR : c * feats + (pair + 1) * PAIR]
            for c in range(3)
        )
        stacked = stacked_heads(query)
        on_clean = dot_nt(stacked, key[LEN:])
        on_noisy = dot_nt(stacked[: 2 * LEN], key[:LEN])
        clean_weights, noisy_weights = [], []
        for block in range(4):
            clean, head = divmod(block, 2)
            at = slice(block * LEN, (block + 1) * LEN)
            if clean:
                scores = on_clean[at] + bias_clean
                maximum = jnp.max(scores, axis=-1, keepdims=True)
                raised = jnp.exp(scores - maximum)
                summed = jnp.sum(raised, axis=-1, keepdims=True)
                clean_weights.append((raised * (1.0 / summed)).astype(BF))
            else:
                far = on_clean[at] + bias_noisy[:, LEN:]
                near = on_noisy[at] + bias_noisy[:, :LEN]
                maximum = jnp.max(jnp.maximum(far, near), axis=-1, keepdims=True)
                far, near = jnp.exp(far - maximum), jnp.exp(near - maximum)
                summed = jnp.sum(far + near, axis=-1, keepdims=True)
                inverse = 1.0 / summed
                clean_weights.append((far * inverse).astype(BF))
                noisy_weights.append((near * inverse).astype(BF))
            sums[clean] = jnp.where(
                lane == pair * 2 + head, maximum + jnp.log(summed), sums[clean]
            )
        out = dot(jnp.concatenate(clean_weights), value[LEN:])
        near = dot(jnp.concatenate(noisy_weights), value[:LEN])
        noisy = [out[h * LEN : (h + 1) * LEN] + near[h * LEN : (h + 1) * LEN] for h in range(2)]
        clean = [out[(2 + h) * LEN : (3 + h) * LEN] for h in range(2)]
        cols = slice(pair * PAIR, (pair + 1) * PAIR)
        heads[:LEN, cols] = jnp.where(lane < HD, *noisy).astype(BF)
        heads[LEN:, cols] = jnp.where(lane < HD, *clean).astype(BF)
    for clean in range(2):
        rows = slice(clean * LEN, (clean + 1) * LEN)
        logsums[rows, :] = sums[clean]
        part[rows, :] = dot_nt(heads[rows, :], weight[:, :feats]).astype(BF)


ERF_NUM = (
    -2.72614225801306e-10,
    2.77068142495902e-08,
    -2.10102402082508e-06,
    -5.69250639462346e-05,
    -7.34990630326855e-04,
    -2.95459980854025e-03,
    -1.60960333262415e-02,
)
ERF_DEN = (
    -1.45660718464996e-05,
    -2.13374055278905e-04,
    -1.68282697438203e-03,
    -7.37332916720468e-03,
    -1.42647390514189e-02,
)


def gelu_parts(v):
    u = jnp.clip(v * (0.5**0.5), -4.0, 4.0)
    square = u * u
    num = jnp.full_like(u, ERF_NUM[0])
    for c in ERF_NUM[1:]:
        num = num * square + c
    den = jnp.full_like(u, ERF_DEN[0])
    for c in ERF_DEN[1:]:
        den = den * square + c
    half = 0.5 + 0.5 * (u * num / den)
    bell = jnp.exp(v * v * -0.5) * 0.3989422804014327
    return v * half, half + v * bell


def upper_kernel(micro, inputs, own, other, gains, weight, middle, second_norm, active, slope):
    base = micro * 2 * LEN
    step, wide = 256, 512
    for start in range(0, 2 * LEN, step):
        rows = pl.ds(start, step)
        value = inputs[pl.ds(base + start, step), :].astype(F32) + (
            own[rows, :].astype(F32) + other[rows, :].astype(F32)
        )
        middle[rows, :] = value
        normed, _ = norm_parts(value)
        low = (normed * gains[1:2, :]).astype(BF)
        second_norm[rows, :] = low
        for c in range(0, weight.shape[1], wide):
            out, grad = gelu_parts(dot(low, weight[:, c : c + wide]))
            active[rows, c : c + wide] = out.astype(BF)
            slope[rows, c : c + wide] = grad.astype(BF)


def masked_rows(cotangent, start, step, length):
    place = lax.broadcasted_iota(jnp.int32, (step, 1), 0) + start % LEN
    rows = cotangent[pl.ds(start, step), :]
    return jnp.where(place < length, rows, jnp.zeros_like(rows))


def hidden_back_kernel(micro, lengths, cotangent, slope, lower, upper, upper_grad, part):
    base = micro * 2 * LEN
    step, wide = 256, 512
    for start in range(0, 2 * LEN, step):
        rows = pl.ds(start, step)
        low = masked_rows(cotangent, base + start, step, lengths[micro])
        total = jnp.zeros((step, part.shape[1]), F32)
        for c in range(0, lower.shape[1], wide):
            grad = dot(low, lower[:, c : c + wide]) * slope[rows, c : c + wide].astype(F32)
            grad = grad.astype(BF)
            upper_grad[rows, c : c + wide] = grad
            total = total + dot_nt(grad, upper[:, c : c + wide])
        part[rows, :] = total.astype(BF)


def middle_back_kernel(
    micro, lengths, cotangent, own, other, middle, gains, weight, middle_grad, low, head_grad
):
    base = micro * 2 * LEN
    step = 256
    feats = head_grad.shape[1]
    for start in range(0, 2 * LEN, step):
        rows = pl.ds(start, step)
        upstream = masked_rows(cotangent, base + start, step, lengths[micro]).astype(F32)
        back = own[rows, :].astype(F32) + other[rows, :].astype(F32)
        normed, inverse = norm_parts(middle[rows, :])
        grad = upstream + norm_back(normed, inverse, back, gains[1:2, :])
        middle_grad[rows, :] = grad
        low_grad = grad.astype(BF)
        low[rows, :] = low_grad
        head_grad[rows, :] = dot(low_grad, weight[:, :feats]).astype(BF)


def attend_back_kernel(
    micro, lengths, mixed, logsums, head_grad, cosine, sine, mixed_grad, key_sum, value_sum
):
    feats = head_grad.shape[1]
    bias_noisy, bias_clean = visible_bias(lengths[micro])
    base = micro * 2 * LEN
    cos_rows, sin_rows = cosine[...], sine[...]
    rows_of = [slice(block * LEN, (block + 1) * LEN) for block in range(4)]

    def turn_back(u):
        return u * cos_rows - swap_halves(u) * sin_rows

    lane = lax.broadcasted_iota(jnp.int32, (LEN, LANES), 1)
    for pair in range(feats // PAIR):
        cols = [
            slice(c * feats + pair * PAIR, c * feats + (pair + 1) * PAIR) for c in range(3)
        ]
        query, key, value = (mixed[pl.ds(base, 2 * LEN), c] for c in cols)
        stacked = stacked_heads(query)
        stacked_grad = stacked_heads(
            head_grad[pl.ds(base, 2 * LEN), pair * PAIR : (pair + 1) * PAIR]
        )
        score = [
            dot_nt(stacked[: 2 * LEN], key[:LEN]),
            dot_nt(stacked, key[LEN:]),
        ]
        prob_grad = [
            dot_nt(stacked_grad[: 2 * LEN], value[:LEN]),
            dot_nt(stacked_grad, value[LEN:]),
        ]
        probs_low, score_low = [[], []], [[], []]
        for block, at in enumerate(rows_of):
            clean, head = divmod(block, 2)
            index = pair * 2 + head
            logsum = logsums[pl.ds(base + clean * LEN, LEN), index : index + 1]
            parts = (1,) if clean else (0, 1)
            biases = {1: bias_clean} if clean else {0: bias_noisy[:, :LEN], 1: bias_noisy[:, LEN:]}
            probs = {p: jnp.exp(score[p][at] + biases[p] - logsum) for p in parts}
            products = [probs[p] * prob_grad[p][at] for p in parts]
            inner = jnp.sum(sum(products[1:], products[0]), axis=-1, keepdims=True)
            for p in parts:
                probs_low[p].append(probs[p].astype(BF))
                score_low[p].append((probs[p] * (prob_grad[p][at] - inner)).astype(BF))
        probs_low = [jnp.concatenate(blocks) for blocks in probs_low]
        score_low = [jnp.concatenate(blocks) for blocks in score_low]
        near, far = dot(score_low[0], key[:LEN]), dot(score_low[1], key[LEN:])
        noisy = [near[rows_of[h]] + far[rows_of[h]] for h in range(2)]
        clean = [far[rows_of[2 + h]] for h in range(2)]
        for p in range(2):
            rows = slice(p * LEN, (p + 1) * LEN)
            used = slice(0, (2 + 2 * p) * LEN)
            query_grad = jnp.where(lane < HD, *(clean if p else noisy))
            key_grad = dot_tn(score_low[p], stacked[used])
            value_grad = dot_tn(probs_low[p], stacked_grad[used])
            mixed_grad[rows, cols[0]] = turn_back(query_grad * SCALE).astype(BF)
            mixed_grad[rows, cols[1]] = turn_back(key_grad).astype(BF)
            mixed_grad[rows, cols[2]] = value_grad.astype(BF)


def put_blocks(place, product, scratch, column, x_first):
    z, y, x = place[0], place[1], place[2]
    rows = product.shape[0] // CHIPS
    for chip in range(CHIPS):
        to_z = lax.rem(chip // 4 + NZ - z, NZ)
        to_y, to_x = y ^ (chip // 2 % 2), x ^ (chip % 2)
        at = (to_x * 2 + to_y if x_first else to_y * 2 + to_x) * NZ + to_z
        scratch[pl.ds(pl.multiple_of(at * rows, rows), rows), column] = product[
            chip * rows : (chip + 1) * rows
        ].astype(BF)


def write_products(place, products, outs, scratch):
    if len(outs) == 1:
        for column, value in products:
            outs[0][:, column : column + value.shape[1]] = value.astype(BF)
        return
    cut = outs[0].shape[1]
    end = cut + outs[2].shape[1]
    for column, value in products:
        for part, (first, last) in enumerate(((0, cut), (cut, end))):
            low, high = max(column, first), min(column + value.shape[1], last)
            if low < high:
                put_blocks(
                    place,
                    value[:, low - column : high - column],
                    scratch[part],
                    slice(low - first, high - first),
                    part == 0,
                )
    size = outs[0].shape[0]
    for part in range(2):
        outs[2 * part][...] = scratch[part][:size, :]
        outs[2 * part + 1][...] = scratch[part][size:, :]


def product_out(width, columns, cut, local):
    if local:
        cuts = (cut, columns - cut)
        out = [((width // 2, c), BF) for c in cuts for _ in range(2)]
        return out, [pltpu.VMEM((width, c), BF) for c in cuts]
    return [((width, columns), BF)], []


def sum_products(turned, right, column, wide=256):
    products = []
    for c in range(0, right.shape[1], wide):
        high = min(c + wide, right.shape[1])
        products.append((column + c, dot(turned[...], right[:, c:high])))
    return products


def lower_grad_kernel(outs, place, lengths, cotangent, active, *refs):
    out_refs, (turned, *scratch) = refs[:outs], refs[outs:]
    for micro in range(2):
        for start in range(micro * 2 * LEN, (micro + 1) * 2 * LEN, LEN):
            low = masked_rows(cotangent, start, LEN, lengths[micro])
            turned[:, start : start + LEN] = low.T
    write_products(place, sum_products(turned, active, 0), out_refs, scratch)


def grads_kernel(count, outs, place, *refs):
    pairs, out_refs = refs[: 2 * count], refs[2 * count : 2 * count + outs]
    turned, *scratch = refs[2 * count + outs :]
    products, column = [], 0
    for left, right in zip(pairs[::2], pairs[1::2]):
        for start in range(0, left.shape[0], LEN):
            turned[:, start : start + LEN] = left[start : start + LEN, :].T
        products += sum_products(turned, right, column)
        column += right.shape[1]
    write_products(place, products, out_refs, scratch)


def grad_parts(place, pairs, cut, local, name):
    width, columns = pairs[0][0].shape[1], sum(right.shape[1] for _, right in pairs)
    out, scratch = product_out(width, columns, cut, local)
    return call(
        partial(grads_kernel, len(pairs), len(out)),
        out,
        (place, *(a for pair in pairs for a in pair)),
        smem=(0,),
        scratch=[pltpu.VMEM((width, 4 * LEN), BF)] + scratch,
        name=name,
    )


def half_rows(micro):
    return pl.ds(micro * 2 * LEN, 2 * LEN)


def write_gains(weight, gains):
    columns = weight[:, weight.shape[1] - LANES :].astype(F32)
    gains[...] = columns.T[: gains.shape[0], :]


def first_step(assembles, *refs):
    if assembles:
        place, near_a, far_a, near_b, far_b, inputs, cosine, sine, *outs = refs
        gains, first_norm, mixed, weight = outs
        assemble_kernel(place, near_a, far_a, near_b, far_b, weight)
    else:
        weight, inputs, cosine, sine, gains, first_norm, mixed = refs
    write_gains(weight, gains)
    qkv_kernel(inputs, gains, weight, cosine, sine, first_norm, mixed)


def attend_step(lengths, mixed, weight, heads, logsums, part):
    for m in range(2):
        at = half_rows(m)
        attend_kernel(m, lengths, mixed, weight, heads.at[at], logsums.at[at], part.at[at])


def upper_step(assembles, *refs):
    count = 4 if assembles else 1
    place = None
    if assembles:
        place, near_a, far_a, near_b, far_b, *refs = refs
        lengths, inputs, own, other, gains, cotangent, *outs = refs
        outs, parts, (weight, *scratch) = outs[:4], outs[4:8], outs[8:]
        assemble_kernel(place, near_a, far_a, near_b, far_b, weight)
    else:
        weight, lengths, inputs, own, other, gains, cotangent, *outs = refs
        outs, parts, scratch = outs[:4], outs[4:5], outs[5:]
    for m in range(2):
        at = half_rows(m)
        upper_kernel(
            m, inputs, own.at[at], other.at[at], gains, weight, *(out.at[at] for out in outs)
        )
    lower_grad_kernel(count, place, lengths, cotangent, outs[2], *parts, *scratch)


def hidden_step(assembles, *refs):
    if assembles:
        place, part_a, far_a, part_b, far_b, *refs = refs
        lengths, cotangent, slope, upper, second_norm, active, part, ffn, *parts = refs
        *parts, lower, upper_grad, turned, scratch_a, scratch_b = parts
        assemble_late_kernel(place, part_a, far_a, part_b, far_b, lower)
    else:
        lower, lengths, cotangent, slope, upper, second_norm, active, part, ffn, *parts = refs
        *parts, upper_grad, turned = parts
    for m in range(2):
        at = half_rows(m)
        hidden_back_kernel(
            m, lengths, cotangent, slope.at[at], lower, upper, upper_grad.at[at], part.at[at]
        )
    for start in range(0, active.shape[0], LEN):
        at = pl.ds(start, LEN)
        ffn[at, :] = dot_nt(active[at, :], lower[...]).astype(BF)
    if assembles:
        scratch = [turned, scratch_a, scratch_b]
        grads_kernel(1, len(parts), place, second_norm, upper_grad, *parts, *scratch)
    else:
        grads_kernel(1, len(parts), None, second_norm, upper_grad, *parts, turned)


def middle_step(
    lengths, cotangent, own, other, middle, gains, weight, middle_grad, low, head_grad
):
    for m in range(2):
        at = half_rows(m)
        middle_back_kernel(
            m,
            lengths,
            cotangent,
            own.at[at],
            other.at[at],
            middle.at[at],
            gains,
            weight,
            middle_grad.at[at],
            low.at[at],
            head_grad.at[at],
        )


def early_back_step(
    lengths,
    mixed,
    logsums,
    head_grad,
    cosine,
    sine,
    middle,
    ffn,
    ffn_other,
    early,
    results,
    key_sum,
    value_sum,
):
    attend_back_kernel(
        0, lengths, mixed, logsums, head_grad, cosine, sine, early, key_sum, value_sum
    )
    for start in range(0, middle.shape[0], LEN):
        at = pl.ds(start, LEN)
        total = ffn[at, :].astype(F32) + ffn_other[at, :].astype(F32)
        results[at, :] = (middle[at, :] + total).astype(BF)


def last_back_step(micro, outs, place, lengths, *refs):
    mixed, logsums, head_grad, cosine, sine, low, heads, first_norm, early, *refs = refs
    late, *refs = refs
    out_refs, (key_sum, value_sum, *scratch) = refs[:outs], refs[outs:]
    attend_back_kernel(
        micro, lengths, mixed, logsums, head_grad, cosine, sine, late, key_sum, value_sum
    )
    turned, *scratch = scratch
    rows = 2 * LEN

    def turn(left):
        for start in range(0, left.shape[0], LEN):
            turned[:, start : start + LEN] = left[start : start + LEN, :].T

    turn(low)
    products = sum_products(turned, heads, 0)
    turn(first_norm)
    for c in range(0, late.shape[1], LEN):
        high = min(c + LEN, late.shape[1])
        total = dot(turned[:, :rows], early[:, c:high]) + dot(turned[:, rows:], late[:, c:high])
        products.append((heads.shape[1] + c, total))
    write_products(place, products, out_refs, scratch)


def tail_kernel(early, late, weight, part):
    half, feats = early.shape[0], early.shape[1] // 3
    for start in range(0, 2 * half, LEN):
        mixed_grad = (early if start < half else late)[pl.ds(start % half, LEN), :]
        part[pl.ds(start, LEN), :] = dot_nt(mixed_grad, weight[:, feats : 4 * feats]).astype(BF)


def last_kernel(own, other, middle_grad, inputs, gains, input_grad):
    step = 128
    for start in range(0, inputs.shape[0], step):
        at = pl.ds(start, step)
        back = own[at, :].astype(F32) + other[at, :].astype(F32)
        normed, inverse = norm_parts(inputs[at, :].astype(F32))
        input_grad[at, :] = middle_grad[at, :] + norm_back(normed, inverse, back, gains[0:1, :])


def gains_step(own, other, weight, first, second, new, first_new, second_new, low):
    grad = (own[...] + other[...]) / weight[...].astype(BF).astype(F32)
    new[...], first_new[...], second_new[...] = adamw_update(
        weight[...], first[...], second[...], grad, RATE_GAIN, 0.0
    )
    low[...] = new[...].astype(BF)


def chip_pairs(move):
    pairs = []
    for chip in range(CHIPS):
        to_z, to_y, to_x = move(chip // 4, chip // 2 % 2, chip % 2)
        pairs.append((chip, to_z * 4 + to_y * 2 + to_x))
    return pairs


SWAP_X = chip_pairs(lambda z, y, x: (z, y, 1 - x))
SWAP_Y = chip_pairs(lambda z, y, x: (z, 1 - y, x))
SHIFT_Z = {k: chip_pairs(lambda z, y, x, k=k: ((z + k) % NZ, y, x)) for k in (1, 2, 3)}


def exchange(value, pairs, name):
    with jax.named_scope(name):
        return lax.ppermute(value, "dp", pairs)


tie = lax.optimization_barrier


def start_gather(name, shard, shifts=(1, 2, 3)):
    if lax.axis_size("dp") != CHIPS:
        return [lax.all_gather(shard, "dp", axis=0, tiled=True)] if 1 in shifts else [shard]
    return [shard] + [exchange(shard, SHIFT_Z[k], f"{name}_z{k}") for k in shifts]


def spread_near(name, arrived, cut):
    if len(arrived) == 1:
        return arrived
    rows, columns = arrived[0].shape
    out = [((NZ * rows, cut), BF), ((NZ * rows, columns - cut), BF)]
    part_a, part_b = call(stack_kernel, out, arrived, name="stack")
    return [
        part_a,
        exchange(part_a, SWAP_X, f"{name}_near_a"),
        part_b,
        exchange(part_b, SWAP_Y, f"{name}_near_b"),
    ]


def spread_far(name, near):
    if len(near) == 1:
        return near
    rows = 2 * near[0].shape[0]
    out = [((rows, near[0].shape[1]), BF), ((rows, near[2].shape[1]), BF)]
    near_a, near_b = call(pair_kernel, out, near, name="pair")
    far_a = exchange(near_a, SWAP_Y, f"{name}_far_a")
    return [near_a, far_a, near_b, exchange(near_b, SWAP_X, f"{name}_far_b")]


def step_with_weight(step, place, pieces, args, out, smem=(), scratch=(), name=None):
    if len(pieces) == 1:
        smem = [i + 1 for i in smem]
        held = dict(smem=smem, scratch=scratch, name=name)
        outs = call(partial(step, False), out, (pieces[0], *args), **held)
        return [*outs, pieces[0]]
    smem = [0] + [i + 1 + len(pieces) for i in smem]
    whole = ((2 * pieces[0].shape[0], pieces[0].shape[1] + pieces[2].shape[1]), BF)
    held = dict(smem=smem, scratch=scratch, name=name)
    return call(partial(step, True), [*out, whole], (place, *pieces, *args), **held)


def gather_near(name, shard):
    if lax.axis_size("dp") != CHIPS:
        return lax.all_gather(shard, "dp", axis=0, tiled=True)
    rows, columns = shard.shape
    cut = columns // 2
    part_a, part_b = shard[:, :cut], shard[:, cut:]
    got_a = exchange(part_a, SWAP_X, f"{name}_near_a")
    got_b = exchange(part_b, SWAP_Y, f"{name}_near_b")
    out = [((2 * rows, columns), BF)]
    return call(join_kernel, out, (part_a, got_a, part_b, got_b), name="join")[0]


def gather_z(name, block, shifts):
    if lax.axis_size("dp") != CHIPS:
        return []
    return [exchange(block, SHIFT_Z[k], f"{name}_z{k}") for k in shifts]


def gather_far(name, arrived):
    if len(arrived) == 1:
        return arrived
    rows, columns = arrived[0].shape
    cut = columns // 2
    out = [((NZ * rows, cut), BF)] * 2
    part_a, part_b = call(stack_kernel, out, arrived, name="stack")
    far_a = exchange(part_a, SWAP_Y, f"{name}_far_a")
    return [part_a, far_a, part_b, exchange(part_b, SWAP_X, f"{name}_far_b")]


def scatter_first(name, parts):
    if len(parts) == 1:
        return parts
    kept_a, sent_a, kept_b, sent_b = parts
    return [
        kept_a,
        exchange(sent_a, SWAP_X, f"{name}_first_a"),
        kept_b,
        exchange(sent_b, SWAP_Y, f"{name}_first_b"),
    ]


def scatter_half(halves):
    if len(halves) == 1:
        return halves
    rows = halves[0].shape[0] // 2
    out = [((rows, h.shape[1]), d) for h in (halves[0], halves[2]) for d in (F32, BF)]
    return call(half_kernel, out, halves, name="half")


def scatter_second(name, halves):
    if len(halves) == 1:
        return halves
    own_a, send_a, own_b, send_b = halves
    return [
        own_a,
        exchange(send_a, SWAP_Y, f"{name}_second_a"),
        own_b,
        exchange(send_b, SWAP_X, f"{name}_second_b"),
    ]


def scatter_column(columns):
    if len(columns) == 1:
        return columns
    rows, count = columns[0].shape[0] // NZ, columns[0].shape[1] + columns[2].shape[1]
    out = [((rows, count), F32)] + [((rows, count), BF)] * 3
    return call(column_kernel, out, columns, name="column")


def scatter_last(name, columns):
    if len(columns) == 1:
        return [lax.psum_scatter(columns[0], "dp", scatter_dimension=0, tiled=True)]
    mine, *sends = columns
    return [mine] + [exchange(s, SHIFT_Z[k], f"{name}_z{k}") for k, s in enumerate(sends, 1)]


def added(parts):
    return sum(p.astype(F32) for p in parts)


def swapped(value):
    return lax.ppermute(value, "mp", [(0, 1), (1, 0)])


def rotation():
    freqs = np.float32(10000.0) ** (np.float32(-2.0) * np.arange(HD // 2, dtype=np.float32) / np.float32(HD))
    angles = (np.arange(LEN, dtype=np.float32)[:, None] * freqs[None, :]).astype(np.float64)
    cosine, sine = np.cos(angles), np.sin(angles)
    cosine = np.tile(cosine, (1, 4)).astype(np.float32)
    return cosine, np.tile(np.concatenate([-sine, sine], axis=1), (1, 2)).astype(np.float32)


def row_sums(value):
    ones = jnp.ones((1, value.shape[1]), F32)
    contract = (((1,), (1,)), ((), ()))
    return lax.dot_general(
        ones, value, contract, precision=lax.Precision.HIGHEST, preferred_element_type=F32
    )


def adamw_update(weight, first, second, grad, rate, decay):
    first_new = BETA_ONE * first + (1.0 - BETA_ONE) * grad
    second_new = BETA_TWO * second + (1.0 - BETA_TWO) * grad * grad
    corrected = (
        first_new
        / (1.0 - BETA_ONE**STEP)
        / (jnp.sqrt(second_new / (1.0 - BETA_TWO**STEP)) + ADAM_EPS)
    )
    return (weight - rate * (corrected + decay * weight), first_new, second_new)


def shards(
    inputs,
    cotangent,
    lengths,
    proj_weight,
    output_weight,
    upper_weight,
    lower_weight,
    norm_gains,
    proj_first,
    output_first,
    upper_first,
    lower_first,
    gains_first,
    proj_second,
    output_second,
    upper_second,
    lower_second,
    gains_second,
):
    micro_count, _, row_count, width = inputs.shape
    feats = proj_weight.shape[2]
    hidden = upper_weight.shape[1]
    shard_rows = proj_weight.shape[0]
    local = lax.axis_size("dp") == CHIPS
    chip = lax.axis_index("dp").astype(jnp.int32)
    place = jnp.stack([chip // 4, chip // 2 % 2, chip % 2])
    micros = range(micro_count)
    lengths = lengths.reshape(-1)
    flat_in = inputs.reshape(-1, width)
    flat_ct = cotangent.reshape(-1, width)

    cosine, sine = (jnp.asarray(table) for table in rotation())

    gain_columns = jnp.pad(norm_gains.T.astype(BF), ((0, 0), (0, LANES - 2)))
    shard_one = jnp.concatenate(
        [
            output_weight.astype(BF).T,
            proj_weight.astype(BF).reshape(shard_rows, 3 * feats),
            gain_columns,
        ],
        axis=1,
    )
    upper_low, lower_low = upper_weight.astype(BF), lower_weight.astype(BF).T
    total_rows = micro_count * row_count
    wide, features = (total_rows, width), (total_rows, feats)
    arrived = start_gather("one", shard_one)
    near_lower = gather_near("lower", lower_low)
    arrived, upper_low, near_lower = tie((arrived, upper_low, near_lower))
    near = spread_near("one", arrived, 2 * feats)
    arrived_upper = start_gather("upper", upper_low, (1, 3))
    near, arrived_upper, upper_low = tie((near, arrived_upper, upper_low))
    pieces = spread_far("one", near)
    opposite = start_gather("upper", upper_low, (2,))[1:]
    opposite, near_lower = tie((opposite, near_lower)) if local else (opposite, near_lower)
    arrived_upper = [*arrived_upper[:2], *opposite, *arrived_upper[2:]]
    beside_lower = gather_z("lower", near_lower, (1, 3))
    near_upper = spread_near("upper", arrived_upper, hidden // 2)
    gains_c, first_norm, mixed, one = step_with_weight(
        first_step,
        place,
        pieces,
        (flat_in, cosine, sine),
        [((8, width), F32), (wide, BF), ((total_rows, 3 * feats), BF)],
        name="qkv",
    )
    mixed, near_upper, beside_lower, near_lower = tie((mixed, near_upper, beside_lower, near_lower))
    opposite_lower = gather_z("lower", near_lower, (2,))
    far_upper = spread_far("upper", near_upper)
    heads, logsums, attn = call(
        attend_step,
        [(features, BF), ((total_rows, LANES), F32), (wide, BF)],
        (lengths, mixed, one),
        smem=(0,),
        name="attend",
    )
    far_upper, opposite_lower, attn = tie((far_upper, opposite_lower, attn))
    arrived_lower = [near_lower, *beside_lower[:1], *opposite_lower, *beside_lower[1:]]
    attn_other = swapped(attn)
    far_lower = gather_far("lower", arrived_lower)
    hidden_rows = (total_rows, hidden)
    part_out, part_scratch = product_out(width, hidden, hidden // 2, local)
    turned = pltpu.VMEM((width, total_rows), BF)
    middle, second_norm, active, slope, *lower_parts, upper_c = step_with_weight(
        upper_step,
        place,
        far_upper,
        (lengths, flat_in, attn, attn_other, gains_c, flat_ct),
        [(wide, F32), (wide, BF), (hidden_rows, BF), (hidden_rows, BF), *part_out],
        smem=(0,),
        scratch=[turned, *part_scratch],
        name="upper",
    )
    lower_parts, far_lower = tie((lower_parts, far_lower))
    lower_half = scatter_first("lower_sum", lower_parts)
    seconds, ffn, *upper_parts, _ = step_with_weight(
        hidden_step,
        place,
        far_lower,
        (lengths, flat_ct, slope, upper_c, second_norm, active),
        [(wide, BF), (wide, BF), *part_out],
        smem=(0,),
        scratch=[pltpu.VMEM(hidden_rows, BF), turned, *part_scratch],
        name="hidden_back",
    )
    upper_parts, lower_half, seconds = tie((upper_parts, lower_half, seconds))
    lower_half, seconds = tie((scatter_half(lower_half), seconds))
    lower_column = scatter_second("lower_sum", lower_half)
    seconds_other = swapped(seconds)
    upper_half = scatter_first("upper_sum", upper_parts)
    ffn_other = swapped(ffn)
    middle_grad, low, head_grad = call(
        middle_step,
        [(wide, F32), (wide, BF), (features, BF)],
        (lengths, flat_ct, seconds, seconds_other, middle, gains_c, one),
        smem=(0,),
        name="middle_back",
    )
    grad_shape = (row_count, 3 * feats)
    sums_of = [pltpu.VMEM((row_count, LANES), F32)] * 2
    early, results = call(
        early_back_step,
        [(grad_shape, BF), (wide, BF)],
        (lengths, mixed, logsums, head_grad, cosine, sine, middle, ffn, ffn_other),
        smem=(0,),
        scratch=sums_of,
        name="attend_back",
    )
    early, head_grad, lower_column, upper_half = tie((early, head_grad, lower_column, upper_half))
    lower_sum = scatter_last("lower_sum", scatter_column(lower_column))
    upper_column = scatter_second("upper_sum", scatter_half(upper_half))
    part_out, part_scratch = product_out(width, 4 * feats, 2 * feats, local)
    late, *one_parts = call(
        partial(last_back_step, 1, len(part_out)),
        [(grad_shape, BF), *part_out],
        (place, lengths, mixed, logsums, head_grad, cosine, sine, low, heads, first_norm, early),
        smem=(0, 1),
        scratch=[*sums_of, turned, *part_scratch],
        name="last_back",
    )
    late, one_parts, upper_column, lower_sum = tie((late, one_parts, upper_column, lower_sum))
    one_half = scatter_first("one_sum", one_parts)
    upper_sum = scatter_last("upper_sum", scatter_column(upper_column))
    (sums,) = call(tail_kernel, [(wide, BF)], (early, late, one), name="tail")
    sums, one_half, upper_sum = tie((sums, one_half, upper_sum))
    one_column = scatter_second("one_sum", scatter_half(one_half))
    sums_other = swapped(sums)
    (input_grad,) = call(
        last_kernel,
        [(wide, F32)],
        (sums, sums_other, middle_grad, flat_in, gains_c),
        name="last",
    )
    one_column, input_grad = tie((one_column, input_grad))
    one_column, lower_sum, upper_sum = tie((scatter_column(one_column), lower_sum, upper_sum))
    one_sum = scatter_last("one_sum", one_column)
    lower_grad = added(lower_sum).T
    upper_wgrad = added(upper_sum)
    one_grad = tie(added(one_sum))
    turn = lambda a: a.transpose(1, 0, 2)
    proj_wgrad = jnp.stack([one_grad[:, c * feats : (c + 1) * feats] for c in (1, 2, 3)])
    proj_update = adamw_update(
        turn(proj_weight), turn(proj_first), turn(proj_second), proj_wgrad, RATE_MATRIX, DECAY
    )
    output_grad = one_grad[:, :feats].T
    kept = [
        row_sums(shard_one[:, feats : 4 * feats].astype(F32) * one_grad[:, feats:]),
        row_sums(upper_weight.astype(BF).astype(F32) * upper_wgrad),
    ]
    kept = jnp.concatenate(kept)
    gains_update = call(
        gains_step,
        [(norm_gains.shape, F32)] * 3 + [(norm_gains.shape, BF)],
        (kept, swapped(kept), norm_gains, gains_first, gains_second),
        name="gains",
    )

    updates = [
        [turn(u) for u in proj_update],
        adamw_update(output_weight, output_first, output_second, output_grad, RATE_OUTPUT, DECAY),
        adamw_update(upper_weight, upper_first, upper_second, upper_wgrad, RATE_MATRIX, DECAY),
        adamw_update(lower_weight, lower_first, lower_second, lower_grad, RATE_MATRIX, DECAY),
    ]
    return (
        results.reshape(inputs.shape),
        input_grad.reshape(inputs.shape),
        *[u[0] for u in updates],
        gains_update[0],
        *[u[1] for u in updates],
        gains_update[1],
        *[u[2] for u in updates],
        gains_update[2],
        *[u[0].astype(BF) for u in updates],
        gains_update[3],
    )


def solution(mesh):
    rows = P(None, "dp", None, None)
    weights = (P("dp", None, "mp"), P("mp", "dp"), P("dp", "mp"), P("mp", "dp"), P(None, "dp"))
    in_specs = (rows, rows, P(None, "dp"), *weights * 3)
    out_specs = (rows, rows, *weights * 4)
    return jax.shard_map(shards, mesh=mesh, in_specs=in_specs, out_specs=out_specs, check_vma=False)
```
